32 devices in a mesh: seq: 4 (over z), tp: 8 (over y, x, core).
Axes of the slice: x: 2, y: 2, z: 4, core: 2. Of those that a mesh axis runs over, the one named last changes fastest.
Arguments:
- patch_tokens: bfloat16 [2, 4096, 1024], P(None, 'seq'), may hold values from -6 to 6
- plane_tokens: bfloat16 [2, 3072, 1024], P(None, 'seq'), may hold values from -6 to 6
- norm1_gain: float32 [1024], replicated, may hold values from 0.5 to 1.5
- norm1_bias: float32 [1024], replicated, may hold values from -1 to 1
- w_query: bfloat16 [1024, 1024], P(None, 'tp'), may hold values from -0.375 to 0.375
- w_key: bfloat16 [1024, 1024], P(None, 'tp'), may hold values from -0.1875 to 0.1875
- w_value: bfloat16 [1024, 1024], P(None, 'tp'), may hold values from -0.1875 to 0.1875
- w_out: bfloat16 [1024, 1024], P('tp'), may hold values from -2 to 2
- norm2_gain: float32 [1024], replicated, may hold values from 0.5 to 1.5
- norm2_bias: float32 [1024], replicated, may hold values from -1 to 1
- w_up: bfloat16 [1024, 4096], P(None, 'tp'), may hold values from -0.1875 to 0.1875
- w_down: bfloat16 [4096, 1024], P('tp'), may hold values from -0.09375 to 0.09375
- w_unpatch: bfloat16 [1024, 2048], P(None, 'tp'), may hold values from -0.1875 to 0.1875
- b_unpatch: float32 [2048], P('tp'), may hold values from -3 to 3
- w_dec1: float32 [32, 64], replicated, may hold values from -1 to 1
- b_dec1: float32 [64], replicated, may hold values from -3 to 3
- w_dec2: float32 [64, 4], replicated, may hold values from -0.75 to 0.75
- tile_index: int32 [2, 3, 128], P(None, None, 'seq'), may hold values from 0 to 1023
- corner_weights: bfloat16 [2, 128, 3, 64, 128], P(None, 'seq', None, 'tp'), may hold values from 0 to 1, as said below
- ray_count: int32 [2], replicated, may hold values from 32 to 128, as said below
- color_grad: float32 [2, 3, 128], P(None, None, ('seq', 'tp')), may hold values from -6 to 6
Outputs:
- colors: float32 [2, 3, 128], P(None, None, ('seq', 'tp'))
- patch_grad: float32 [2, 4096, 1024], P(None, ('seq', 'tp'))
- plane_grad: float32 [2, 3072, 1024], P(None, ('seq', 'tp'))
- norm1_gain_grad: float32 [1024], P('tp')
- norm1_bias_grad: float32 [1024], P('tp')
- query_grad: float32 [1024, 1024], P(None, 'tp')
- key_grad: float32 [1024, 1024], P(None, 'tp')
- value_grad: float32 [1024, 1024], P(None, 'tp')
- out_weight_grad: float32 [1024, 1024], P('tp')
- norm2_gain_grad: float32 [1024], P('tp')
- norm2_bias_grad: float32 [1024], P('tp')
- up_grad: float32 [1024, 4096], P(None, 'tp')
- down_grad: float32 [4096, 1024], P('tp')
- unpatch_grad: float32 [1024, 2048], P(None, 'tp')
- unpatch_bias_grad: float32 [2048], P('tp')
- dec1_grad: float32 [32, 64], P(None, 'tp')
- dec1_bias_grad: float32 [64], P('tp')
- dec2_grad: float32 [64, 4], P('tp')
The draws below stay inside these ranges and needn't reach their ends.
Inputs may be any that keep to these rules, and one draw needn't show every extreme that they name: Scene n's live rays are its first ray_count[n] ray slots; the later slots are padding. Some scene has all 128 slots live. `corner_weights`: for each ray, plane and sample, the column over the 64 pixels holds the bilinear weights of one point inside the 8 by 8 tile: nonnegative, at most four nonzero, summing to one.
All inputs are finite; a program needn't handle non-finite values.
Results may differ from the reference program's by a relative error of at most 0.023.
Values may be sent and summed in bfloat16 or wider, within the bound.
No kernel may reach another device: no remote copies, remote signals or barrier semaphores. Data moves between devices by JAX's collectives and lax.ppermute only.
A program may use at most 448 MiB of HBM per device.

```python
import math
import jax
import jax.numpy as jnp
from jax import lax

D = 1024
HEADS = 16
HEAD_DIM = 64
FF = 4096
CH = 32
TILE_PX = 64
TRI_SIDE = 32
PATCH_TOK = 4096
SAMPLES = 128
DEC_HID = 64
SCN = 2
TRI_TOK = 3072
RAYS = 128


def draw_corner_weights(key, part):
    tile_side = math.isqrt(TILE_PX)
    first_key, second_key = jax.random.split(key)
    draw_shape = (SCN, RAYS, 3, 1, SAMPLES)
    along_x = jax.random.uniform(first_key, draw_shape, jnp.float32, 0.0, tile_side - 1.0)
    along_y = jax.random.uniform(second_key, draw_shape, jnp.float32, 0.0, tile_side - 1.0)
    pixels = jnp.arange(TILE_PX, dtype=jnp.int32)
    column = (pixels % tile_side).astype(jnp.float32).reshape(1, 1, 1, TILE_PX, 1)
    row_place = (pixels // tile_side).astype(jnp.float32).reshape(1, 1, 1, TILE_PX, 1)
    weight = jnp.maximum(0.0, 1.0 - jnp.abs(along_x - column)) * jnp.maximum(0.0, 1.0 - jnp.abs(along_y - row_place))
    return weight.astype(jnp.bfloat16)


def draw_ray_count(key, part):
    first_key, second_key = jax.random.split(key)
    counts = jax.random.randint(first_key, (SCN,), RAYS // 4, RAYS + 1)
    chosen = jax.random.randint(second_key, (), 0, SCN)
    return jnp.where(jnp.arange(SCN) == chosen, RAYS, counts).astype(jnp.int32)


def place_ends(drawn, key, low, largest):
    longest = drawn.shape.index(max(drawn.shape))
    spots = []
    for shift in (0, 1):
        where = [jax.random.randint(jax.random.fold_in(key, axis), (), 0, length) for axis, length in enumerate(drawn.shape)]
        where[longest] = (where[longest] + shift) % drawn.shape[longest]
        spots.append(tuple(where))
    return drawn.at[spots[0]].set(low).at[spots[1]].set(largest)


def block_levels(rng, extent, shards, smallest, top_value):
    def one(dim, blocks):
        draws = jax.random.uniform(jax.random.fold_in(jax.random.fold_in(rng, 6), dim), (blocks,), jnp.float32, smallest / len(shards), top_value / len(shards))
        return jnp.repeat(jnp.exp(draws), extent[dim] // blocks).reshape((-1,) + (1,) * (len(extent) - dim - 1))

    loudness = one(*shards[0])
    for cut in shards[1:]:
        loudness = loudness * one(*cut)
    return loudness


def gaussian(key, shape, deviation, reach, shards=(), kind=jnp.bfloat16):
    drawn = deviation * jax.random.normal(key, shape, jnp.float32)
    if shards:
        drawn = drawn * block_levels(key, shape, shards, -0.22, 0.18)
    return jnp.clip(drawn, -reach, reach).astype(kind)


def setup_inputs(seed: int = 0) -> dict:
    key_list = jax.random.split(jax.random.key(seed), 22)
    patch_tokens = gaussian(key_list[0], (SCN, PATCH_TOK, D), 1.0, 6.0, ((1, 4),))
    plane_tokens = gaussian(key_list[1], (SCN, TRI_TOK, D), 1.0, 6.0, ((1, 4),))
    norm1_gain = jnp.clip(1.0 + 0.1 * jax.random.normal(key_list[2], (D,), jnp.float32), 0.5, 1.5)
    norm1_bias = gaussian(key_list[3], (D,), 0.2, 1.0, (), jnp.float32)
    w_query = gaussian(key_list[4], (D, D), (D // 4) ** -0.5, 0.375, ((1, 8),))
    w_key = gaussian(key_list[5], (D, D), D ** -0.5, 0.1875, ((1, 8),))
    w_value = gaussian(key_list[6], (D, D), D ** -0.5, 0.1875, ((1, 8),))
    w_out = gaussian(key_list[7], (D, D), (HEAD_DIM // 8) ** -0.5, 2.0, ((0, 8),))
    norm2_gain = jnp.clip(1.0 + 0.1 * jax.random.normal(key_list[8], (D,), jnp.float32), 0.5, 1.5)
    norm2_bias = gaussian(key_list[9], (D,), 0.2, 1.0, (), jnp.float32)
    w_up = gaussian(key_list[10], (D, FF), D ** -0.5, 0.1875, ((1, 8),))
    w_down = gaussian(key_list[11], (FF, D), FF ** -0.5, 0.09375, ((0, 8),))
    w_unpatch = gaussian(key_list[12], (D, TILE_PX * CH), D ** -0.5, 0.1875, ((1, 8),))
    b_unpatch = gaussian(key_list[13], (TILE_PX * CH,), 0.5, 3.0, ((0, 8),), jnp.float32)
    w_dec1 = gaussian(key_list[14], (CH, DEC_HID), CH ** -0.5, 1.0, (), jnp.float32)
    b_dec1 = gaussian(key_list[15], (DEC_HID,), 0.5, 3.0, (), jnp.float32)
    w_dec2 = gaussian(key_list[16], (DEC_HID, 4), DEC_HID ** -0.5, 0.75, (), jnp.float32)
    tile_index = place_ends(jax.random.randint(key_list[17], (SCN, 3, RAYS), 0, TRI_SIDE * TRI_SIDE), jax.random.fold_in(key_list[17], 1), 0, (TRI_SIDE * TRI_SIDE) - 1).astype(jnp.int32)
    corner_weights = draw_corner_weights(jax.random.fold_in(key_list[21], 71), 0)
    ray_count = draw_ray_count(jax.random.fold_in(key_list[21], 71), 0)
    color_grad = gaussian(key_list[20], (SCN, 3, RAYS), 1.0, 6.0, ((2, 32),), jnp.float32)
    return {"patch_tokens": patch_tokens, "plane_tokens": plane_tokens, "norm1_gain": norm1_gain, "norm1_bias": norm1_bias, "w_query": w_query, "w_key": w_key, "w_value": w_value, "w_out": w_out, "norm2_gain": norm2_gain, "norm2_bias": norm2_bias, "w_up": w_up, "w_down": w_down, "w_unpatch": w_unpatch, "b_unpatch": b_unpatch, "w_dec1": w_dec1, "b_dec1": b_dec1, "w_dec2": w_dec2, "tile_index": tile_index, "corner_weights": corner_weights, "ray_count": ray_count, "color_grad": color_grad}


@jax.custom_vjp
def low(v):
    return lax.optimization_barrier(v.astype(jnp.bfloat16)).astype(jnp.float32)

@jax.custom_vjp
def low_back(v):
    return v

def low_keep(v):
    return (low(v), None)

def low_pass(kept, grad):
    return (grad,)

def back_keep(v):
    return (v, None)

def back_low(kept, grad):
    return (low(grad),)
low.defvjp(low_keep, low_pass)
low_back.defvjp(back_keep, back_low)

def norm_rows(token_rows, norm_gain, norm_shift):
    centre = lax.optimization_barrier(jnp.mean(token_rows, axis=-1, keepdims=True))
    offset = token_rows - centre
    spread = lax.optimization_barrier(jnp.mean(offset * offset, axis=-1, keepdims=True))
    return offset * lax.rsqrt(spread + 1e-05) * norm_gain + norm_shift

def render(features, dec_first, dec_bias, dec_second, live_rays):
    preact = jnp.einsum('ch,...cs->...hs', dec_first, features, precision=lax.Precision.HIGHEST) + dec_bias[:, None]
    hidden = jax.nn.silu(preact)
    output = jnp.einsum('hk,...hs->...ks', dec_second, hidden, precision=lax.Precision.HIGHEST)
    density = jax.nn.softplus(output[..., 0, :])
    colour = jax.nn.sigmoid(output[..., 1:, :])
    optical = density * (2.0 / output.shape[-1])
    through = jnp.exp(-(jnp.cumsum(optical, axis=-1) - optical))
    weight = through * (1.0 - jnp.exp(-optical))
    return lax.optimization_barrier(jnp.sum(weight[..., None, :] * colour, axis=-1)) * live_rays[..., None]

def one_head(head_data):
    query_head, key_head, value_head = head_data
    scores = low_back(jnp.dot(query_head, key_head.T, precision=lax.Precision.HIGHEST) * HEAD_DIM ** (-0.5))
    shares = jax.nn.softmax(scores, axis=-1)
    return jnp.dot(low(shares), value_head, precision=lax.Precision.HIGHEST)

def split_heads(matrix):
    return matrix.reshape(matrix.shape[0], HEADS, HEAD_DIM).transpose(1, 0, 2)

def scene_colours(params, scene_data):
    norm1_gain, norm1_bias, w_query, w_key, w_value, w_out, norm2_gain, norm2_bias, w_up, w_down, w_unpatch, b_unpatch, w_dec1, b_dec1, w_dec2 = params
    patch_rows, plane_rows, corner_block, index_block, count_value = scene_data
    token_rows = jnp.concatenate([patch_rows, plane_rows], axis=0)
    normed = low(norm_rows(token_rows, norm1_gain, norm1_bias))
    queries = low(low_back(jnp.dot(normed[PATCH_TOK:], w_query, precision=lax.Precision.HIGHEST)))
    key_rows = low(low_back(jnp.dot(normed, w_key, precision=lax.Precision.HIGHEST)))
    value_rows = low(low_back(jnp.dot(normed, w_value, precision=lax.Precision.HIGHEST)))
    mixed = lax.map(jax.checkpoint(one_head), (split_heads(queries), split_heads(key_rows), split_heads(value_rows)))
    mixed = low(low_back(mixed.transpose(1, 0, 2).reshape(TRI_TOK, D)))
    hidden = plane_rows + low_back(jnp.dot(mixed, w_out, precision=lax.Precision.HIGHEST))
    normed2 = low(norm_rows(hidden, norm2_gain, norm2_bias))
    active = low(jax.nn.gelu(low_back(jnp.dot(normed2, w_up, precision=lax.Precision.HIGHEST))))
    result = hidden + low_back(jnp.dot(active, w_down, precision=lax.Precision.HIGHEST))
    tile_rows = low(low_back(jnp.dot(low(result), w_unpatch, precision=lax.Precision.HIGHEST) + b_unpatch))
    plane_offset = (jnp.arange(3, dtype=jnp.int32) * (TRI_SIDE * TRI_SIDE))[:, None]
    picked = tile_rows[(index_block + plane_offset).astype(jnp.int32)].reshape(3, RAYS, TILE_PX, CH)
    features = jnp.einsum('prxc,rpxs->rcs', picked, corner_block.astype(jnp.float32), precision=lax.Precision.HIGHEST)
    live_rays = (jnp.arange(RAYS, dtype=jnp.int32) < count_value).astype(jnp.float32)
    return render(features, w_dec1, b_dec1, w_dec2, live_rays).T

def reference(patch_tokens, plane_tokens, norm1_gain, norm1_bias, w_query, w_key, w_value, w_out, norm2_gain, norm2_bias, w_up, w_down, w_unpatch, b_unpatch, w_dec1, b_dec1, w_dec2, tile_index, corner_weights, ray_count, color_grad):
    params = jax.tree.map(lambda member: member.astype(jnp.float32), (norm1_gain, norm1_bias, w_query, w_key, w_value, w_out, norm2_gain, norm2_bias, w_up, w_down, w_unpatch, b_unpatch, w_dec1, b_dec1, w_dec2))

    def forward(patch_rows, plane_rows, weights_all):

        def per_scene(scene_data):
            return scene_colours(weights_all, scene_data)
        return lax.map(jax.checkpoint(per_scene), (patch_rows, plane_rows, corner_weights, tile_index, ray_count))
    colours, pullback = jax.vjp(forward, patch_tokens.astype(jnp.float32), plane_tokens.astype(jnp.float32), params)
    patch_grad, plane_grad, param_grads = pullback(color_grad)
    gain1_grad, bias1_grad, query_grad, key_grad, value_grad, out_weight_grad, gain2_grad, bias2_grad, up_grad, down_grad, unpatch_grad, unpatch_bias_grad, dec1_grad, dec1_bias_grad, dec2_grad = param_grads
    return (colours, patch_grad, plane_grad, gain1_grad, bias1_grad, query_grad, key_grad, value_grad, out_weight_grad, gain2_grad, bias2_grad, up_grad, down_grad, unpatch_grad, unpatch_bias_grad, dec1_grad, dec1_bias_grad, dec2_grad)
```

```python
import jax
import jax.numpy as jnp
from jax import lax
from jax.sharding import PartitionSpec as P

HEAD_DIM = 64
CH = 32
TRI_SIDE = 32
BF = jnp.bfloat16
F32 = jnp.float32
HIGH = lax.Precision.HIGHEST


def dot(spec, *operands):
    return jnp.einsum(spec, *operands, preferred_element_type=F32)


def standard_rows(token_rows):
    centre = jnp.mean(token_rows, axis=-1, keepdims=True)
    offset = token_rows - centre
    spread = jnp.mean(offset * offset, axis=-1, keepdims=True)
    scale = lax.rsqrt(spread + 1e-05)
    return offset * scale, scale


def norm_rows(token_rows, norm_gain, norm_shift):
    return standard_rows(token_rows)[0] * norm_gain + norm_shift


def norm_back(standard, scale, norm_gain, grad):
    scaled = grad * norm_gain
    first = jnp.mean(scaled, axis=-1, keepdims=True)
    second = jnp.mean(scaled * standard, axis=-1, keepdims=True)
    return scale * (scaled - first - standard * second)


def xor_pairs(size, mask):
    return [(i, i ^ mask) for i in range(size)]


def hyper_sum(value, axes):
    for axis in axes:
        size = lax.axis_size(axis)
        mask = 1
        while mask < size:
            value = value + lax.ppermute(value, axis, xor_pairs(size, mask))
            mask *= 2
    return value


def render(features, dec_first, dec_bias, dec_second, live_rays):
    preact = jnp.einsum("ch,...cs->...hs", dec_first, features, precision=HIGH) + dec_bias[:, None]
    hidden = jax.nn.silu(preact)
    output = jnp.einsum("hk,...hs->...ks", dec_second, hidden, precision=HIGH)
    samples = output.shape[-1]
    density = jax.nn.softplus(output[..., 0, :])
    colour = jax.nn.sigmoid(output[..., 1:, :])
    optical = density * (2.0 / samples)
    place = jnp.arange(samples)
    before = (place[:, None] < place[None, :]).astype(F32)
    through = jnp.exp(-jnp.einsum("...t,ts->...s", optical, before, precision=HIGH))
    weight = through * (1.0 - jnp.exp(-optical))
    return jnp.sum(weight[..., None, :] * colour, axis=-1) * live_rays[..., None]


def on_device(
    patch_tokens,
    plane_tokens,
    norm1_gain,
    norm1_bias,
    w_query,
    w_key,
    w_value,
    w_out,
    norm2_gain,
    norm2_bias,
    w_up,
    w_down,
    w_unpatch,
    b_unpatch,
    w_dec1,
    b_dec1,
    w_dec2,
    tile_index,
    corner_weights,
    ray_count,
    color_grad,
):
    scenes, patch_local, width = patch_tokens.shape
    plane_local = plane_tokens.shape[1]
    seq_count, tp_count = lax.axis_size("seq"), lax.axis_size("tp")
    seq_rank, tp_rank = lax.axis_index("seq"), lax.axis_index("tp")
    own_patch = patch_local // tp_count
    own_plane = plane_local // tp_count
    cols = w_query.shape[1]
    heads = cols // HEAD_DIM
    ray_seq = tile_index.shape[2]
    rays = ray_seq // tp_count
    picks = 3 * rays
    seq_picks = tp_count * scenes * picks
    all_picks = seq_count * seq_picks
    score_scale = HEAD_DIM**-0.5

    base = (jnp.arange(3, dtype=jnp.int32) * (TRI_SIDE * TRI_SIDE))[None, :, None]
    ids = (tile_index + base).reshape(scenes, 3, tp_count, rays)
    ids = jnp.transpose(ids, (2, 0, 1, 3)).reshape(tp_count, scenes, picks)
    ids = lax.all_gather(ids, "seq", axis=0)
    local_ids = ids - seq_rank * plane_local
    inside = (local_ids >= 0) & (local_ids < plane_local)
    scene_base = (jnp.arange(scenes, dtype=jnp.int32) * plane_local)[None, None, :, None]
    row_ids = jnp.where(inside, local_ids + scene_base, -1).reshape(all_picks)
    onehot = (
        row_ids[:, None] == jnp.arange(scenes * plane_local, dtype=jnp.int32)[None, :]
    ).astype(BF)

    w_out_all = lax.all_gather(w_out, "tp", axis=0)
    bias_high = b_unpatch.astype(BF)
    rest = b_unpatch - bias_high.astype(F32)
    bias_mid = rest.astype(BF)
    bias_low = (rest - bias_mid.astype(F32)).astype(BF)
    bias_rows = jnp.stack([bias_high, bias_mid, bias_low] + [jnp.zeros_like(bias_high)] * 13)
    unpatch_all = lax.all_gather(jnp.concatenate([w_unpatch, bias_rows]), "tp", axis=0)
    qkv_weight = jnp.concatenate([w_key, w_value, w_query], axis=1)
    qkv_all = lax.all_gather(qkv_weight, "tp", axis=0)
    key_weight = qkv_weight[:, : 2 * cols]

    corners = corner_weights.reshape(
        scenes, tp_count, rays, 3, corner_weights.shape[3], corner_weights.shape[4]
    )
    corners = lax.all_to_all(jnp.moveaxis(corners, 1, 0), "tp", 0, 0, tiled=True)

    picked_rows = lax.psum_scatter(
        jnp.dot(onehot, plane_tokens.reshape(-1, width)), "seq", scatter_dimension=0, tiled=True
    )

    plane_normed = norm_rows(plane_tokens.astype(F32), norm1_gain, norm1_bias).astype(BF)
    patch_normed = norm_rows(patch_tokens.astype(F32), norm1_gain, norm1_bias).astype(BF)
    query_rows = dot("nrd,de->nre", plane_normed, w_query).astype(BF)
    queries = hyper_sum(jnp.dot(onehot, query_rows.reshape(-1, cols)), ("seq",))
    normed = jnp.concatenate([patch_normed, plane_normed], axis=1)
    key_value = dot("nrd,de->nre", normed, key_weight).astype(BF)

    def by_scene(value):
        value = value.reshape(seq_count, tp_count, scenes, picks, -1)
        return jnp.moveaxis(value, 2, 0).reshape(scenes, seq_count * tp_count * picks, -1)

    def by_seq(value):
        value = value.reshape(scenes, seq_count, tp_count, picks, -1)
        return jnp.moveaxis(value, 0, 2).reshape(seq_count, seq_picks, -1)

    def in_heads(value):
        return value.reshape(value.shape[:-1] + (heads, HEAD_DIM))

    query_heads = in_heads(by_scene(queries))
    key_heads = in_heads(key_value[..., :cols])
    value_heads = in_heads(key_value[..., cols:])
    scores = dot("nqhd,nkhd->nhqk", query_heads, key_heads) * score_scale
    row_max = jnp.max(scores, axis=-1, keepdims=True)
    raised = jnp.exp(scores - row_max)
    row_total = jnp.sum(raised, axis=-1)
    part = dot("nhqk,nkhd->nqhd", raised.astype(BF), value_heads)
    part = part / jnp.moveaxis(row_total, 1, 2)[..., None]
    logsum = row_max[..., 0] + jnp.log(row_total)
    part = by_seq(part.astype(BF).reshape(scenes, -1, cols))
    part = lax.all_to_all(part, "seq", 0, 0, tiled=True)
    logsum_parts = lax.all_gather(logsum, "seq", axis=0)
    top = jnp.max(logsum_parts, axis=0)
    logsum = top + jnp.log(jnp.sum(jnp.exp(logsum_parts - top), axis=0))
    share = jnp.exp(logsum_parts - logsum)
    share = share.reshape(seq_count, scenes, heads, seq_count, tp_count, picks)
    share = lax.dynamic_index_in_dim(share, seq_rank, 3, keepdims=False)
    share = jnp.transpose(share, (0, 3, 1, 4, 2)).reshape(seq_count, seq_picks, heads, 1)
    mixed = jnp.sum(in_heads(part.astype(F32)) * share, axis=0).reshape(seq_picks, cols)
    mixed_low = mixed.astype(BF)

    mixed_all = lax.all_gather(mixed_low, "tp", axis=0)
    branch = dot("tre,ted->rd", mixed_all, w_out_all)
    hidden_state = picked_rows.astype(F32) + branch
    normed2 = norm_rows(hidden_state, norm2_gain, norm2_bias).astype(BF)
    preact = jnp.dot(normed2, w_up, preferred_element_type=F32)
    active = jax.nn.gelu(preact).astype(BF)
    down = jnp.dot(active, w_down, preferred_element_type=F32).astype(BF)
    own_rows = scenes * picks

    def sum_own(value):
        value = lax.all_to_all(value.reshape(tp_count, own_rows, width), "tp", 0, 0, tiled=True)
        return jnp.sum(value.astype(F32), axis=0)

    hidden_own = lax.dynamic_slice_in_dim(hidden_state, tp_rank * own_rows, own_rows, 0)
    result_own = (hidden_own + sum_own(down)).astype(BF)
    ones = jnp.ones((own_rows, 3), BF)
    result_wide = jnp.concatenate([result_own, ones, jnp.zeros((own_rows, 13), BF)], axis=1)
    tiles = dot("kd,tdc->ktc", result_wide, unpatch_all).astype(BF)
    tile_cols = tiles.shape[2]
    pixels = tile_cols // CH
    picked = tiles.reshape(scenes, 3, rays, tp_count, pixels, CH)
    features = dot("nprtxc,tnrpxs->nrcs", picked, corners)
    first_ray = (seq_rank * tp_count + tp_rank) * rays
    live_rays = (
        (first_ray + jnp.arange(rays, dtype=jnp.int32))[None, :] < ray_count[:, None]
    ).astype(F32)

    def draw_colours(feature_rows, dec_first, dec_bias, dec_second):
        return render(feature_rows, dec_first, dec_bias, dec_second, live_rays)

    colours, pullback = jax.vjp(draw_colours, features, w_dec1, b_dec1, w_dec2)
    grad_features, dec1_part, dec1_bias_part, dec2_part = pullback(jnp.moveaxis(color_grad, 1, -1))
    grad_tiles = jnp.einsum(
        "nrcs,tnrpxs->nprtxc", grad_features, corners.astype(F32), precision=HIGH
    ).astype(BF)
    grad_tiles = grad_tiles.reshape(own_rows, tp_count, tile_cols)
    unpatch_bias_part = jnp.sum(grad_tiles.astype(F32), axis=0).reshape(-1)
    grad_result = dot("ktc,tdc->kd", grad_tiles, unpatch_all[:, :width])
    grad_tile_cols = lax.all_to_all(jnp.moveaxis(grad_tiles, 1, 0), "tp", 0, 0, tiled=True)
    result_all = lax.all_gather(result_own, "tp", axis=0, tiled=True)
    unpatch_part = dot("rd,rc->dc", result_all, grad_tile_cols.reshape(seq_picks, tile_cols))

    result_rows = lax.all_gather(grad_result.astype(BF), "tp", axis=0, tiled=True)
    down_part = dot("rf,rd->fd", active, result_rows)
    grad_active = dot("rd,fd->rf", result_rows, w_down)
    grad_preact = jax.vjp(jax.nn.gelu, preact)[1](grad_active)[0].astype(BF)
    up_part = dot("rd,rf->df", normed2, grad_preact)
    grad_normed2 = sum_own(dot("rf,df->rd", grad_preact, w_up).astype(BF))
    standard2, scale2 = standard_rows(hidden_own)
    gain2_part = jnp.sum(grad_normed2 * standard2, axis=0)
    shift2_part = jnp.sum(grad_normed2, axis=0)
    grad_hidden = grad_result + norm_back(standard2, scale2, norm2_gain, grad_normed2)
    hidden_rows = lax.all_gather(grad_hidden.astype(BF), "tp", axis=0, tiled=True)
    out_part = dot("re,rd->ed", mixed_low, hidden_rows)
    grad_mixed = dot("rd,ed->re", hidden_rows, w_out).astype(BF)
    inner = jnp.sum(in_heads(mixed * grad_mixed.astype(F32)), axis=-1)
    inner = lax.all_gather(inner.T, "seq", axis=0)
    inner = inner.reshape(seq_count, heads, tp_count, scenes, picks)
    inner = jnp.transpose(inner, (3, 1, 0, 2, 4)).reshape(scenes, heads, -1)
    hidden_cols = lax.dynamic_slice_in_dim(hidden_rows, tp_rank * cols, cols, 1)
    sent = lax.all_gather(jnp.concatenate([grad_mixed, hidden_cols], axis=1), "seq", axis=0)
    grad_heads = in_heads(by_scene(sent[..., :cols]))
    hidden_cols = sent[..., cols:].reshape(all_picks, cols)

    scores = dot("nqhd,nkhd->nhqk", query_heads, key_heads) * score_scale
    shares = jnp.exp(scores - logsum[..., None])
    grad_shares = dot("nqhd,nkhd->nhqk", grad_heads, value_heads)
    grad_scores = (shares * (grad_shares - inner[..., None])).astype(BF) * BF(score_scale)
    grad_query = dot("nhqk,nkhd->nqhd", grad_scores, key_heads)
    grad_key = dot("nhqk,nqhd->nkhd", grad_scores, query_heads)
    grad_value = dot("nhqk,nqhd->nkhd", shares.astype(BF), grad_heads)

    def flat(value):
        return value.reshape(value.shape[:2] + (cols,))

    grad_kv = jnp.concatenate([flat(grad_key), flat(grad_value)], axis=-1).astype(BF)
    grad_query = by_seq(flat(grad_query).astype(BF)).reshape(all_picks, cols)
    grad_query = hyper_sum(grad_query, ("seq",))
    scattered = dot("kr,kd->rd", onehot, jnp.concatenate([grad_query, hidden_cols], axis=1))
    scattered = scattered.astype(BF).reshape(scenes, plane_local, 2 * cols)
    grad_query = scattered[..., :cols]
    query_part = dot("nrd,nre->de", plane_normed, grad_query)
    kv_part = dot("nrd,nre->de", normed, grad_kv)

    kv_sum = jnp.sum(grad_kv.astype(F32), axis=(0, 1))
    query_sum = jnp.sum(grad_query.astype(F32), axis=(0, 1))
    key_wide, query_wide = key_weight.astype(F32), w_query.astype(F32)
    shift1_part = jnp.sum(key_wide * kv_sum, axis=1) + jnp.sum(query_wide * query_sum, axis=1)
    product = jnp.sum(key_wide * kv_part, axis=1) + jnp.sum(query_wide * query_part, axis=1)
    gain1_part = (product - norm1_bias * shift1_part) / norm1_gain

    small = [gain1_part, shift1_part, gain2_part, shift2_part, unpatch_bias_part]
    small += [dec1_part.reshape(-1), dec1_bias_part, dec2_part.reshape(-1)]
    ends = [0]
    for piece in small:
        ends.append(ends[-1] + piece.shape[0])
    small = hyper_sum(jnp.concatenate(small), ("tp", "seq"))
    small = [small[a:b] for a, b in zip(ends, ends[1:])]

    def own_piece(value, axis=0):
        size = value.shape[axis] // tp_count
        return lax.dynamic_slice_in_dim(value, tp_rank * size, size, axis)

    dec1_grad = own_piece(small[5].reshape(w_dec1.shape), 1)
    dec2_grad = own_piece(small[7].reshape(w_dec2.shape), 0)

    patch_sent = grad_kv[:, :patch_local].reshape(scenes, tp_count, own_patch, 2 * cols)
    patch_sent = lax.all_to_all(jnp.moveaxis(patch_sent, 1, 0), "tp", 0, 0, tiled=True)
    plane_sent = jnp.concatenate([grad_kv[:, patch_local:], scattered], axis=-1)
    plane_sent = plane_sent.reshape(scenes, tp_count, own_plane, 4 * cols)
    plane_sent = lax.all_to_all(jnp.moveaxis(plane_sent, 1, 0), "tp", 0, 0, tiled=True)
    patch_part = dot("tnre,tde->nrd", patch_sent, qkv_all[..., : 2 * cols])
    plane_part = dot("tnre,tde->nrd", plane_sent[..., : 3 * cols], qkv_all)
    plane_extra = jnp.moveaxis(plane_sent[..., 3 * cols :], 0, 2).reshape(scenes, own_plane, width)

    def own_grad(token_rows, own, grad):
        rows = lax.dynamic_slice_in_dim(token_rows, tp_rank * own, own, 1).astype(F32)
        standard, scale = standard_rows(rows)
        return norm_back(standard, scale, norm1_gain, grad)

    patch_grad = own_grad(patch_tokens, own_patch, patch_part)
    plane_grad = own_grad(plane_tokens, own_plane, plane_part) + plane_extra.astype(F32)

    first = (out_part, up_part, down_part, unpatch_part)
    first = lax.psum(tuple(value.astype(BF) for value in first), "seq")
    second = lax.psum((query_part.astype(BF), kv_part.astype(BF)), "seq")
    first = [value.astype(F32) for value in first]
    second = [value.astype(F32) for value in second]
    return (
        jnp.moveaxis(colours, -1, 1),
        patch_grad,
        plane_grad,
        own_piece(small[0]),
        own_piece(small[1]),
        second[0],
        second[1][:, :cols],
        second[1][:, cols:],
        first[0],
        own_piece(small[2]),
        own_piece(small[3]),
        first[1],
        first[2],
        first[3],
        own_piece(small[4]),
        dec1_grad,
        own_piece(small[6]),
        dec2_grad,
    )


def solution(mesh):
    in_specs = (
        P(None, "seq", None),
        P(None, "seq", None),
        P(),
        P(),
        P(None, "tp"),
        P(None, "tp"),
        P(None, "tp"),
        P("tp", None),
        P(),
        P(),
        P(None, "tp"),
        P("tp", None),
        P(None, "tp"),
        P("tp"),
        P(),
        P(),
        P(),
        P(None, None, "seq"),
        P(None, "seq", None, "tp", None),
        P(),
        P(None, None, ("seq", "tp")),
    )
    out_specs = (
        P(None, None, ("seq", "tp")),
        P(None, ("seq", "tp"), None),
        P(None, ("seq", "tp"), None),
        P("tp"),
        P("tp"),
        P(None, "tp"),
        P(None, "tp"),
        P(None, "tp"),
        P("tp", None),
        P("tp"),
        P("tp"),
        P(None, "tp"),
        P("tp", None),
        P(None, "tp"),
        P("tp"),
        P(None, "tp"),
        P("tp"),
        P("tp", None),
    )
    return jax.shard_map(
        on_device, mesh=mesh, in_specs=in_specs, out_specs=out_specs, check_vma=False
    )
```

```python
import functools

import jax
import jax.numpy as jnp
from jax import lax
from jax.experimental import pallas as pl
from jax.experimental.pallas import tpu as pltpu
from jax.sharding import PartitionSpec as P

HEAD_DIM = 64
CH = 32
TRI_SIDE = 32
BF = jnp.bfloat16
F32 = jnp.float32
HIGH = lax.Precision.HIGHEST


def dot(spec, *operands):
    return jnp.einsum(spec, *operands, preferred_element_type=F32)


def standard_rows(token_rows):
    centre = jnp.mean(token_rows, axis=-1, keepdims=True)
    offset = token_rows - centre
    spread = jnp.mean(offset * offset, axis=-1, keepdims=True)
    scale = lax.rsqrt(spread + 1e-05)
    return offset * scale, scale


def norm_rows(token_rows, norm_gain, norm_shift):
    return standard_rows(token_rows)[0] * norm_gain + norm_shift


def norm_back(standard, scale, norm_gain, grad):
    scaled = grad * norm_gain
    first = jnp.mean(scaled, axis=-1, keepdims=True)
    second = jnp.mean(scaled * standard, axis=-1, keepdims=True)
    return scale * (scaled - first - standard * second)


def xor_pairs(size, mask):
    return [(i, i ^ mask) for i in range(size)]


def hyper_sum(value, axes):
    for axis in axes:
        size = lax.axis_size(axis)
        mask = 1
        while mask < size:
            value = value + lax.ppermute(value, axis, xor_pairs(size, mask))
            mask *= 2
    return value


def block_rows(rows, limit):
    best = rows
    for size in range(16, limit + 1, 16):
        if rows % size == 0:
            best = size
    return best


def params():
    return pltpu.CompilerParams(vmem_limit_bytes=44 * 2**20)


def cost(flops, bytes_accessed, transcendentals=0):
    return pl.CostEstimate(
        flops=flops, bytes_accessed=bytes_accessed, transcendentals=transcendentals
    )


def project_kernel(weight_count, rows_ref, gain_ref, bias_ref, *refs):
    weights, (normed_ref, kv_ref, *query_refs) = refs[:weight_count], refs[weight_count:]
    rows = rows_ref[...].astype(F32)
    normed = norm_rows(rows, gain_ref[...], bias_ref[...]).astype(BF)
    normed_ref[...] = normed
    made = [jnp.dot(normed, w[...], preferred_element_type=F32).astype(BF) for w in weights]
    kv_ref[...] = jnp.concatenate(made[:2], axis=1)
    for ref, value in zip(query_refs, made[2:]):
        ref[...] = value


def project(token_rows, gain, bias, *weights):
    rows, width = token_rows.shape
    cols = weights[0].shape[1]
    block = block_rows(rows, 512)
    widths = [width, 2 * cols] + [cols] * (len(weights) - 2)
    whole = lambda i: (0, 0)
    mine = lambda i: (i, 0)
    return pl.pallas_call(
        functools.partial(project_kernel, len(weights)),
        grid=(rows // block,),
        in_specs=[
            pl.BlockSpec((block, width), mine),
            pl.BlockSpec((1, width), whole),
            pl.BlockSpec((1, width), whole),
        ]
        + [pl.BlockSpec((width, cols), whole) for _ in weights],
        out_specs=[pl.BlockSpec((block, w), mine) for w in widths],
        out_shape=[jax.ShapeDtypeStruct((rows, w), BF) for w in widths],
        compiler_params=params(),
        cost_estimate=cost(
            2 * rows * width * cols * len(weights), rows * (width + sum(widths)) * 2
        ),
        name="norm_project",
    )(token_rows, gain[None], bias[None], *weights)


def pieces_of(value):
    high = lax.reduce_precision(value, 8, 7)
    middle = lax.reduce_precision(value - high, 8, 7)
    return [high.astype(BF), middle.astype(BF), (value - high - middle).astype(BF)]


def dot_dims(left, right, left_dim, right_dim):
    dims = (((left_dim,), (right_dim,)), ((), ()))
    return lax.dot_general(left, right, dims, preferred_element_type=F32)


def attend_kernel(heads, q_ref, first_ref, second_ref, out_ref, logsum_ref):
    cols = heads * HEAD_DIM
    parts, stats = [], []
    for h in range(heads):
        here = slice(h * HEAD_DIM, (h + 1) * HEAD_DIM)
        there = slice(cols + h * HEAD_DIM, cols + (h + 1) * HEAD_DIM)
        query = q_ref[0, :, here] * BF(HEAD_DIM**-0.5)
        scores = [dot_dims(ref[0, :, here], query, 1, 1) for ref in (first_ref, second_ref)]
        top = jnp.maximum(*[jnp.max(s, axis=0, keepdims=True) for s in scores])
        raised = [jnp.exp(s - top) for s in scores]
        total = sum(jnp.sum(r, axis=0, keepdims=True) for r in raised)
        mixed = sum(
            dot_dims(ref[0, :, there], r.astype(BF), 0, 0)
            for ref, r in zip((first_ref, second_ref), raised)
        )
        parts.append(mixed / total)
        stats.append(top + jnp.log(total))
    out_ref[0] = jnp.concatenate(parts, axis=0).T.astype(BF)
    logsum_ref[0] = jnp.concatenate(stats, axis=0)


def attend(queries, first, second, heads):
    scenes, count, cols = queries.shape
    keys = first.shape[1] + second.shape[1]
    scene = lambda n: (n, 0, 0)
    return pl.pallas_call(
        functools.partial(attend_kernel, heads),
        grid=(scenes,),
        in_specs=[pl.BlockSpec((1,) + a.shape[1:], scene) for a in (queries, first, second)],
        out_specs=[
            pl.BlockSpec((1, count, cols), scene),
            pl.BlockSpec((1, heads, count), scene),
        ],
        out_shape=[
            jax.ShapeDtypeStruct((scenes, count, cols), BF),
            jax.ShapeDtypeStruct((scenes, heads, count), F32),
        ],
        compiler_params=params(),
        cost_estimate=cost(
            scenes * heads * count * keys * 16 * HEAD_DIM * 2,
            scenes * keys * cols * 4,
            scenes * heads * count * keys,
        ),
        name="attend",
    )(queries, first, second)


def attend_back_kernel(
    heads, q_ref, first_ref, second_ref, grad_ref, logsum_ref, gq_ref, ga_ref, gb_ref
):
    cols = heads * HEAD_DIM
    count = q_ref.shape[1]
    scale = HEAD_DIM**-0.5
    cut = [slice(h * HEAD_DIM, (h + 1) * HEAD_DIM) for h in range(heads)]
    query = [q_ref[0, :, c] * BF(scale) for c in cut]
    grad = [grad_ref[0, :, c] for c in cut]
    ones = jnp.ones((8, HEAD_DIM), F32)
    inner = [
        lax.dot_general(
            ones,
            grad_ref[0, :, cols + c.start : cols + c.stop].astype(F32) * g.astype(F32),
            (((1,), (1,)), ((), ())),
            precision=HIGH,
            preferred_element_type=F32,
        )[:1]
        for c, g in zip(cut, grad)
    ]
    totals = tuple(jnp.zeros((HEAD_DIM, count), F32) for _ in cut)
    for ref, out_ref in ((first_ref, ga_ref), (second_ref, gb_ref)):
        rows = ref.shape[1]
        block = block_rows(rows, 256)

        def step(i, totals, ref=ref, out_ref=out_ref, block=block):
            place = pl.ds(pl.multiple_of(i * block, block), block)
            keys, grads, sums = [], [], []
            for h in range(heads):
                key = ref[0, place, cut[h]]
                value = ref[0, place, slice(cols + cut[h].start, cols + cut[h].stop)]
                shares = jnp.exp(dot_dims(key, query[h], 1, 1) - logsum_ref[0, h : h + 1, :])
                grad_shares = dot_dims(value, grad[h], 1, 1)
                grad_scores = (shares * (grad_shares - inner[h])).astype(BF)
                keys.append(jnp.dot(grad_scores, query[h], preferred_element_type=F32))
                grads.append(jnp.dot(shares.astype(BF), grad[h], preferred_element_type=F32))
                sums.append(totals[h] + dot_dims(key, grad_scores, 0, 0))
            out_ref[0, place, :] = jnp.concatenate(keys + grads, axis=1).astype(BF)
            return tuple(sums)

        totals = lax.fori_loop(0, rows // block, step, totals)
    gq_ref[0] = (jnp.concatenate(totals, axis=0) * scale).T.astype(BF)


def attend_back(queries, first, second, grad, logsum, heads):
    scenes, count, cols = queries.shape
    keys = first.shape[1] + second.shape[1]
    scene = lambda n: (n, 0, 0)
    operands = (queries, first, second, grad, logsum)
    return pl.pallas_call(
        functools.partial(attend_back_kernel, heads),
        grid=(scenes,),
        in_specs=[pl.BlockSpec((1,) + a.shape[1:], scene) for a in operands],
        out_specs=[pl.BlockSpec((1,) + a.shape[1:], scene) for a in (queries, first, second)],
        out_shape=[jax.ShapeDtypeStruct(a.shape, BF) for a in (queries, first, second)],
        compiler_params=params(),
        cost_estimate=cost(
            scenes * heads * count * keys * 40 * HEAD_DIM * 2,
            scenes * keys * cols * 8,
            scenes * heads * count * keys,
        ),
        name="attend_back",
    )(*operands)


def spread(value, axis):
    size, rank = lax.axis_size(axis), lax.axis_index(axis)
    out = jnp.zeros((size,) + value.shape, value.dtype)
    for mask in range(size):
        other = lax.ppermute(value, axis, xor_pairs(size, mask)) if mask else value
        out = lax.dynamic_update_index_in_dim(out, other, rank ^ mask, 0)
    return out


def split_sum(value, axis):
    size, rank = lax.axis_size(axis), lax.axis_index(axis)
    value = value.reshape((size, value.shape[0] // size) + value.shape[1:])
    total = lax.dynamic_index_in_dim(value, rank, 0, keepdims=False)
    for mask in range(1, size):
        block = lax.dynamic_index_in_dim(value, rank ^ mask, 0, keepdims=False).astype(BF)
        total = total + lax.ppermute(block, axis, xor_pairs(size, mask)).astype(F32)
    return total


def render(features, dec_first, dec_bias, dec_second, live_rays):
    preact = jnp.einsum("ch,...cs->...hs", dec_first, features, precision=HIGH) + dec_bias[:, None]
    hidden = jax.nn.silu(preact)
    output = jnp.einsum("hk,...hs->...ks", dec_second, hidden, precision=HIGH)
    samples = output.shape[-1]
    density = jax.nn.softplus(output[..., 0, :])
    colour = jax.nn.sigmoid(output[..., 1:, :])
    optical = density * (2.0 / samples)
    place = jnp.arange(samples)
    before = (place[:, None] < place[None, :]).astype(F32)
    through = jnp.exp(-jnp.einsum("...t,ts->...s", optical, before, precision=HIGH))
    weight = through * (1.0 - jnp.exp(-optical))
    return jnp.sum(weight[..., None, :] * colour, axis=-1) * live_rays[..., None]


def on_device(
    patch_tokens,
    plane_tokens,
    norm1_gain,
    norm1_bias,
    w_query,
    w_key,
    w_value,
    w_out,
    norm2_gain,
    norm2_bias,
    w_up,
    w_down,
    w_unpatch,
    b_unpatch,
    w_dec1,
    b_dec1,
    w_dec2,
    tile_index,
    corner_weights,
    ray_count,
    color_grad,
):
    scenes, patch_local, width = patch_tokens.shape
    plane_local = plane_tokens.shape[1]
    seq_count, tp_count = lax.axis_size("seq"), lax.axis_size("tp")
    seq_rank, tp_rank = lax.axis_index("seq"), lax.axis_index("tp")
    own_patch = patch_local // tp_count
    own_plane = plane_local // tp_count
    cols = w_query.shape[1]
    heads = cols // HEAD_DIM
    ray_seq = tile_index.shape[2]
    rays = ray_seq // tp_count
    picks = 3 * rays
    seq_picks = tp_count * scenes * picks
    all_picks = seq_count * seq_picks
    score_scale = HEAD_DIM**-0.5

    base = (jnp.arange(3, dtype=jnp.int32) * (TRI_SIDE * TRI_SIDE))[None, :, None]
    ids = (tile_index + base).reshape(scenes, 3, tp_count, rays)
    ids = jnp.transpose(ids, (2, 0, 1, 3)).reshape(tp_count, scenes, picks)
    ids = jnp.broadcast_to(ids[None], (seq_count,) + ids.shape)
    ids = lax.all_to_all(ids, "seq", 0, 0, tiled=True)
    plane_normed, plane_kv, query_rows = project(
        plane_tokens.reshape(-1, width), norm1_gain, norm1_bias, w_key, w_value, w_query
    )
    ids, query_rows = lax.optimization_barrier((ids, query_rows))
    local_ids = ids - seq_rank * plane_local
    inside = (local_ids >= 0) & (local_ids < plane_local)
    scene_base = (jnp.arange(scenes, dtype=jnp.int32) * plane_local)[None, None, :, None]
    row_ids = jnp.where(inside, local_ids + scene_base, -1).reshape(all_picks)
    onehot = (
        row_ids[:, None] == jnp.arange(scenes * plane_local, dtype=jnp.int32)[None, :]
    ).astype(BF)

    own_cols = lax.dynamic_slice_in_dim(plane_tokens, tp_rank * cols, cols, 2)
    chosen = jnp.dot(onehot, jnp.concatenate([query_rows, own_cols.reshape(-1, cols)], axis=1))
    chosen, corner_weights, w_key_later, patch_tokens = lax.optimization_barrier(
        (chosen, corner_weights, w_key, patch_tokens)
    )
    chosen = split_sum(chosen, "seq").astype(BF)
    queries = spread(chosen[:, :cols], "seq").reshape(all_picks, cols)
    picked_cols = chosen[:, cols:]

    w_out_all = lax.all_gather(w_out, "tp", axis=0)
    unpatch_all = lax.all_gather(w_unpatch, "tp", axis=0)
    qkv_weight = jnp.concatenate([w_key_later, w_value, w_query], axis=1)
    qkv_all = lax.all_gather(qkv_weight, "tp", axis=0)

    corners = corner_weights.reshape(
        scenes, tp_count, rays, 3, corner_weights.shape[3], corner_weights.shape[4]
    )
    corners = lax.all_to_all(jnp.moveaxis(corners, 1, 0), "tp", 0, 0, tiled=True)

    patch_normed, patch_kv = project(
        patch_tokens.reshape(-1, width), norm1_gain, norm1_bias, w_key, w_value
    )
    queries, corners, patch_kv, picked_cols, w_out_all = lax.optimization_barrier(
        (queries, corners, patch_kv, picked_cols, w_out_all)
    )
    plane_kv = plane_kv.reshape(scenes, plane_local, 2 * cols)
    key_weight = qkv_weight[:, : 2 * cols]
    patch_kv = patch_kv.reshape(scenes, patch_local, 2 * cols)

    def by_scene(value):
        value = value.reshape(seq_count, tp_count, scenes, picks, -1)
        return jnp.moveaxis(value, 2, 0).reshape(scenes, seq_count * tp_count * picks, -1)

    def by_seq(value):
        value = value.reshape(scenes, seq_count, tp_count, picks, -1)
        return jnp.moveaxis(value, 0, 2).reshape(seq_count, seq_picks, -1)

    def in_heads(value):
        return value.reshape(value.shape[:-1] + (heads, HEAD_DIM))

    queries = by_scene(queries)
    part, logsum = attend(queries, patch_kv, plane_kv, heads)
    part = by_seq(part)
    flat = jnp.stack(pieces_of(logsum)).reshape(-1)
    stat_rows = -(-flat.shape[0] // (16 * cols)) * 16
    flat = jnp.pad(flat, (0, stat_rows * cols - flat.shape[0])).reshape(stat_rows, cols)
    flat = jnp.broadcast_to(flat[None], (seq_count, stat_rows, cols))
    part = lax.all_to_all(jnp.concatenate([part, flat], axis=1), "seq", 0, 0, tiled=True)
    logsums = part[:, seq_picks:].reshape(seq_count, -1)[:, : 3 * logsum.size]
    logsums = jnp.sum(logsums.reshape((seq_count, 3) + logsum.shape).astype(F32), axis=1)
    top = jnp.max(logsums, axis=0)
    logsum = top + jnp.log(jnp.sum(jnp.exp(logsums - top), axis=0))
    shares = jnp.exp(logsums - logsum)
    shares = shares.reshape(seq_count, scenes, heads, seq_count, tp_count, picks)
    shares = lax.dynamic_index_in_dim(shares, seq_rank, 3, keepdims=False)
    shares = jnp.transpose(shares, (0, 3, 1, 4, 2)).reshape(seq_count, seq_picks, heads, 1)
    mixed_low = jnp.sum(in_heads(part[:, :seq_picks].astype(F32)) * shares, axis=0)
    mixed_low = mixed_low.reshape(seq_picks, cols).astype(BF)

    bias_rows = jnp.stack(pieces_of(b_unpatch) + [jnp.zeros_like(b_unpatch, BF)] * 13)
    mixed_low = jnp.concatenate([mixed_low, picked_cols], axis=1)
    mixed_low = jnp.concatenate([mixed_low, bias_rows], axis=0)
    mixed_all = lax.all_gather(mixed_low, "tp", axis=0)
    bias_all = jnp.sum(mixed_all[:, seq_picks : seq_picks + 3].astype(F32), axis=1)
    mixed_all, unpatch_all = lax.optimization_barrier((mixed_all[:, :seq_picks], unpatch_all))
    branch = dot("tre,ted->rd", mixed_all[..., :cols], w_out_all)
    picked_rows = jnp.moveaxis(mixed_all[..., cols:], 0, 1).reshape(seq_picks, width)
    picked_rows = picked_rows.astype(F32)
    hidden_state = picked_rows + branch
    normed2 = norm_rows(hidden_state, norm2_gain, norm2_bias).astype(BF)
    preact = jnp.dot(normed2, w_up, preferred_element_type=F32)
    active = jax.nn.gelu(preact).astype(BF)
    down = jnp.dot(active, w_down, preferred_element_type=F32).astype(BF)
    own_rows = scenes * picks

    def to_all(value):
        value = jnp.broadcast_to(value[None], (seq_count,) + value.shape)
        value = value.reshape((seq_count * tp_count,) + value.shape[2:])
        return lax.all_to_all(value, ("seq", "tp"), 0, 0, tiled=True)

    def tp_first(value):
        value = value.reshape((seq_count, tp_count, own_rows) + value.shape[1:])
        return jnp.moveaxis(value, 1, 0).reshape((all_picks,) + value.shape[3:])

    def sum_own(value):
        value = lax.all_to_all(value.reshape(tp_count, own_rows, width), "tp", 0, 0, tiled=True)
        return jnp.sum(value.astype(F32), axis=0)

    hidden_own = lax.dynamic_slice_in_dim(hidden_state, tp_rank * own_rows, own_rows, 0)
    result_own = (hidden_own + sum_own(down)).astype(BF)
    normed2_own = lax.dynamic_slice_in_dim(normed2, tp_rank * own_rows, own_rows, 0)
    tiles = (dot("kd,tdc->ktc", result_own, unpatch_all) + bias_all).astype(BF)
    tile_cols = tiles.shape[2]
    pixels = tile_cols // CH
    picked = tiles.reshape(scenes, 3, rays, tp_count, pixels, CH)
    features = dot("nprtxc,tnrpxs->nrcs", picked, corners)
    first_ray = (seq_rank * tp_count + tp_rank) * rays
    live_rays = (
        (first_ray + jnp.arange(rays, dtype=jnp.int32))[None, :] < ray_count[:, None]
    ).astype(F32)

    def draw_colours(feature_rows, dec_first, dec_bias, dec_second):
        return render(feature_rows, dec_first, dec_bias, dec_second, live_rays)

    colours, pullback = jax.vjp(draw_colours, features, w_dec1, b_dec1, w_dec2)
    grad_features, dec1_part, dec1_bias_part, dec2_part = pullback(jnp.moveaxis(color_grad, 1, -1))
    grad_tiles = jnp.einsum(
        "nrcs,tnrpxs->nprtxc", grad_features, corners.astype(F32), precision=HIGH
    ).astype(BF)
    grad_tiles = grad_tiles.reshape(own_rows, tp_count, tile_cols)
    grad_result = dot("ktc,tdc->kd", grad_tiles, unpatch_all)
    grad_result_low = grad_result.astype(BF)
    result_rows = lax.all_gather(grad_result_low, "tp", axis=0, tiled=True)
    early = jnp.concatenate([normed2_own, result_own], axis=1)
    grad_active = dot("rd,fd->rf", result_rows, w_down)
    grad_preact = jax.vjp(jax.nn.gelu, preact)[1](grad_active)[0].astype(BF)
    grad_normed2 = dot("rf,df->rd", grad_preact, w_up).astype(BF)
    grad_normed2, qkv_all, early, late = lax.optimization_barrier(
        (grad_normed2, qkv_all, early, grad_result_low)
    )
    early = spread(early, "seq").reshape(-1, 2 * width)
    late = spread(late, "seq").reshape(-1, width)
    grad_normed2 = sum_own(grad_normed2)
    standard2, scale2 = standard_rows(hidden_own)
    gain2_part = jnp.sum(grad_normed2 * standard2, axis=0)
    shift2_part = jnp.sum(grad_normed2, axis=0)
    grad_hidden = grad_result + norm_back(standard2, scale2, norm2_gain, grad_normed2)
    def to_owner(value):
        return lax.all_to_all(value, "tp", 0, 0, tiled=True)

    def by_owner(value, own):
        value = value.reshape(-1, tp_count, own, value.shape[-1])
        return jnp.moveaxis(value, 1, 0)

    normed_picks = norm_rows(picked_rows, norm1_gain, norm1_bias).astype(BF)
    hidden_low = grad_hidden.astype(BF)
    grad_mixed = dot("kd,ted->tke", hidden_low, w_out_all).astype(BF)
    hidden_cols = jnp.moveaxis(hidden_low.reshape(own_rows, tp_count, cols), 1, 0)
    mixed_own = lax.dynamic_slice_in_dim(mixed_all[..., :cols], tp_rank * own_rows, own_rows, 1)
    sent = to_all(jnp.concatenate([grad_mixed, mixed_own], axis=-1))
    early = lax.all_gather(early, "tp", axis=0, tiled=True)
    late = lax.all_gather(late, "tp", axis=0, tiled=True)
    later = jnp.concatenate([hidden_cols, jnp.moveaxis(grad_tiles, 1, 0)], axis=-1)
    sent, later, early = lax.optimization_barrier((sent, later, early))
    later = to_all(later).reshape(all_picks, cols + tile_cols)

    scene_sent = by_scene(sent)
    made, kv_sent = [], []
    for n in range(scenes):
        here = [value[n : n + 1] for value in (queries, patch_kv, plane_kv, scene_sent, logsum)]
        if n == scenes - 1:
            here, later = lax.optimization_barrier((here, later))
        one = attend_back(*here, heads)
        if n:
            one, kv_sent[-1] = lax.optimization_barrier((one, kv_sent[-1]))
        made.append(one)
        kv_sent.append(
            to_owner(
                jnp.concatenate([by_owner(one[1], own_patch), by_owner(one[2], own_plane)], axis=2)
            )
        )
    grad_query = jnp.concatenate([one[0] for one in made], axis=0)
    flat_patch = [one[1].reshape(-1, 2 * cols) for one in made]
    flat_plane = [one[2].reshape(-1, 2 * cols) for one in made]
    hidden_cols = later[:, :cols]
    hidden_cols_all = lax.all_gather(hidden_cols, "tp", axis=0)
    out_grad = dot(
        "re,trd->etd", sent.reshape(all_picks, 2 * cols)[:, cols:], hidden_cols_all
    ).reshape(cols, width)
    grad_query = split_sum(by_seq(grad_query).reshape(all_picks, cols), "seq").astype(BF)
    kv_part = sum(
        dot("rd,re->de", rows[n * (rows.shape[0] // scenes) :][: rows.shape[0] // scenes], flat[n])
        for rows, flat in ((patch_normed, flat_patch), (plane_normed, flat_plane))
        for n in range(scenes)
    )
    grad_query, kv_part, late, place = lax.optimization_barrier(
        (grad_query, kv_part, late, tp_rank)
    )
    patch_own = lax.dynamic_slice_in_dim(patch_tokens, place * own_patch, own_patch, 1)
    plane_own = lax.dynamic_slice_in_dim(plane_tokens, place * own_plane, own_plane, 1)
    query_part = dot("rd,re->de", normed_picks, grad_query)
    grad_query_all = spread(grad_query, "seq").reshape(all_picks, cols)
    scattered = dot("kr,kd->rd", onehot, jnp.concatenate([grad_query_all, hidden_cols], axis=1))
    scattered = scattered.astype(BF)

    kv_sum = sum(jnp.sum(flat.astype(F32), axis=0) for flat in flat_patch + flat_plane)
    query_sum = jnp.sum(grad_query.astype(F32), axis=0)
    key_wide, query_wide = key_weight.astype(F32), w_query.astype(F32)
    shift1_part = jnp.sum(key_wide * kv_sum, axis=1) + jnp.sum(query_wide * query_sum, axis=1)
    product = jnp.sum(key_wide * kv_part, axis=1) + jnp.sum(query_wide * query_part, axis=1)
    gain1_part = (product - norm1_bias * shift1_part) / norm1_gain

    normed2_all, result_all, grad_result_all = early[:, :width], early[:, width:], late
    tile_cols_all = tp_first(later[:, cols:])
    unpatch_grad = dot("rd,rc->dc", result_all, tile_cols_all)
    unpatch_bias_grad = jnp.sum(tile_cols_all.astype(F32), axis=0)
    preact_all = jnp.dot(normed2_all, w_up, preferred_element_type=F32)
    active_all, gelu_pull = jax.vjp(jax.nn.gelu, preact_all)
    down_grad = dot("rf,rd->fd", active_all.astype(BF), grad_result_all)
    grad_preact_all = gelu_pull(dot("rd,fd->rf", grad_result_all, w_down))[0].astype(BF)
    up_grad = dot("rd,rf->df", normed2_all, grad_preact_all)

    scattered, kv_sent, up_grad = lax.optimization_barrier((scattered, kv_sent, up_grad))
    extra_sent = to_owner(by_owner(scattered, own_plane))

    def own_sums(pieces):
        pieces = [piece.reshape(tp_count, -1) for piece in pieces]
        ends = [0]
        for piece in pieces:
            ends.append(ends[-1] + piece.shape[1])
        pieces, _ = lax.optimization_barrier((jnp.concatenate(pieces, axis=1), extra_sent))
        total = jnp.sum(to_all(pieces), axis=0)
        return [total[a:b] for a, b in zip(ends, ends[1:])]

    dec1_cols = w_dec1.shape[1] // tp_count
    dec1_part = jnp.moveaxis(dec1_part.reshape(-1, tp_count, dec1_cols), 1, 0)
    (
        gain1_grad,
        shift1_grad,
        gain2_grad,
        shift2_grad,
        dec1_grad,
        dec1_bias_grad,
        dec2_grad,
    ) = own_sums(
        [gain1_part, shift1_part, gain2_part, shift2_part, dec1_part, dec1_bias_part, dec2_part]
    )

    kv_sent = jnp.concatenate(kv_sent, axis=1)
    kv_back = dot("tnre,tde->nrd", kv_sent, qkv_all[..., : 2 * cols])
    patch_part, plane_part = kv_back[:, :own_patch], kv_back[:, own_patch:]
    plane_part = plane_part + dot("tnre,tde->nrd", extra_sent[..., :cols], qkv_all[..., 2 * cols :])
    plane_extra = jnp.moveaxis(extra_sent[..., cols:], 0, 2).reshape(scenes, own_plane, width)

    def own_grad(rows, grad):
        standard, scale = standard_rows(rows.astype(F32))
        return norm_back(standard, scale, norm1_gain, grad)

    patch_grad = own_grad(patch_own, patch_part)
    plane_grad = own_grad(plane_own, plane_part) + plane_extra.astype(F32)

    qkv_grad = lax.psum(jnp.concatenate([kv_part, query_part], axis=1).astype(BF), "seq")
    qkv_grad = qkv_grad.astype(F32)
    return (
        jnp.moveaxis(colours, -1, 1),
        patch_grad,
        plane_grad,
        gain1_grad,
        shift1_grad,
        qkv_grad[:, 2 * cols :],
        qkv_grad[:, :cols],
        qkv_grad[:, cols : 2 * cols],
        out_grad,
        gain2_grad,
        shift2_grad,
        up_grad,
        down_grad,
        unpatch_grad,
        unpatch_bias_grad,
        dec1_grad.reshape(-1, dec1_cols),
        dec1_bias_grad,
        dec2_grad.reshape(-1, w_dec2.shape[1]),
    )


def solution(mesh):
    in_specs = (
        P(None, "seq", None),
        P(None, "seq", None),
        P(),
        P(),
        P(None, "tp"),
        P(None, "tp"),
        P(None, "tp"),
        P("tp", None),
        P(),
        P(),
        P(None, "tp"),
        P("tp", None),
        P(None, "tp"),
        P("tp"),
        P(),
        P(),
        P(),
        P(None, None, "seq"),
        P(None, "seq", None, "tp", None),
        P(),
        P(None, None, ("seq", "tp")),
    )
    out_specs = (
        P(None, None, ("seq", "tp")),
        P(None, ("seq", "tp"), None),
        P(None, ("seq", "tp"), None),
        P("tp"),
        P("tp"),
        P(None, "tp"),
        P(None, "tp"),
        P(None, "tp"),
        P("tp", None),
        P("tp"),
        P("tp"),
        P(None, "tp"),
        P("tp", None),
        P(None, "tp"),
        P("tp"),
        P(None, "tp"),
        P("tp"),
        P("tp", None),
    )
    return jax.shard_map(
        on_device, mesh=mesh, in_specs=in_specs, out_specs=out_specs, check_vma=False
    )
```

```python
import functools

import jax
import jax.numpy as jnp
from jax import lax
from jax.experimental import pallas as pl
from jax.experimental.pallas import tpu as pltpu
from jax.sharding import PartitionSpec as P

HEAD_DIM = 64
CH = 32
TRI_SIDE = 32
BF = jnp.bfloat16
F32 = jnp.float32
HIGH = lax.Precision.HIGHEST


def dot(spec, *operands):
    return jnp.einsum(spec, *operands, preferred_element_type=F32)


def standard_rows(token_rows):
    centre = jnp.mean(token_rows, axis=-1, keepdims=True)
    offset = token_rows - centre
    spread = jnp.mean(offset * offset, axis=-1, keepdims=True)
    scale = lax.rsqrt(spread + 1e-05)
    return offset * scale, scale


def norm_rows(token_rows, norm_gain, norm_shift):
    return standard_rows(token_rows)[0] * norm_gain + norm_shift


def norm_back(standard, scale, norm_gain, grad):
    scaled = grad * norm_gain
    first = jnp.mean(scaled, axis=-1, keepdims=True)
    second = jnp.mean(scaled * standard, axis=-1, keepdims=True)
    return scale * (scaled - first - standard * second)


def xor_pairs(size, mask):
    return [(i, i ^ mask) for i in range(size)]


def hyper_sum(value, axes):
    for axis in axes:
        size = lax.axis_size(axis)
        mask = 1
        while mask < size:
            value = value + lax.ppermute(value, axis, xor_pairs(size, mask))
            mask *= 2
    return value


def block_rows(rows, limit):
    best = rows
    for size in range(16, limit + 1, 16):
        if rows % size == 0:
            best = size
    return best


def params():
    return pltpu.CompilerParams(vmem_limit_bytes=60 * 2**20)


def cost(flops, bytes_accessed, transcendentals=0):
    return pl.CostEstimate(
        flops=flops, bytes_accessed=bytes_accessed, transcendentals=transcendentals
    )


def project_kernel(weight_count, rows_ref, gain_ref, bias_ref, *refs):
    weights, (normed_ref, kv_ref, *query_refs) = refs[:weight_count], refs[weight_count:]
    rows = rows_ref[...].astype(F32)
    normed = norm_rows(rows, gain_ref[...], bias_ref[...]).astype(BF)
    normed_ref[...] = normed
    made = [jnp.dot(normed, w[...], preferred_element_type=F32).astype(BF) for w in weights]
    kv_ref[...] = jnp.concatenate(made[:2], axis=1)
    for ref, value in zip(query_refs, made[2:]):
        ref[...] = value


def project(token_rows, gain, bias, *weights):
    rows, width = token_rows.shape
    cols = weights[0].shape[1]
    block = block_rows(rows, 512)
    widths = [width, 2 * cols] + [cols] * (len(weights) - 2)
    whole = lambda i: (0, 0)
    mine = lambda i: (i, 0)
    return pl.pallas_call(
        functools.partial(project_kernel, len(weights)),
        grid=(rows // block,),
        in_specs=[
            pl.BlockSpec((block, width), mine),
            pl.BlockSpec((1, width), whole),
            pl.BlockSpec((1, width), whole),
        ]
        + [pl.BlockSpec((width, cols), whole) for _ in weights],
        out_specs=[pl.BlockSpec((block, w), mine) for w in widths],
        out_shape=[jax.ShapeDtypeStruct((rows, w), BF) for w in widths],
        compiler_params=params(),
        cost_estimate=cost(
            2 * rows * width * cols * len(weights), rows * (width + sum(widths)) * 2
        ),
        name="norm_project",
    )(token_rows, gain[None], bias[None], *weights)


def pieces_of(value):
    high = lax.reduce_precision(value, 8, 7)
    middle = lax.reduce_precision(value - high, 8, 7)
    return [high.astype(BF), middle.astype(BF), (value - high - middle).astype(BF)]


def dot_dims(left, right, left_dim, right_dim):
    dims = (((left_dim,), (right_dim,)), ((), ()))
    return lax.dot_general(left, right, dims, preferred_element_type=F32)


def attend_kernel(heads, q_ref, first_ref, second_ref, out_ref, logsum_ref):
    cols = heads * HEAD_DIM
    parts, stats = [], []
    for h in range(heads):
        here = slice(h * HEAD_DIM, (h + 1) * HEAD_DIM)
        there = slice(cols + h * HEAD_DIM, cols + (h + 1) * HEAD_DIM)
        query = q_ref[0, :, here] * BF(HEAD_DIM**-0.5)
        scores = [dot_dims(ref[0, :, here], query, 1, 1) for ref in (first_ref, second_ref)]
        top = jnp.maximum(*[jnp.max(s, axis=0, keepdims=True) for s in scores])
        raised = [jnp.exp(s - top) for s in scores]
        total = sum(jnp.sum(r, axis=0, keepdims=True) for r in raised)
        mixed = sum(
            dot_dims(ref[0, :, there], r.astype(BF), 0, 0)
            for ref, r in zip((first_ref, second_ref), raised)
        )
        parts.append(mixed / total)
        stats.append(top + jnp.log(total))
    out_ref[0] = jnp.concatenate(parts, axis=0).T.astype(BF)
    logsum_ref[0] = jnp.concatenate(stats, axis=0)


def attend(queries, first, second, heads):
    scenes, count, cols = queries.shape
    keys = first.shape[1] + second.shape[1]
    scene = lambda n: (n, 0, 0)
    return pl.pallas_call(
        functools.partial(attend_kernel, heads),
        grid=(scenes,),
        in_specs=[pl.BlockSpec((1,) + a.shape[1:], scene) for a in (queries, first, second)],
        out_specs=[
            pl.BlockSpec((1, count, cols), scene),
            pl.BlockSpec((1, heads, count), scene),
        ],
        out_shape=[
            jax.ShapeDtypeStruct((scenes, count, cols), BF),
            jax.ShapeDtypeStruct((scenes, heads, count), F32),
        ],
        compiler_params=params(),
        cost_estimate=cost(
            scenes * heads * count * keys * 16 * HEAD_DIM * 2,
            scenes * keys * cols * 4,
            scenes * heads * count * keys,
        ),
        name="attend",
    )(queries, first, second)


def attend_back_kernel(heads, *refs):
    q_ref, first_ref, second_ref, grad_ref, logsum_ref, na_ref, nb_ref = refs[:7]
    gq_ref, ga_ref, gb_ref, part_ref, sum_ref = refs[-5:]
    if len(refs) > 12:
        part_ref[...] = refs[7][...]
        sum_ref[...] = refs[8][...]
    else:
        part_ref[...] = jnp.zeros_like(part_ref)
        sum_ref[...] = jnp.zeros_like(sum_ref)
    cols = heads * HEAD_DIM
    count = q_ref.shape[1]
    scale = HEAD_DIM**-0.5
    cut = [slice(h * HEAD_DIM, (h + 1) * HEAD_DIM) for h in range(heads)]
    query = [q_ref[0, :, c] * BF(scale) for c in cut]
    grad = [grad_ref[0, :, c] for c in cut]
    ones = jnp.ones((8, HEAD_DIM), F32)
    inner = [
        lax.dot_general(
            ones,
            grad_ref[0, :, cols + c.start : cols + c.stop].astype(F32) * g.astype(F32),
            (((1,), (1,)), ((), ())),
            precision=HIGH,
            preferred_element_type=F32,
        )[:1]
        for c, g in zip(cut, grad)
    ]
    totals = tuple(jnp.zeros((HEAD_DIM, count), F32) for _ in cut)
    for ref, out_ref, normed_ref in ((first_ref, ga_ref, na_ref), (second_ref, gb_ref, nb_ref)):
        rows = ref.shape[1]
        block = block_rows(rows, 256)

        def step(i, totals, ref=ref, out_ref=out_ref, normed_ref=normed_ref, block=block):
            place = pl.ds(pl.multiple_of(i * block, block), block)
            keys, grads, sums = [], [], []
            for h in range(heads):
                key = ref[0, place, cut[h]]
                value = ref[0, place, slice(cols + cut[h].start, cols + cut[h].stop)]
                shares = jnp.exp(dot_dims(key, query[h], 1, 1) - logsum_ref[0, h : h + 1, :])
                grad_shares = dot_dims(value, grad[h], 1, 1)
                grad_scores = (shares * (grad_shares - inner[h])).astype(BF)
                keys.append(jnp.dot(grad_scores, query[h], preferred_element_type=F32))
                grads.append(jnp.dot(shares.astype(BF), grad[h], preferred_element_type=F32))
                sums.append(totals[h] + dot_dims(key, grad_scores, 0, 0))
            made = jnp.concatenate(keys + grads, axis=1).astype(BF)
            out_ref[0, place, :] = made
            part_ref[...] += dot_dims(made, normed_ref[0, place, :], 0, 0)
            sum_ref[...] += jnp.sum(made.astype(F32), axis=0, keepdims=True)
            return tuple(sums)

        totals = lax.fori_loop(0, rows // block, step, totals)
    gq_ref[0] = (jnp.concatenate(totals, axis=0) * scale).T.astype(BF)


def attend_back(scene, queries, first, second, grad, logsum, normed_first, normed_second, before, heads):
    scenes, count, cols = queries.shape
    keys, width = first.shape[1] + second.shape[1], normed_first.shape[2]
    mine = lambda i: (scene, 0, 0)
    whole = lambda i: (0, 0)
    operands = (queries, first, second, grad, logsum, normed_first, normed_second)
    totals = [(2 * cols, width), (1, 2 * cols)]
    outs = [(1,) + a.shape[1:] for a in (queries, first, second)]
    return pl.pallas_call(
        functools.partial(attend_back_kernel, heads),
        grid=(1,),
        in_specs=[pl.BlockSpec((1,) + a.shape[1:], mine) for a in operands]
        + [pl.BlockSpec(a.shape, whole) for a in before],
        out_specs=[pl.BlockSpec(a, lambda i: (0, 0, 0)) for a in outs]
        + [pl.BlockSpec(a, whole) for a in totals],
        out_shape=[jax.ShapeDtypeStruct(a, BF) for a in outs]
        + [jax.ShapeDtypeStruct(a, F32) for a in totals],
        compiler_params=params(),
        cost_estimate=cost(
            heads * count * keys * 40 * HEAD_DIM * 2 + 4 * keys * cols * width,
            keys * (cols * 8 + width * 2),
            heads * count * keys,
        ),
        name="attend_back",
    )(*operands, *before)


def finish_kernel(cols, kv_ref, extra_ref, weight_ref, gain_ref, patch_ref, plane_ref, *outs):
    own_patch = patch_ref.shape[1]
    parts = kv_ref.shape[0]
    total = sum(dot_dims(kv_ref[t, 0], weight_ref[t, : 2 * cols], 1, 0) for t in range(parts))
    more = sum(
        dot_dims(extra_ref[t, 0, :, :cols], weight_ref[t, 2 * cols :], 1, 0)
        for t in range(parts)
    )
    grads = (total[:own_patch], total[own_patch:] + more)
    extra = jnp.concatenate([extra_ref[t, 0, :, cols:] for t in range(parts)], axis=1)
    added = (0.0, extra.astype(F32))
    for ref, out_ref, grad, plus in zip((patch_ref, plane_ref), outs, grads, added):
        standard, scale = standard_rows(ref[0].astype(F32))
        out_ref[0] = norm_back(standard, scale, gain_ref[...], grad) + plus


def finish(kv_sent, extra_sent, weights, patch_own, plane_own, gain, cols):
    parts, scenes, rows, _ = kv_sent.shape
    width = weights.shape[2]
    scene = lambda n: (n, 0, 0)
    by_part = lambda n: (0, n, 0, 0)
    return pl.pallas_call(
        functools.partial(finish_kernel, cols),
        grid=(scenes,),
        in_specs=[
            pl.BlockSpec((parts, 1) + kv_sent.shape[2:], by_part),
            pl.BlockSpec((parts, 1) + extra_sent.shape[2:], by_part),
            pl.BlockSpec(weights.shape, lambda n: (0, 0, 0)),
            pl.BlockSpec((1, width), lambda n: (0, 0)),
            pl.BlockSpec((1,) + patch_own.shape[1:], scene),
            pl.BlockSpec((1,) + plane_own.shape[1:], scene),
        ],
        out_specs=[pl.BlockSpec((1,) + a.shape[1:], scene) for a in (patch_own, plane_own)],
        out_shape=[jax.ShapeDtypeStruct(a.shape, F32) for a in (patch_own, plane_own)],
        compiler_params=params(),
        cost_estimate=cost(
            scenes * rows * width * parts * 3 * cols * 2, weights.size * 2 + rows * width * 16
        ),
        name="finish",
    )(kv_sent, extra_sent, weights, gain[None], patch_own, plane_own)


def spread(value, axis):
    size, rank = lax.axis_size(axis), lax.axis_index(axis)
    out = jnp.zeros((size,) + value.shape, value.dtype)
    for mask in range(size):
        other = lax.ppermute(value, axis, xor_pairs(size, mask)) if mask else value
        out = lax.dynamic_update_index_in_dim(out, other, rank ^ mask, 0)
    return out


def split_sum(value, axis):
    size, rank = lax.axis_size(axis), lax.axis_index(axis)
    value = value.reshape((size, value.shape[0] // size) + value.shape[1:])
    total = lax.dynamic_index_in_dim(value, rank, 0, keepdims=False)
    for mask in range(1, size):
        block = lax.dynamic_index_in_dim(value, rank ^ mask, 0, keepdims=False).astype(BF)
        total = total + lax.ppermute(block, axis, xor_pairs(size, mask)).astype(F32)
    return total


def render(features, dec_first, dec_bias, dec_second, live_rays):
    preact = jnp.einsum("ch,...cs->...hs", dec_first, features, precision=HIGH) + dec_bias[:, None]
    hidden = jax.nn.silu(preact)
    output = jnp.einsum("hk,...hs->...ks", dec_second, hidden, precision=HIGH)
    samples = output.shape[-1]
    density = jax.nn.softplus(output[..., 0, :])
    colour = jax.nn.sigmoid(output[..., 1:, :])
    optical = density * (2.0 / samples)
    place = jnp.arange(samples)
    before = (place[:, None] < place[None, :]).astype(F32)
    through = jnp.exp(-jnp.einsum("...t,ts->...s", optical, before, precision=HIGH))
    weight = through * (1.0 - jnp.exp(-optical))
    return jnp.sum(weight[..., None, :] * colour, axis=-1) * live_rays[..., None]


def on_device(
    patch_tokens,
    plane_tokens,
    norm1_gain,
    norm1_bias,
    w_query,
    w_key,
    w_value,
    w_out,
    norm2_gain,
    norm2_bias,
    w_up,
    w_down,
    w_unpatch,
    b_unpatch,
    w_dec1,
    b_dec1,
    w_dec2,
    tile_index,
    corner_weights,
    ray_count,
    color_grad,
):
    scenes, patch_local, width = patch_tokens.shape
    plane_local = plane_tokens.shape[1]
    seq_count, tp_count = lax.axis_size("seq"), lax.axis_size("tp")
    seq_rank, tp_rank = lax.axis_index("seq"), lax.axis_index("tp")
    own_patch = patch_local // tp_count
    own_plane = plane_local // tp_count
    cols = w_query.shape[1]
    heads = cols // HEAD_DIM
    ray_seq = tile_index.shape[2]
    rays = ray_seq // tp_count
    picks = 3 * rays
    seq_picks = tp_count * scenes * picks
    all_picks = seq_count * seq_picks
    score_scale = HEAD_DIM**-0.5

    base = (jnp.arange(3, dtype=jnp.int32) * (TRI_SIDE * TRI_SIDE))[None, :, None]
    ids = (tile_index + base).reshape(scenes, 3, tp_count, rays)
    ids = jnp.transpose(ids, (2, 0, 1, 3)).reshape(tp_count, scenes, picks)
    ids = jnp.broadcast_to(ids[None], (seq_count,) + ids.shape)
    ids = lax.all_to_all(ids, "seq", 0, 0, tiled=True)
    plane_normed, plane_kv, query_rows = project(
        plane_tokens.reshape(-1, width), norm1_gain, norm1_bias, w_key, w_value, w_query
    )
    ids, query_rows = lax.optimization_barrier((ids, query_rows))
    local_ids = ids - seq_rank * plane_local
    inside = (local_ids >= 0) & (local_ids < plane_local)
    scene_base = (jnp.arange(scenes, dtype=jnp.int32) * plane_local)[None, None, :, None]
    row_ids = jnp.where(inside, local_ids + scene_base, -1).reshape(all_picks)
    onehot = (
        row_ids[:, None] == jnp.arange(scenes * plane_local, dtype=jnp.int32)[None, :]
    ).astype(BF)

    own_cols = lax.dynamic_slice_in_dim(plane_tokens, tp_rank * cols, cols, 2)
    chosen = jnp.dot(onehot, jnp.concatenate([query_rows, own_cols.reshape(-1, cols)], axis=1))
    chosen, corner_weights, w_key_later, patch_tokens = lax.optimization_barrier(
        (chosen, corner_weights, w_key, patch_tokens)
    )
    chosen = split_sum(chosen, "seq").astype(BF)
    queries = spread(chosen[:, :cols], "seq").reshape(all_picks, cols)
    picked_cols = chosen[:, cols:]

    w_out_all = lax.all_gather(w_out, "tp", axis=0)
    unpatch_all = lax.all_gather(w_unpatch, "tp", axis=0)
    qkv_weight = jnp.concatenate([w_key_later.T, w_value.T, w_query.T], axis=0)
    qkv_all = lax.all_gather(qkv_weight, "tp", axis=0)

    corners = corner_weights.reshape(
        scenes, tp_count, rays, 3, corner_weights.shape[3], corner_weights.shape[4]
    )
    corners = lax.all_to_all(jnp.moveaxis(corners, 1, 0), "tp", 0, 0, tiled=True)

    patch_normed, patch_kv = project(
        patch_tokens.reshape(-1, width), norm1_gain, norm1_bias, w_key, w_value
    )
    queries, corners, patch_kv, picked_cols, w_out_all = lax.optimization_barrier(
        (queries, corners, patch_kv, picked_cols, w_out_all)
    )
    plane_kv = plane_kv.reshape(scenes, plane_local, 2 * cols)
    patch_kv = patch_kv.reshape(scenes, patch_local, 2 * cols)

    def by_scene(value):
        value = value.reshape(seq_count, tp_count, scenes, picks, -1)
        return jnp.moveaxis(value, 2, 0).reshape(scenes, seq_count * tp_count * picks, -1)

    def by_seq(value):
        value = value.reshape(scenes, seq_count, tp_count, picks, -1)
        return jnp.moveaxis(value, 0, 2).reshape(seq_count, seq_picks, -1)

    def in_heads(value):
        return value.reshape(value.shape[:-1] + (heads, HEAD_DIM))

    queries = by_scene(queries)
    part, logsum = attend(queries, patch_kv, plane_kv, heads)
    part = by_seq(part)
    flat = jnp.stack(pieces_of(logsum)).reshape(-1)
    stat_rows = -(-flat.shape[0] // (16 * cols)) * 16
    flat = jnp.pad(flat, (0, stat_rows * cols - flat.shape[0])).reshape(stat_rows, cols)
    flat = jnp.broadcast_to(flat[None], (seq_count, stat_rows, cols))
    part = lax.all_to_all(jnp.concatenate([part, flat], axis=1), "seq", 0, 0, tiled=True)
    logsums = part[:, seq_picks:].reshape(seq_count, -1)[:, : 3 * logsum.size]
    logsums = jnp.sum(logsums.reshape((seq_count, 3) + logsum.shape).astype(F32), axis=1)
    top = jnp.max(logsums, axis=0)
    logsum = top + jnp.log(jnp.sum(jnp.exp(logsums - top), axis=0))
    shares = jnp.exp(logsums - logsum)
    shares = shares.reshape(seq_count, scenes, heads, seq_count, tp_count, picks)
    shares = lax.dynamic_index_in_dim(shares, seq_rank, 3, keepdims=False)
    shares = jnp.transpose(shares, (0, 3, 1, 4, 2)).reshape(seq_count, seq_picks, heads, 1)
    mixed_low = jnp.sum(in_heads(part[:, :seq_picks].astype(F32)) * shares, axis=0)
    mixed_low = mixed_low.reshape(seq_picks, cols).astype(BF)

    bias_rows = jnp.stack(pieces_of(b_unpatch) + [jnp.zeros_like(b_unpatch, BF)] * 13)
    mixed_low = jnp.concatenate([mixed_low, picked_cols], axis=1)
    mixed_low = jnp.concatenate([mixed_low, bias_rows], axis=0)
    mixed_all = lax.all_gather(mixed_low, "tp", axis=0)
    bias_all = jnp.sum(mixed_all[:, seq_picks : seq_picks + 3].astype(F32), axis=1)
    mixed_all, unpatch_all = lax.optimization_barrier((mixed_all[:, :seq_picks], unpatch_all))
    branch = dot("tre,ted->rd", mixed_all[..., :cols], w_out_all)
    picked_rows = jnp.moveaxis(mixed_all[..., cols:], 0, 1).reshape(seq_picks, width)
    picked_rows = picked_rows.astype(F32)
    hidden_state = picked_rows + branch
    normed2 = norm_rows(hidden_state, norm2_gain, norm2_bias).astype(BF)
    preact = jnp.dot(normed2, w_up, preferred_element_type=F32)
    active = jax.nn.gelu(preact).astype(BF)
    down = jnp.dot(active, w_down, preferred_element_type=F32).astype(BF)
    own_rows = scenes * picks

    def to_all(value):
        value = jnp.broadcast_to(value[None], (seq_count,) + value.shape)
        value = value.reshape((seq_count * tp_count,) + value.shape[2:])
        return lax.all_to_all(value, ("seq", "tp"), 0, 0, tiled=True)

    def tp_first(value):
        value = value.reshape((seq_count, tp_count, own_rows) + value.shape[1:])
        return jnp.moveaxis(value, 1, 0).reshape((all_picks,) + value.shape[3:])

    def sum_own(value):
        value = lax.all_to_all(value.reshape(tp_count, own_rows, width), "tp", 0, 0, tiled=True)
        return jnp.sum(value.astype(F32), axis=0)

    hidden_own = lax.dynamic_slice_in_dim(hidden_state, tp_rank * own_rows, own_rows, 0)
    result_own = (hidden_own + sum_own(down)).astype(BF)
    normed2_own = lax.dynamic_slice_in_dim(normed2, tp_rank * own_rows, own_rows, 0)
    tiles = (dot("kd,tdc->ktc", result_own, unpatch_all) + bias_all).astype(BF)
    tile_cols = tiles.shape[2]
    pixels = tile_cols // CH
    picked = tiles.reshape(scenes, 3, rays, tp_count, pixels, CH)
    features = dot("nprtxc,tnrpxs->nrcs", picked, corners)
    first_ray = (seq_rank * tp_count + tp_rank) * rays
    live_rays = (
        (first_ray + jnp.arange(rays, dtype=jnp.int32))[None, :] < ray_count[:, None]
    ).astype(F32)

    def draw_colours(feature_rows, dec_first, dec_bias, dec_second):
        return render(feature_rows, dec_first, dec_bias, dec_second, live_rays)

    colours, pullback = jax.vjp(draw_colours, features, w_dec1, b_dec1, w_dec2)
    grad_features, dec1_part, dec1_bias_part, dec2_part = pullback(jnp.moveaxis(color_grad, 1, -1))
    grad_tiles = jnp.einsum(
        "nrcs,tnrpxs->nprtxc", grad_features, corners.astype(F32), precision=HIGH
    ).astype(BF)
    grad_tiles = grad_tiles.reshape(own_rows, tp_count, tile_cols)
    grad_result = dot("ktc,tdc->kd", grad_tiles, unpatch_all)
    grad_result_low = grad_result.astype(BF)
    result_rows = lax.all_gather(grad_result_low, "tp", axis=0, tiled=True)
    grad_active = dot("rd,fd->rf", result_rows, w_down)
    grad_preact = jax.vjp(jax.nn.gelu, preact)[1](grad_active)[0].astype(BF)
    grad_normed2 = dot("rf,df->rd", grad_preact, w_up).astype(BF)
    grad_normed2, qkv_all = lax.optimization_barrier((grad_normed2, qkv_all))
    grad_normed2 = sum_own(grad_normed2)
    standard2, scale2 = standard_rows(hidden_own)
    gain2_part = jnp.sum(grad_normed2 * standard2, axis=0)
    shift2_part = jnp.sum(grad_normed2, axis=0)
    grad_hidden = grad_result + norm_back(standard2, scale2, norm2_gain, grad_normed2)
    def to_owner(value):
        return lax.all_to_all(value, "tp", 0, 0, tiled=True)

    def by_owner(value, own):
        value = value.reshape(-1, tp_count, own, value.shape[-1])
        return jnp.moveaxis(value, 1, 0)

    normed_picks = norm_rows(picked_rows, norm1_gain, norm1_bias).astype(BF)
    hidden_low = grad_hidden.astype(BF)
    grad_mixed = dot("kd,ted->tke", hidden_low, w_out_all).astype(BF)
    hidden_cols = jnp.moveaxis(hidden_low.reshape(own_rows, tp_count, cols), 1, 0)
    early = jnp.concatenate([normed2_own, result_own, grad_result_low, hidden_low], axis=1)
    early = spread(early, "seq").reshape(-1, 4 * width)
    mixed_own = lax.dynamic_slice_in_dim(mixed_all[..., :cols], tp_rank * own_rows, own_rows, 1)
    sent = to_all(jnp.concatenate([grad_mixed, mixed_own], axis=-1))
    later = jnp.concatenate([hidden_cols, jnp.moveaxis(grad_tiles, 1, 0)], axis=-1)
    sent, later, early_rows = lax.optimization_barrier((sent, later, early))
    later = to_all(later).reshape(all_picks, cols + tile_cols)

    early = lax.all_gather(early_rows, "tp", axis=0, tiled=True)
    scene_sent = by_scene(sent)
    made, totals = [], []
    operands = (queries, patch_kv, plane_kv, scene_sent, logsum)
    operands += (
        patch_normed.reshape(scenes, patch_local, width),
        plane_normed.reshape(scenes, plane_local, width),
    )
    for n in range(scenes):
        if n == scenes - 1:
            operands, later = lax.optimization_barrier((operands, later))
        *one, part, sums = attend_back(n, *operands, totals, heads)
        made.append(one)
        totals = [part, sums]
    kv_sent = to_owner(
        jnp.concatenate(
            [
                jnp.concatenate([by_owner(one[1], own_patch), by_owner(one[2], own_plane)], axis=2)
                for one in made
            ],
            axis=1,
        )
    )
    grad_query = jnp.concatenate([one[0] for one in made], axis=0)
    kv_part, kv_sum = totals
    hidden_cols = later[:, :cols]
    grad_query = split_sum(by_seq(grad_query).reshape(all_picks, cols), "seq").astype(BF)
    grad_query, early, place = lax.optimization_barrier((grad_query, early, tp_rank))
    patch_own = lax.dynamic_slice_in_dim(patch_tokens, place * own_patch, own_patch, 1)
    plane_own = lax.dynamic_slice_in_dim(plane_tokens, place * own_plane, own_plane, 1)
    query_part = dot("rd,re->ed", normed_picks, grad_query)
    grad_query_all = spread(grad_query, "seq").reshape(all_picks, cols)
    scattered = dot("kr,kd->rd", onehot, jnp.concatenate([grad_query_all, hidden_cols], axis=1))
    scattered = scattered.astype(BF)

    query_sum = jnp.sum(grad_query.astype(F32), axis=0)
    sums = jnp.concatenate([kv_sum[0], query_sum])[:, None]
    wide = qkv_weight.astype(F32)
    shift1_part = jnp.sum(wide * sums, axis=0)
    qkv_part = jnp.concatenate([kv_part, query_part], axis=0)
    product = jnp.sum(wide * qkv_part, axis=0)
    gain1_part = (product - norm1_bias * shift1_part) / norm1_gain

    normed2_all, result_all = early[:, :width], early[:, width : 2 * width]
    grad_result_all, grad_hidden_all = early[:, 2 * width : 3 * width], early[:, 3 * width :]
    out_grad = dot(
        "re,rd->ed", tp_first(sent.reshape(all_picks, 2 * cols)[:, cols:]), grad_hidden_all
    )
    tile_cols_all = tp_first(later[:, cols:])
    unpatch_grad = dot("rd,rc->dc", result_all, tile_cols_all)
    unpatch_bias_grad = jnp.sum(tile_cols_all.astype(F32), axis=0)
    preact_all = jnp.dot(normed2_all, w_up, preferred_element_type=F32)
    active_all, gelu_pull = jax.vjp(jax.nn.gelu, preact_all)
    down_grad = dot("rf,rd->fd", active_all.astype(BF), grad_result_all)
    grad_preact_all = gelu_pull(dot("rd,fd->rf", grad_result_all, w_down))[0].astype(BF)
    up_grad = dot("rd,rf->df", normed2_all, grad_preact_all)

    scattered, kv_sent, up_grad, down_grad = lax.optimization_barrier(
        (scattered, kv_sent, up_grad, down_grad)
    )
    extra_sent = to_owner(by_owner(scattered, own_plane))

    def own_sums(pieces):
        pieces = [piece.reshape(tp_count, -1) for piece in pieces]
        ends = [0]
        for piece in pieces:
            ends.append(ends[-1] + piece.shape[1])
        pieces, _ = lax.optimization_barrier((jnp.concatenate(pieces, axis=1), extra_sent))
        total = jnp.sum(to_all(pieces), axis=0)
        return [total[a:b] for a, b in zip(ends, ends[1:])]

    dec1_cols = w_dec1.shape[1] // tp_count
    dec1_part = jnp.moveaxis(dec1_part.reshape(-1, tp_count, dec1_cols), 1, 0)
    (
        gain1_grad,
        shift1_grad,
        gain2_grad,
        shift2_grad,
        dec1_grad,
        dec1_bias_grad,
        dec2_grad,
    ) = own_sums(
        [gain1_part, shift1_part, gain2_part, shift2_part, dec1_part, dec1_bias_part, dec2_part]
    )

    patch_grad, plane_grad = finish(
        kv_sent, extra_sent, qkv_all, patch_own, plane_own, norm1_gain, cols
    )
    qkv_grad = lax.psum(qkv_part.astype(BF), "seq").astype(F32)
    return (
        jnp.moveaxis(colours, -1, 1),
        patch_grad,
        plane_grad,
        gain1_grad,
        shift1_grad,
        qkv_grad[2 * cols :].T,
        qkv_grad[:cols].T,
        qkv_grad[cols : 2 * cols].T,
        out_grad,
        gain2_grad,
        shift2_grad,
        up_grad,
        down_grad,
        unpatch_grad,
        unpatch_bias_grad,
        dec1_grad.reshape(-1, dec1_cols),
        dec1_bias_grad,
        dec2_grad.reshape(-1, w_dec2.shape[1]),
    )


def solution(mesh):
    in_specs = (
        P(None, "seq", None),
        P(None, "seq", None),
        P(),
        P(),
        P(None, "tp"),
        P(None, "tp"),
        P(None, "tp"),
        P("tp", None),
        P(),
        P(),
        P(None, "tp"),
        P("tp", None),
        P(None, "tp"),
        P("tp"),
        P(),
        P(),
        P(),
        P(None, None, "seq"),
        P(None, "seq", None, "tp", None),
        P(),
        P(None, None, ("seq", "tp")),
    )
    out_specs = (
        P(None, None, ("seq", "tp")),
        P(None, ("seq", "tp"), None),
        P(None, ("seq", "tp"), None),
        P("tp"),
        P("tp"),
        P(None, "tp"),
        P(None, "tp"),
        P(None, "tp"),
        P("tp", None),
        P("tp"),
        P("tp"),
        P(None, "tp"),
        P("tp", None),
        P(None, "tp"),
        P("tp"),
        P(None, "tp"),
        P("tp"),
        P("tp", None),
    )
    return jax.shard_map(
        on_device, mesh=mesh, in_specs=in_specs, out_specs=out_specs, check_vma=False
    )
```

```python
import functools

import jax
import jax.numpy as jnp
from jax import lax
from jax.experimental import pallas as pl
from jax.experimental.pallas import tpu as pltpu
from jax.sharding import PartitionSpec as P

HEAD_DIM = 64
CH = 32
TRI_SIDE = 32
BF = jnp.bfloat16
F32 = jnp.float32
HIGH = lax.Precision.HIGHEST


def dot(spec, *operands):
    return jnp.einsum(spec, *operands, preferred_element_type=F32)


def standard_rows(token_rows):
    centre = jnp.mean(token_rows, axis=-1, keepdims=True)
    offset = token_rows - centre
    spread = jnp.mean(offset * offset, axis=-1, keepdims=True)
    scale = lax.rsqrt(spread + 1e-05)
    return offset * scale, scale


def norm_rows(token_rows, norm_gain, norm_shift):
    return standard_rows(token_rows)[0] * norm_gain + norm_shift


def norm_back(standard, scale, norm_gain, grad):
    scaled = grad * norm_gain
    first = jnp.mean(scaled, axis=-1, keepdims=True)
    second = jnp.mean(scaled * standard, axis=-1, keepdims=True)
    return scale * (scaled - first - standard * second)


def xor_pairs(size, mask):
    return [(i, i ^ mask) for i in range(size)]


def hyper_sum(value, axes):
    for axis in axes:
        size = lax.axis_size(axis)
        mask = 1
        while mask < size:
            value = value + lax.ppermute(value, axis, xor_pairs(size, mask))
            mask *= 2
    return value


def block_rows(rows, limit):
    best = rows
    for size in range(16, limit + 1, 16):
        if rows % size == 0:
            best = size
    return best


def params():
    return pltpu.CompilerParams(vmem_limit_bytes=60 * 2**20)


def cost(flops, bytes_accessed, transcendentals=0):
    return pl.CostEstimate(
        flops=flops, bytes_accessed=bytes_accessed, transcendentals=transcendentals
    )


def project_kernel(weight_count, rows_ref, gain_ref, bias_ref, *refs):
    weights, (normed_ref, kv_ref, *query_refs) = refs[:weight_count], refs[weight_count:]
    rows = rows_ref[...].astype(F32)
    normed = norm_rows(rows, gain_ref[...], bias_ref[...]).astype(BF)
    normed_ref[...] = normed
    made = [jnp.dot(normed, w[...], preferred_element_type=F32).astype(BF) for w in weights]
    kv_ref[...] = jnp.concatenate(made[:2], axis=1)
    for ref, value in zip(query_refs, made[2:]):
        ref[...] = value


def project(token_rows, gain, bias, *weights):
    rows, width = token_rows.shape
    cols = weights[0].shape[1]
    block = block_rows(rows, 512)
    widths = [width, 2 * cols] + [cols] * (len(weights) - 2)
    whole = lambda i: (0, 0)
    mine = lambda i: (i, 0)
    return pl.pallas_call(
        functools.partial(project_kernel, len(weights)),
        grid=(rows // block,),
        in_specs=[
            pl.BlockSpec((block, width), mine),
            pl.BlockSpec((1, width), whole),
            pl.BlockSpec((1, width), whole),
        ]
        + [pl.BlockSpec((width, cols), whole) for _ in weights],
        out_specs=[pl.BlockSpec((block, w), mine) for w in widths],
        out_shape=[jax.ShapeDtypeStruct((rows, w), BF) for w in widths],
        compiler_params=params(),
        cost_estimate=cost(
            2 * rows * width * cols * len(weights), rows * (width + sum(widths)) * 2
        ),
        name="norm_project",
    )(token_rows, gain[None], bias[None], *weights)


def pieces_of(value):
    high = lax.reduce_precision(value, 8, 7)
    middle = lax.reduce_precision(value - high, 8, 7)
    return [high.astype(BF), middle.astype(BF), (value - high - middle).astype(BF)]


def dot_dims(left, right, left_dim, right_dim):
    dims = (((left_dim,), (right_dim,)), ((), ()))
    return lax.dot_general(left, right, dims, preferred_element_type=F32)


def attend_kernel(heads, q_ref, first_ref, second_ref, out_ref, logsum_ref):
    cols = heads * HEAD_DIM
    parts, stats = [], []
    for h in range(heads):
        here = slice(h * HEAD_DIM, (h + 1) * HEAD_DIM)
        there = slice(cols + h * HEAD_DIM, cols + (h + 1) * HEAD_DIM)
        query = q_ref[0, :, here] * BF(HEAD_DIM**-0.5)
        scores = [dot_dims(ref[0, :, here], query, 1, 1) for ref in (first_ref, second_ref)]
        top = jnp.maximum(*[jnp.max(s, axis=0, keepdims=True) for s in scores])
        raised = [jnp.exp(s - top) for s in scores]
        total = sum(jnp.sum(r, axis=0, keepdims=True) for r in raised)
        mixed = sum(
            dot_dims(ref[0, :, there], r.astype(BF), 0, 0)
            for ref, r in zip((first_ref, second_ref), raised)
        )
        parts.append(mixed / total)
        stats.append(top + jnp.log(total))
    out_ref[0] = jnp.concatenate(parts, axis=0).T.astype(BF)
    logsum_ref[0] = jnp.concatenate(stats, axis=0)


def attend(queries, first, second, heads):
    scenes, count, cols = queries.shape
    keys = first.shape[1] + second.shape[1]
    scene = lambda n: (n, 0, 0)
    return pl.pallas_call(
        functools.partial(attend_kernel, heads),
        grid=(scenes,),
        in_specs=[pl.BlockSpec((1,) + a.shape[1:], scene) for a in (queries, first, second)],
        out_specs=[
            pl.BlockSpec((1, count, cols), scene),
            pl.BlockSpec((1, heads, count), scene),
        ],
        out_shape=[
            jax.ShapeDtypeStruct((scenes, count, cols), BF),
            jax.ShapeDtypeStruct((scenes, heads, count), F32),
        ],
        compiler_params=params(),
        cost_estimate=cost(
            scenes * heads * count * keys * 16 * HEAD_DIM * 2,
            scenes * keys * cols * 4,
            scenes * heads * count * keys,
        ),
        name="attend",
    )(queries, first, second)


def attend_back_kernel(heads, *refs):
    q_ref, first_ref, second_ref, grad_ref, logsum_ref, na_ref, nb_ref = refs[:7]
    gq_ref, ga_ref, gb_ref, part_ref, sum_ref = refs[-5:]
    if len(refs) > 12:
        part_ref[...] = refs[7][...]
        sum_ref[...] = refs[8][...]
    else:
        part_ref[...] = jnp.zeros_like(part_ref)
        sum_ref[...] = jnp.zeros_like(sum_ref)
    cols = heads * HEAD_DIM
    count = q_ref.shape[1]
    scale = HEAD_DIM**-0.5
    cut = [slice(h * HEAD_DIM, (h + 1) * HEAD_DIM) for h in range(heads)]
    query = [q_ref[0, :, c] * BF(scale) for c in cut]
    grad = [grad_ref[0, :, c] for c in cut]
    ones = jnp.ones((8, HEAD_DIM), F32)
    inner = [
        lax.dot_general(
            ones,
            grad_ref[0, :, cols + c.start : cols + c.stop].astype(F32) * g.astype(F32),
            (((1,), (1,)), ((), ())),
            precision=HIGH,
            preferred_element_type=F32,
        )[:1]
        for c, g in zip(cut, grad)
    ]
    totals = tuple(jnp.zeros((HEAD_DIM, count), F32) for _ in cut)
    for ref, out_ref, normed_ref in ((first_ref, ga_ref, na_ref), (second_ref, gb_ref, nb_ref)):
        rows = ref.shape[1]
        block = block_rows(rows, 512)

        def step(i, totals, ref=ref, out_ref=out_ref, normed_ref=normed_ref, block=block):
            place = pl.ds(pl.multiple_of(i * block, block), block)
            keys, grads, sums = [], [], []
            for h in range(heads):
                key = ref[0, place, cut[h]]
                value = ref[0, place, slice(cols + cut[h].start, cols + cut[h].stop)]
                shares = jnp.exp(dot_dims(key, query[h], 1, 1) - logsum_ref[0, h : h + 1, :])
                grad_shares = dot_dims(value, grad[h], 1, 1)
                grad_scores = (shares * (grad_shares - inner[h])).astype(BF)
                keys.append(jnp.dot(grad_scores, query[h], preferred_element_type=F32))
                grads.append(jnp.dot(shares.astype(BF), grad[h], preferred_element_type=F32))
                sums.append(totals[h] + dot_dims(key, grad_scores, 0, 0))
            made = jnp.concatenate(keys + grads, axis=1).astype(BF)
            out_ref[0, place, :] = made
            part_ref[...] += dot_dims(made, normed_ref[0, place, :], 0, 0)
            sum_ref[...] += jnp.sum(made.astype(F32), axis=0, keepdims=True)
            return tuple(sums)

        totals = lax.fori_loop(0, rows // block, step, totals, unroll=True)
    gq_ref[0] = (jnp.concatenate(totals, axis=0) * scale).T.astype(BF)


def attend_back(scene, queries, first, second, grad, logsum, normed_first, normed_second, before, heads):
    scenes, count, cols = queries.shape
    keys, width = first.shape[1] + second.shape[1], normed_first.shape[2]
    mine = lambda i: (scene, 0, 0)
    whole = lambda i: (0, 0)
    operands = (queries, first, second, grad, logsum, normed_first, normed_second)
    totals = [(2 * cols, width), (1, 2 * cols)]
    outs = [(1,) + a.shape[1:] for a in (queries, first, second)]
    return pl.pallas_call(
        functools.partial(attend_back_kernel, heads),
        grid=(1,),
        in_specs=[pl.BlockSpec((1,) + a.shape[1:], mine) for a in operands]
        + [pl.BlockSpec(a.shape, whole) for a in before],
        out_specs=[pl.BlockSpec(a, lambda i: (0, 0, 0)) for a in outs]
        + [pl.BlockSpec(a, whole) for a in totals],
        out_shape=[jax.ShapeDtypeStruct(a, BF) for a in outs]
        + [jax.ShapeDtypeStruct(a, F32) for a in totals],
        compiler_params=params(),
        cost_estimate=cost(
            heads * count * keys * 40 * HEAD_DIM * 2 + 4 * keys * cols * width,
            keys * (cols * 8 + width * 2),
            heads * count * keys,
        ),
        name="attend_back",
    )(*operands, *before)


def finish_kernel(cols, rank_ref, kv_ref, extra_ref, weight_ref, gain_ref, patch_ref, plane_ref, *outs):
    own_patch = patch_ref.shape[2]
    parts = kv_ref.shape[0]
    total = sum(dot_dims(kv_ref[t, 0], weight_ref[t, : 2 * cols], 1, 0) for t in range(parts))
    more = sum(
        dot_dims(extra_ref[t, 0, :, :cols], weight_ref[t, 2 * cols :], 1, 0)
        for t in range(parts)
    )
    grads = (total[:own_patch], total[own_patch:] + more)
    extra = jnp.concatenate([extra_ref[t, 0, :, cols:] for t in range(parts)], axis=1)
    added = (0.0, extra.astype(F32))
    for ref, out_ref, grad, plus in zip((patch_ref, plane_ref), outs, grads, added):
        standard, scale = standard_rows(ref[0, 0].astype(F32))
        out_ref[0] = norm_back(standard, scale, gain_ref[...], grad) + plus


def finish(kv_sent, extra_sent, weights, patch_rows, plane_rows, gain, rank, cols):
    parts, scenes, rows, _ = kv_sent.shape
    width = weights.shape[2]
    tokens = [a.reshape(scenes, parts, -1, width) for a in (patch_rows, plane_rows)]
    by_part = lambda n, rank: (0, n, 0, 0)
    spec = pltpu.PrefetchScalarGridSpec(
        num_scalar_prefetch=1,
        grid=(scenes,),
        in_specs=[
            pl.BlockSpec((parts, 1) + kv_sent.shape[2:], by_part),
            pl.BlockSpec((parts, 1) + extra_sent.shape[2:], by_part),
            pl.BlockSpec(weights.shape, lambda n, rank: (0, 0, 0)),
            pl.BlockSpec((1, width), lambda n, rank: (0, 0)),
        ]
        + [pl.BlockSpec((1, 1) + a.shape[2:], lambda n, rank: (n, rank[0], 0, 0)) for a in tokens],
        out_specs=[pl.BlockSpec((1,) + a.shape[2:], lambda n, rank: (n, 0, 0)) for a in tokens],
    )
    return pl.pallas_call(
        functools.partial(finish_kernel, cols),
        grid_spec=spec,
        out_shape=[jax.ShapeDtypeStruct((scenes,) + a.shape[2:], F32) for a in tokens],
        compiler_params=params(),
        cost_estimate=cost(
            scenes * rows * width * parts * 3 * cols * 2, weights.size * 2 + rows * width * 16
        ),
        name="finish",
    )(rank.reshape(1), kv_sent, extra_sent, weights, gain[None], *tokens)


def turn_kernel(rank_ref, *refs):
    parts, outs = refs[:-3], refs[-3:]
    cols, size = outs[0].shape[1], parts[0].shape[1]
    for mask, part in enumerate(parts):
        place = pl.ds(pl.multiple_of((rank_ref[0] ^ mask) * size, size), size)
        for k, ref in enumerate(outs):
            ref[place, :] = part[k * cols : (k + 1) * cols].astype(F32).T


def turn(rank, parts):
    rows, width = parts[0].shape[0], parts[0].shape[1] * len(parts)
    whole = lambda i, r: (0, 0)
    spec = pltpu.PrefetchScalarGridSpec(
        num_scalar_prefetch=1,
        grid=(1,),
        in_specs=[pl.BlockSpec(a.shape, whole) for a in parts],
        out_specs=[pl.BlockSpec((width, rows // 3), whole)] * 3,
    )
    return pl.pallas_call(
        turn_kernel,
        grid_spec=spec,
        out_shape=[jax.ShapeDtypeStruct((width, rows // 3), F32)] * 3,
        compiler_params=params(),
        cost_estimate=cost(1, 1),
        name="turn",
    )(rank.reshape(1), *parts)


def gelu_parts(value):
    slope = 0.7978845608028654
    square = value * value
    bent = jnp.tanh(slope * value * (1.0 + 0.044715 * square))
    half = 0.5 * (1.0 + bent)
    rise = 0.5 * value * (1.0 - bent * bent) * (slope * (1.0 + 0.134145 * square))
    return value * half, half + rise


def weights_kernel(width, rows_ref, up_ref, down_ref, mixed_ref, tile_ref, *outs):
    up_out, down_out, mix_out, tile_out, sum_out = outs
    unit_step, pick_step = pl.program_id(0), pl.program_id(1)
    normed, result, grad_result, grad_hidden = [
        rows_ref[:, k * width : (k + 1) * width] for k in range(4)
    ]

    @pl.when(pick_step == 0)
    def _():
        up_out[...] = jnp.zeros_like(up_out)
        down_out[...] = jnp.zeros_like(down_out)

    @pl.when((pick_step == 0) & (unit_step == 0))
    def _():
        mix_out[...] = jnp.zeros_like(mix_out)
        tile_out[...] = jnp.zeros_like(tile_out)
        sum_out[...] = jnp.zeros_like(sum_out)

    preact = jnp.dot(normed, up_ref[...], preferred_element_type=F32)
    active, slope = gelu_parts(preact)
    down_out[...] += dot_dims(active.astype(BF), grad_result, 0, 0)
    grad = (dot_dims(grad_result, down_ref[...], 1, 1) * slope).astype(BF)
    up_out[...] += dot_dims(normed, grad, 0, 0)

    @pl.when(unit_step == 0)
    def _():
        mix_out[...] += dot_dims(mixed_ref[...], grad_hidden, 0, 0)
        tile_out[...] += dot_dims(result, tile_ref[...], 0, 0)
        sum_out[...] += jnp.sum(tile_ref[...].astype(F32), axis=0, keepdims=True)


def weight_grads(rows, w_up, w_down, mixed, tiles):
    picks, width = rows.shape[0], rows.shape[1] // 4
    units, cols, tile_cols = w_up.shape[1], mixed.shape[1], tiles.shape[1]
    block, units_block = block_rows(picks, 768), block_rows(units, 512)
    here = lambda g, p: (p, 0)
    whole = lambda g, p: (0, 0)
    return pl.pallas_call(
        functools.partial(weights_kernel, width),
        grid=(units // units_block, picks // block),
        in_specs=[
            pl.BlockSpec((block, 4 * width), here),
            pl.BlockSpec((width, units_block), lambda g, p: (0, g)),
            pl.BlockSpec((units_block, width), lambda g, p: (g, 0)),
            pl.BlockSpec((block, cols), here),
            pl.BlockSpec((block, tile_cols), here),
        ],
        out_specs=[
            pl.BlockSpec((width, units_block), lambda g, p: (0, g)),
            pl.BlockSpec((units_block, width), lambda g, p: (g, 0)),
            pl.BlockSpec((cols, width), whole),
            pl.BlockSpec((width, tile_cols), whole),
            pl.BlockSpec((1, tile_cols), whole),
        ],
        out_shape=[
            jax.ShapeDtypeStruct(shape, F32)
            for shape in (
                (width, units),
                (units, width),
                (cols, width),
                (width, tile_cols),
                (1, tile_cols),
            )
        ],
        compiler_params=params(),
        cost_estimate=cost(
            2 * picks * width * (4 * units + cols + tile_cols),
            rows.size * 2 + width * units * 12,
            picks * units,
        ),
        name="weight_grads",
    )(rows, w_up, w_down, mixed, tiles)


def scatter_kernel(scenes, own, rank_ref, ids_ref, hidden_ref, *refs):
    parts, out_ref = refs[:-1], refs[-1]
    rank = rank_ref[0]
    seq_picks = parts[0].shape[0]
    values = [
        jnp.concatenate([part[...], hidden_ref[rank ^ m]], axis=1) for m, part in enumerate(parts)
    ]
    row = lax.broadcasted_iota(jnp.int32, (own, seq_picks), 0)
    blocks = out_ref.shape[0]

    def step(t, carry):
        for n in range(scenes):
            first = (n * blocks + t) * own
            total = sum(
                jnp.dot(
                    (row + first == ids_ref[rank ^ m]).astype(F32).astype(BF),
                    value,
                    preferred_element_type=F32,
                )
                for m, value in enumerate(values)
            )
            out_ref[t, n] = total.astype(BF)
        return carry

    lax.fori_loop(0, blocks, step, 0)


def scatter(rank, ids, hidden, parts, shape):
    spec = pltpu.PrefetchScalarGridSpec(
        num_scalar_prefetch=1,
        grid=(1,),
        in_specs=[
            pl.BlockSpec(a.shape, lambda i, r, k=a.ndim: (0,) * k) for a in (ids, hidden, *parts)
        ],
        out_specs=pl.BlockSpec(shape, lambda i, r: (0, 0, 0, 0)),
    )
    return pl.pallas_call(
        functools.partial(scatter_kernel, shape[1], shape[2]),
        grid_spec=spec,
        out_shape=jax.ShapeDtypeStruct(shape, BF),
        compiler_params=params(),
        cost_estimate=cost(2 * shape[0] * shape[1] * shape[2] * shape[3] * ids.size, hidden.size * 8),
        name="scatter",
    )(rank.reshape(1), ids, hidden, *parts)


def spread(value, axis):
    size, rank = lax.axis_size(axis), lax.axis_index(axis)
    out = jnp.zeros((size,) + value.shape, value.dtype)
    for mask in range(size):
        other = lax.ppermute(value, axis, xor_pairs(size, mask)) if mask else value
        out = lax.dynamic_update_index_in_dim(out, other, rank ^ mask, 0)
    return out


def split_sum(value, axis):
    size, rank = lax.axis_size(axis), lax.axis_index(axis)
    value = value.reshape((size, value.shape[0] // size) + value.shape[1:])
    total = lax.dynamic_index_in_dim(value, rank, 0, keepdims=False)
    for mask in range(1, size):
        block = lax.dynamic_index_in_dim(value, rank ^ mask, 0, keepdims=False).astype(BF)
        total = total + lax.ppermute(block, axis, xor_pairs(size, mask)).astype(F32)
    return total


def dot_high(left, right, left_dim, right_dim):
    dims = (((left_dim,), (right_dim,)), ((), ()))
    return lax.dot_general(left, right, dims, precision=HIGH, preferred_element_type=F32)


def render_kernel(*refs):
    came_ref, hidden_ref, unpatch_ref, shift_ref, corner_ref, select_ref = refs[:6]
    w1_ref, b1_ref, w2_ref, live_ref, cotangent_ref = refs[6:11]
    (result_ref, colour_ref, tiles_ref, grad_ref, low_ref, g1_ref, gb_ref, g2_ref) = refs[11:]
    parts, rows, _ = came_ref.shape
    rays, _, samples = corner_ref.shape
    result = hidden_ref[...] + sum(came_ref[t].astype(F32) for t in range(parts))
    result = result.astype(BF)
    result_ref[...] = result
    tiles = [
        (jnp.dot(result, unpatch_ref[t], preferred_element_type=F32) + shift_ref[t]).astype(BF)
        for t in range(parts)
    ]
    tiles = jnp.concatenate(tiles, axis=0)
    lines, tile_cols = corner_ref.shape[1], tiles.shape[1]

    def place(shape, dim):
        return lax.broadcasted_iota(jnp.int32, shape, dim)

    pixel_mask = tile_cols // CH - 1
    pixel = place((lines, tile_cols), 1) >> (CH.bit_length() - 1)
    pixel = (pixel == (place((lines, tile_cols), 0) & pixel_mask)).astype(F32)
    pick_out = (place((CH, tile_cols), 1) & (CH - 1)) == place((CH, tile_cols), 0)
    pick_out = pick_out.astype(F32).astype(BF)
    units = b1_ref.shape[1]
    bias = jnp.where(place((units, units), 0) == place((units, units), 1), b1_ref[...], 0.0)
    bias = jnp.sum(bias, axis=1, keepdims=True)
    features = []
    for r in range(rays):
        mine = jnp.dot(select_ref[r], tiles, preferred_element_type=F32) * pixel
        mine = dot_dims(mine.astype(BF), pick_out, 1, 1).astype(BF)
        features.append(dot_dims(mine, corner_ref[r], 0, 0))
    features = jnp.concatenate(features, axis=1)
    preact = dot_high(w1_ref[...], features, 0, 0) + bias
    gate = 1.0 / (1.0 + jnp.exp(-preact))
    hidden = preact * gate
    output = dot_high(w2_ref[...], hidden, 0, 0)

    def by_ray(row):
        return jnp.concatenate(
            [row[:, r * samples : (r + 1) * samples] for r in range(rays)], axis=0
        )

    def in_row(value):
        return jnp.concatenate([value[r : r + 1] for r in range(rays)], axis=1)

    first = by_ray(output[0:1])
    density = jnp.maximum(first, 0.0) + jnp.log1p(jnp.exp(-jnp.abs(first)))
    shades = [1.0 / (1.0 + jnp.exp(-by_ray(output[k : k + 1]))) for k in (1, 2, 3)]
    optical = density * (2.0 / samples)
    before = (
        lax.broadcasted_iota(jnp.int32, (samples, samples), 0)
        < lax.broadcasted_iota(jnp.int32, (samples, samples), 1)
    ).astype(F32)
    through = jnp.exp(-dot_high(optical, before, 1, 0))
    kept = jnp.exp(-optical)
    weight = through * (1.0 - kept)
    live = live_ref[...]
    colour_ref[...] = jnp.concatenate(
        [jnp.sum(weight * shade, axis=1, keepdims=True) * live for shade in shades], axis=1
    )
    grads = [cotangent_ref[:, k : k + 1] * live for k in range(3)]
    grad_weight = sum(g * shade for g, shade in zip(grads, shades))
    grad_before = -through * grad_weight * (1.0 - kept)
    grad_optical = dot_high(grad_before, before, 1, 1) + grad_weight * through * kept
    grad_first = grad_optical * (2.0 / samples) * (1.0 / (1.0 + jnp.exp(-first)))
    grad_shades = [g * weight * shade * (1.0 - shade) for g, shade in zip(grads, shades)]
    grad_output = jnp.concatenate([in_row(g) for g in [grad_first] + grad_shades], axis=0)
    grad_preact = jnp.dot(w2_ref[...], grad_output, precision=HIGH, preferred_element_type=F32)
    grad_preact = grad_preact * (gate * (1.0 + preact * (1.0 - gate)))
    g2_ref[...] = dot_high(hidden, grad_output, 1, 1)
    gb_ref[...] = jnp.sum(grad_preact, axis=1, keepdims=True)
    g1_ref[...] = dot_high(features, grad_preact, 1, 1)
    grad_features = jnp.dot(w1_ref[...], grad_preact, precision=HIGH, preferred_element_type=F32)
    total = jnp.zeros(tiles.shape, F32)
    for r in range(rays):
        mine = grad_features[:, r * samples : (r + 1) * samples]
        mine = dot_high(corner_ref[r].astype(F32), mine, 1, 1).astype(BF)
        mine = jnp.dot(mine, pick_out, preferred_element_type=F32) * pixel
        total = total + dot_dims(select_ref[r], mine.astype(BF), 0, 0)
    grad = jnp.zeros(grad_ref.shape, F32)
    for t in range(parts):
        mine = total[t * rows : (t + 1) * rows].astype(BF)
        tiles_ref[t] = mine
        grad = grad + dot_dims(mine, unpatch_ref[t], 1, 1)
    grad_ref[...] = grad
    low_ref[...] = grad.astype(BF)


def render(came, hidden_own, unpatch, shift, corners, w1, b1, w2, live, cotangent):
    parts, rows, width = came.shape
    scenes, rays, tile_cols = corners.shape[1], corners.shape[2], unpatch.shape[2]
    pixels, samples = corners.shape[4], corners.shape[5]
    corners = jnp.transpose(corners, (1, 2, 0, 3, 4, 5))
    corners = corners.reshape(scenes * rays, parts * 3 * pixels, samples)
    ray = jnp.arange(scenes * rays)[:, None, None]
    line = jnp.arange(parts * 3 * pixels)[None, :, None]
    source = (line // (3 * pixels)) * rows + (line // pixels) % 3 * rays
    source = source + (ray // rays) * (3 * rays) + ray % rays
    select = (source == jnp.arange(parts * rows)[None, None, :]).astype(BF)
    hidden_units = w1.shape[1]
    operands = (came, hidden_own, unpatch, shift[:, None], corners, select)
    operands += (w1, b1[None], w2, live, cotangent)
    outs = [
        ((rows, width), BF),
        (cotangent.shape, F32),
        ((parts, rows, tile_cols), BF),
        ((rows, width), F32),
        ((rows, width), BF),
        (w1.shape, F32),
        ((hidden_units, 1), F32),
        (w2.shape, F32),
    ]
    return pl.pallas_call(
        render_kernel,
        out_shape=[jax.ShapeDtypeStruct(shape, kind) for shape, kind in outs],
        compiler_params=params(),
        cost_estimate=cost(8 * rows * width * tile_cols * parts, unpatch.size * 2, 0),
        name="render",
    )(*operands)


def on_device(
    patch_tokens,
    plane_tokens,
    norm1_gain,
    norm1_bias,
    w_query,
    w_key,
    w_value,
    w_out,
    norm2_gain,
    norm2_bias,
    w_up,
    w_down,
    w_unpatch,
    b_unpatch,
    w_dec1,
    b_dec1,
    w_dec2,
    tile_index,
    corner_weights,
    ray_count,
    color_grad,
):
    scenes, patch_local, width = patch_tokens.shape
    plane_local = plane_tokens.shape[1]
    seq_count, tp_count = lax.axis_size("seq"), lax.axis_size("tp")
    seq_rank, tp_rank = lax.axis_index("seq"), lax.axis_index("tp")
    own_patch = patch_local // tp_count
    own_plane = plane_local // tp_count
    cols = w_query.shape[1]
    heads = cols // HEAD_DIM
    ray_seq = tile_index.shape[2]
    rays = ray_seq // tp_count
    picks = 3 * rays
    seq_picks = tp_count * scenes * picks
    all_picks = seq_count * seq_picks
    score_scale = HEAD_DIM**-0.5

    base = (jnp.arange(3, dtype=jnp.int32) * (TRI_SIDE * TRI_SIDE))[None, :, None]
    ids = (tile_index + base).reshape(scenes, 3, tp_count, rays)
    ids = jnp.transpose(ids, (2, 0, 1, 3)).reshape(tp_count, scenes, picks)
    ids = jnp.broadcast_to(ids[None], (seq_count,) + ids.shape)
    ids = lax.all_to_all(ids, "seq", 0, 0, tiled=True)
    plane_normed, plane_kv, query_rows = project(
        plane_tokens.reshape(-1, width), norm1_gain, norm1_bias, w_key, w_value, w_query
    )
    ids, query_rows = lax.optimization_barrier((ids, query_rows))
    local_ids = ids - seq_rank * plane_local
    inside = (local_ids >= 0) & (local_ids < plane_local)
    scene_base = (jnp.arange(scenes, dtype=jnp.int32) * plane_local)[None, None, :, None]
    row_ids = jnp.where(inside, local_ids + scene_base, -1).reshape(all_picks)
    onehot = (
        row_ids[:, None] == jnp.arange(scenes * plane_local, dtype=jnp.int32)[None, :]
    ).astype(BF)

    own_cols = lax.dynamic_slice_in_dim(plane_tokens, tp_rank * cols, cols, 2)
    chosen = jnp.dot(onehot, jnp.concatenate([query_rows, own_cols.reshape(-1, cols)], axis=1))
    chosen, corner_weights, w_key_later, patch_tokens = lax.optimization_barrier(
        (chosen, corner_weights, w_key, patch_tokens)
    )
    chosen = split_sum(chosen, "seq").astype(BF)
    chosen, patch_tokens = lax.optimization_barrier((chosen, patch_tokens))
    queries = spread(chosen[:, :cols], "seq").reshape(all_picks, cols)
    picked_cols = chosen[:, cols:]

    w_out_all = lax.all_gather(w_out, "tp", axis=0)
    unpatch_all = lax.all_gather(w_unpatch, "tp", axis=0)
    qkv_weight = jnp.concatenate([w_key_later.T, w_value.T, w_query.T], axis=0)
    qkv_all = lax.all_gather(qkv_weight, "tp", axis=0)

    corners = corner_weights.reshape(
        scenes, tp_count, rays, 3, corner_weights.shape[3], corner_weights.shape[4]
    )
    corners = lax.all_to_all(jnp.moveaxis(corners, 1, 0), "tp", 0, 0, tiled=True)

    patch_normed, patch_kv = project(
        patch_tokens.reshape(-1, width), norm1_gain, norm1_bias, w_key, w_value
    )
    queries, corners, patch_kv, picked_cols, w_out_all = lax.optimization_barrier(
        (queries, corners, patch_kv, picked_cols, w_out_all)
    )
    plane_kv = plane_kv.reshape(scenes, plane_local, 2 * cols)
    patch_kv = patch_kv.reshape(scenes, patch_local, 2 * cols)

    def by_scene(value):
        value = value.reshape(seq_count, tp_count, scenes, picks, -1)
        return jnp.moveaxis(value, 2, 0).reshape(scenes, seq_count * tp_count * picks, -1)

    def by_seq(value):
        value = value.reshape(scenes, seq_count, tp_count, picks, -1)
        return jnp.moveaxis(value, 0, 2).reshape(seq_count, seq_picks, -1)

    def in_heads(value):
        return value.reshape(value.shape[:-1] + (heads, HEAD_DIM))

    queries = by_scene(queries)
    part, logsum = attend(queries, patch_kv, plane_kv, heads)
    part = by_seq(part)
    flat = jnp.stack(pieces_of(logsum)).reshape(-1)
    stat_rows = -(-flat.shape[0] // (16 * cols)) * 16
    flat = jnp.pad(flat, (0, stat_rows * cols - flat.shape[0])).reshape(stat_rows, cols)
    flat = jnp.broadcast_to(flat[None], (seq_count, stat_rows, cols))
    part = lax.all_to_all(jnp.concatenate([part, flat], axis=1), "seq", 0, 0, tiled=True)
    logsums = part[:, seq_picks:].reshape(seq_count, -1)[:, : 3 * logsum.size]
    logsums = jnp.sum(logsums.reshape((seq_count, 3) + logsum.shape).astype(F32), axis=1)
    top = jnp.max(logsums, axis=0)
    logsum = top + jnp.log(jnp.sum(jnp.exp(logsums - top), axis=0))
    shares = jnp.exp(logsums - logsum)
    shares = shares.reshape(seq_count, scenes, heads, seq_count, tp_count, picks)
    shares = lax.dynamic_index_in_dim(shares, seq_rank, 3, keepdims=False)
    shares = jnp.transpose(shares, (0, 3, 1, 4, 2)).reshape(seq_count, seq_picks, heads, 1)
    mixed_low = jnp.sum(in_heads(part[:, :seq_picks].astype(F32)) * shares, axis=0)
    mixed_low = mixed_low.reshape(seq_picks, cols).astype(BF)

    bias_rows = jnp.stack(pieces_of(b_unpatch) + [jnp.zeros_like(b_unpatch, BF)] * 13)
    mixed_low = jnp.concatenate([mixed_low, picked_cols], axis=1)
    mixed_low = jnp.concatenate([mixed_low, bias_rows], axis=0)
    mixed_all = lax.all_gather(mixed_low, "tp", axis=0)
    bias_all = jnp.sum(mixed_all[:, seq_picks : seq_picks + 3].astype(F32), axis=1)
    mixed_all, unpatch_all = lax.optimization_barrier((mixed_all[:, :seq_picks], unpatch_all))
    branch = dot("tre,ted->rd", mixed_all[..., :cols], w_out_all)
    picked_rows = jnp.moveaxis(mixed_all[..., cols:], 0, 1).reshape(seq_picks, width)
    picked_rows = picked_rows.astype(F32)
    hidden_state = picked_rows + branch
    normed2 = norm_rows(hidden_state, norm2_gain, norm2_bias).astype(BF)
    preact = jnp.dot(normed2, w_up, preferred_element_type=F32)
    active = jax.nn.gelu(preact).astype(BF)
    down = jnp.dot(active, w_down, preferred_element_type=F32).astype(BF)
    own_rows = scenes * picks

    def to_all(value):
        value = jnp.broadcast_to(value[None], (seq_count,) + value.shape)
        value = value.reshape((seq_count * tp_count,) + value.shape[2:])
        return lax.all_to_all(value, ("seq", "tp"), 0, 0, tiled=True)

    def tp_first(value):
        value = value.reshape((seq_count, tp_count, own_rows) + value.shape[1:])
        return jnp.moveaxis(value, 1, 0).reshape((all_picks,) + value.shape[3:])

    def to_own(value):
        return lax.all_to_all(value.reshape(tp_count, own_rows, width), "tp", 0, 0, tiled=True)

    hidden_own = lax.dynamic_slice_in_dim(hidden_state, tp_rank * own_rows, own_rows, 0)
    normed2_own = lax.dynamic_slice_in_dim(normed2, tp_rank * own_rows, own_rows, 0)
    tile_cols = w_unpatch.shape[1]
    first_ray = (seq_rank * tp_count + tp_rank) * rays
    live_rays = (
        (first_ray + jnp.arange(rays, dtype=jnp.int32))[None, :] < ray_count[:, None]
    ).astype(F32)
    (
        result_own,
        colours,
        grad_tiles,
        grad_result,
        grad_result_low,
        dec1_part,
        dec1_bias_part,
        dec2_part,
    ) = render(
        to_own(down),
        hidden_own,
        unpatch_all,
        bias_all,
        corners,
        w_dec1,
        b_dec1,
        w_dec2,
        live_rays.reshape(-1, 1),
        jnp.moveaxis(color_grad, 1, -1).reshape(-1, 3),
    )
    colours = colours.reshape(scenes, rays, 3)
    result_rows = lax.all_gather(grad_result_low, "tp", axis=0, tiled=True)
    grad_active = dot("rd,fd->rf", result_rows, w_down)
    grad_preact = jax.vjp(jax.nn.gelu, preact)[1](grad_active)[0].astype(BF)
    grad_normed2 = dot("rf,df->rd", grad_preact, w_up).astype(BF)
    grad_normed2, qkv_all = lax.optimization_barrier((grad_normed2, qkv_all))
    dec1_cols = w_dec1.shape[1] // tp_count
    dec1_part = jnp.moveaxis(dec1_part.reshape(-1, tp_count, dec1_cols), 1, 0)
    small = [dec1_part, dec1_bias_part, dec2_part]
    small = jnp.concatenate([piece.reshape(tp_count, -1) for piece in small], axis=1)
    colours = jnp.moveaxis(colours, -1, 1)
    grad_normed2, small, colours = lax.optimization_barrier(
        (to_own(grad_normed2), small, colours)
    )
    grad_normed2 = jnp.sum(grad_normed2.astype(F32), axis=0)
    standard2, scale2 = standard_rows(hidden_own)
    gain2_part = jnp.sum(grad_normed2 * standard2, axis=0)
    shift2_part = jnp.sum(grad_normed2, axis=0)
    grad_hidden = grad_result + norm_back(standard2, scale2, norm2_gain, grad_normed2)
    def to_owner(value):
        return lax.all_to_all(value, "tp", 0, 0, tiled=True)

    def by_owner(value, own):
        value = value.reshape(-1, tp_count, own, value.shape[-1])
        return jnp.moveaxis(value, 1, 0)

    normed_picks = norm_rows(picked_rows, norm1_gain, norm1_bias).astype(BF)
    hidden_low = grad_hidden.astype(BF)
    grad_mixed = dot("kd,ted->tke", hidden_low, w_out_all).astype(BF)
    hidden_cols = jnp.moveaxis(hidden_low.reshape(own_rows, tp_count, cols), 1, 0)
    early = jnp.concatenate([normed2_own, result_own, grad_result_low, hidden_low], axis=1)
    early = spread(early, "seq").reshape(-1, 4 * width)
    mixed_own = lax.dynamic_slice_in_dim(mixed_all[..., :cols], tp_rank * own_rows, own_rows, 1)
    sent = to_all(jnp.concatenate([grad_mixed, mixed_own], axis=-1))
    later = jnp.concatenate([hidden_cols, grad_tiles], axis=-1)
    small = [gain2_part.reshape(tp_count, -1), shift2_part.reshape(tp_count, -1), small]
    small = jnp.concatenate(small, axis=1)
    sent, later, early_rows, small = lax.optimization_barrier((sent, later, early, small))
    later = to_all(later).reshape(all_picks, cols + tile_cols)

    early = lax.all_gather(early_rows, "tp", axis=0, tiled=True)
    scene_sent = by_scene(sent)
    made, totals = [], []
    operands = (queries, patch_kv, plane_kv, scene_sent, logsum)
    operands += (
        patch_normed.reshape(scenes, patch_local, width),
        plane_normed.reshape(scenes, plane_local, width),
    )
    for n in range(scenes):
        if n == scenes - 1:
            operands, later = lax.optimization_barrier((operands, later))
        *one, part, sums = attend_back(n, *operands, totals, heads)
        made.append(one)
        totals = [part, sums]
    kv_sent = to_owner(
        jnp.concatenate(
            [
                jnp.concatenate([by_owner(one[1], own_patch), by_owner(one[2], own_plane)], axis=2)
                for one in made
            ],
            axis=1,
        )
    )
    grad_query = jnp.concatenate([one[0] for one in made], axis=0)
    kv_part, kv_sum = totals
    hidden_cols = later[:, :cols]
    grad_query = split_sum(by_seq(grad_query).reshape(all_picks, cols), "seq").astype(BF)
    grad_query, sent = lax.optimization_barrier((grad_query, sent))
    query_part = dot("rd,re->ed", normed_picks, grad_query)
    qkv_part = jnp.concatenate([kv_part, query_part], axis=0)
    size = width // seq_count

    def block_of(mask):
        return lax.dynamic_slice_in_dim(qkv_part, (seq_rank ^ mask) * size, size, 1)

    own_block = block_of(0)
    received = []
    for mask in range(1, seq_count):
        block = lax.ppermute(block_of(mask).astype(BF), "seq", xor_pairs(seq_count, mask))
        received.append(block)
    query_parts = [grad_query] + [
        lax.ppermute(grad_query, "seq", xor_pairs(seq_count, mask)) for mask in range(1, seq_count)
    ]
    query_sum = jnp.sum(grad_query.astype(F32), axis=0)
    sums = jnp.concatenate([kv_sum[0], query_sum])[:, None]
    wide = qkv_weight.astype(F32)
    shift1_part = jnp.sum(wide * sums, axis=0)
    product = jnp.sum(wide * qkv_part, axis=0)
    gain1_part = (product - norm1_bias * shift1_part) / norm1_gain

    up_grad, down_grad, out_grad, unpatch_grad, unpatch_bias_grad = weight_grads(
        early,
        w_up,
        w_down,
        tp_first(sent.reshape(all_picks, 2 * cols)[:, cols:]),
        tp_first(later[:, cols:]),
    )
    query_parts, own_block, up_grad = lax.optimization_barrier((query_parts, own_block, up_grad))
    qkv_sum = (own_block + sum(block.astype(F32) for block in received)).astype(BF)
    scattered = scatter(
        seq_rank,
        row_ids.reshape(seq_count, 1, seq_picks),
        hidden_cols.reshape(seq_count, seq_picks, cols),
        query_parts,
        (tp_count, scenes, own_plane, 2 * cols),
    )

    unpatch_bias_grad = unpatch_bias_grad[0]

    scattered, kv_sent, up_grad, qkv_sum = lax.optimization_barrier(
        (scattered, kv_sent, up_grad, qkv_sum)
    )
    extra_sent = to_owner(scattered)
    qkv_parts = [qkv_sum] + [
        lax.ppermute(qkv_sum, "seq", xor_pairs(seq_count, mask)) for mask in range(1, seq_count)
    ]

    pieces = [gain1_part.reshape(tp_count, -1), shift1_part.reshape(tp_count, -1), small]
    pieces, _ = lax.optimization_barrier((jnp.concatenate(pieces, axis=1), extra_sent))
    pieces = jnp.sum(to_all(pieces), axis=0)
    sizes = [width // tp_count] * 4
    sizes += [w_dec1.shape[0] * dec1_cols, dec1_cols, dec1_cols * w_dec2.shape[1]]
    totals = []
    for count in sizes:
        totals.append(pieces[:count])
        pieces = pieces[count:]
    gain1_grad, shift1_grad, gain2_grad, shift2_grad = totals[:4]
    dec1_grad, dec1_bias_grad, dec2_grad = totals[4:]

    patch_grad, plane_grad = finish(
        kv_sent, extra_sent, qkv_all, patch_tokens, plane_tokens, norm1_gain, tp_rank, cols
    )
    qkv_parts, patch_grad = lax.optimization_barrier((qkv_parts, patch_grad))
    key_grad, value_grad, query_grad = turn(seq_rank, qkv_parts)
    return (
        colours,
        patch_grad,
        plane_grad,
        gain1_grad,
        shift1_grad,
        query_grad,
        key_grad,
        value_grad,
        out_grad,
        gain2_grad,
        shift2_grad,
        up_grad,
        down_grad,
        unpatch_grad,
        unpatch_bias_grad,
        dec1_grad.reshape(-1, dec1_cols),
        dec1_bias_grad,
        dec2_grad.reshape(-1, w_dec2.shape[1]),
    )


def solution(mesh):
    in_specs = (
        P(None, "seq", None),
        P(None, "seq", None),
        P(),
        P(),
        P(None, "tp"),
        P(None, "tp"),
        P(None, "tp"),
        P("tp", None),
        P(),
        P(),
        P(None, "tp"),
        P("tp", None),
        P(None, "tp"),
        P("tp"),
        P(),
        P(),
        P(),
        P(None, None, "seq"),
        P(None, "seq", None, "tp", None),
        P(),
        P(None, None, ("seq", "tp")),
    )
    out_specs = (
        P(None, None, ("seq", "tp")),
        P(None, ("seq", "tp"), None),
        P(None, ("seq", "tp"), None),
        P("tp"),
        P("tp"),
        P(None, "tp"),
        P(None, "tp"),
        P(None, "tp"),
        P("tp", None),
        P("tp"),
        P("tp"),
        P(None, "tp"),
        P("tp", None),
        P(None, "tp"),
        P("tp"),
        P(None, "tp"),
        P("tp"),
        P("tp", None),
    )
    return jax.shard_map(
        on_device, mesh=mesh, in_specs=in_specs, out_specs=out_specs, check_vma=False
    )
```

```python
import functools

import jax
import jax.numpy as jnp
from jax import lax
from jax.experimental import pallas as pl
from jax.experimental.pallas import tpu as pltpu
from jax.sharding import PartitionSpec as P

HEAD_DIM = 64
CH = 32
TRI_SIDE = 32
BF = jnp.bfloat16
F32 = jnp.float32
HIGH = lax.Precision.HIGHEST


def dot(spec, *operands):
    return jnp.einsum(spec, *operands, preferred_element_type=F32)


def standard_rows(token_rows):
    centre = jnp.mean(token_rows, axis=-1, keepdims=True)
    offset = token_rows - centre
    spread = jnp.mean(offset * offset, axis=-1, keepdims=True)
    scale = lax.rsqrt(spread + 1e-05)
    return offset * scale, scale


def norm_rows(token_rows, norm_gain, norm_shift):
    return standard_rows(token_rows)[0] * norm_gain + norm_shift


def norm_back(standard, scale, norm_gain, grad):
    scaled = grad * norm_gain
    first = jnp.mean(scaled, axis=-1, keepdims=True)
    second = jnp.mean(scaled * standard, axis=-1, keepdims=True)
    return scale * (scaled - first - standard * second)


def xor_pairs(size, mask):
    return [(i, i ^ mask) for i in range(size)]


def hyper_sum(value, axes):
    for axis in axes:
        size = lax.axis_size(axis)
        mask = 1
        while mask < size:
            value = value + lax.ppermute(value, axis, xor_pairs(size, mask))
            mask *= 2
    return value


def block_rows(rows, limit):
    best = rows
    for size in range(16, limit + 1, 16):
        if rows % size == 0:
            best = size
    return best


def params(size=60):
    return pltpu.CompilerParams(vmem_limit_bytes=size * 2**20)


def cost(flops, bytes_accessed, transcendentals=0):
    return pl.CostEstimate(
        flops=flops, bytes_accessed=bytes_accessed, transcendentals=transcendentals
    )


def project_kernel(weight_count, rows_ref, gain_ref, bias_ref, *refs):
    weights, (normed_ref, kv_ref, *query_refs) = refs[:weight_count], refs[weight_count:]
    rows = rows_ref[...].astype(F32)
    normed = norm_rows(rows, gain_ref[...], bias_ref[...]).astype(BF)
    normed_ref[...] = normed
    made = [jnp.dot(normed, w[...], preferred_element_type=F32).astype(BF) for w in weights]
    kv_ref[...] = jnp.concatenate(made[:2], axis=1)
    for ref, value in zip(query_refs, made[2:]):
        ref[...] = value


def project(token_rows, gain, bias, *weights):
    rows, width = token_rows.shape
    cols = weights[0].shape[1]
    block = block_rows(rows, 512)
    widths = [width, 2 * cols] + [cols] * (len(weights) - 2)
    whole = lambda i: (0, 0)
    mine = lambda i: (i, 0)
    return pl.pallas_call(
        functools.partial(project_kernel, len(weights)),
        grid=(rows // block,),
        in_specs=[
            pl.BlockSpec((block, width), mine),
            pl.BlockSpec((1, width), whole),
            pl.BlockSpec((1, width), whole),
        ]
        + [pl.BlockSpec((width, cols), whole) for _ in weights],
        out_specs=[pl.BlockSpec((block, w), mine) for w in widths],
        out_shape=[jax.ShapeDtypeStruct((rows, w), BF) for w in widths],
        compiler_params=params(),
        cost_estimate=cost(
            2 * rows * width * cols * len(weights), rows * (width + sum(widths)) * 2
        ),
        name="norm_project",
    )(token_rows, gain[None], bias[None], *weights)


def pieces_of(value):
    high = lax.reduce_precision(value, 8, 7)
    middle = lax.reduce_precision(value - high, 8, 7)
    return [high.astype(BF), middle.astype(BF), (value - high - middle).astype(BF)]


def dot_dims(left, right, left_dim, right_dim):
    dims = (((left_dim,), (right_dim,)), ((), ()))
    return lax.dot_general(left, right, dims, preferred_element_type=F32)


def attend_kernel(heads, q_ref, first_ref, second_ref, out_ref, logsum_ref):
    cols = heads * HEAD_DIM
    parts, stats = [], []
    for h in range(heads):
        here = slice(h * HEAD_DIM, (h + 1) * HEAD_DIM)
        there = slice(cols + h * HEAD_DIM, cols + (h + 1) * HEAD_DIM)
        query = q_ref[0, :, here] * BF(HEAD_DIM**-0.5)
        scores = [dot_dims(ref[0, :, here], query, 1, 1) for ref in (first_ref, second_ref)]
        top = jnp.maximum(*[jnp.max(s, axis=0, keepdims=True) for s in scores])
        raised = [jnp.exp(s - top) for s in scores]
        total = sum(jnp.sum(r, axis=0, keepdims=True) for r in raised)
        mixed = sum(
            dot_dims(ref[0, :, there], r.astype(BF), 0, 0)
            for ref, r in zip((first_ref, second_ref), raised)
        )
        parts.append(mixed / total)
        stats.append(top + jnp.log(total))
    out_ref[0] = jnp.concatenate(parts, axis=0).T.astype(BF)
    logsum_ref[0] = jnp.concatenate(stats, axis=0)


def attend(queries, first, second, heads):
    scenes, count, cols = queries.shape
    keys = first.shape[1] + second.shape[1]
    scene = lambda n: (n, 0, 0)
    return pl.pallas_call(
        functools.partial(attend_kernel, heads),
        grid=(scenes,),
        in_specs=[pl.BlockSpec((1,) + a.shape[1:], scene) for a in (queries, first, second)],
        out_specs=[
            pl.BlockSpec((1, count, cols), scene),
            pl.BlockSpec((1, heads, count), scene),
        ],
        out_shape=[
            jax.ShapeDtypeStruct((scenes, count, cols), BF),
            jax.ShapeDtypeStruct((scenes, heads, count), F32),
        ],
        compiler_params=params(),
        cost_estimate=cost(
            scenes * heads * count * keys * 16 * HEAD_DIM * 2,
            scenes * keys * cols * 4,
            scenes * heads * count * keys,
        ),
        name="attend",
    )(queries, first, second)


def attend_back_kernel(heads, *refs):
    q_ref, first_ref, second_ref, grad_ref, logsum_ref, na_ref, nb_ref = refs[:7]
    gq_ref, ga_ref, gb_ref, part_ref, sum_ref = refs[-5:]
    if len(refs) > 12:
        part_ref[...] = refs[7][...]
        sum_ref[...] = refs[8][...]
    else:
        part_ref[...] = jnp.zeros_like(part_ref)
        sum_ref[...] = jnp.zeros_like(sum_ref)
    cols = heads * HEAD_DIM
    count = q_ref.shape[1]
    scale = HEAD_DIM**-0.5
    cut = [slice(h * HEAD_DIM, (h + 1) * HEAD_DIM) for h in range(heads)]
    query = [q_ref[0, :, c] * BF(scale) for c in cut]
    grad = [grad_ref[0, :, c] for c in cut]
    ones = jnp.ones((8, HEAD_DIM), F32)
    inner = [
        lax.dot_general(
            ones,
            grad_ref[0, :, cols + c.start : cols + c.stop].astype(F32) * g.astype(F32),
            (((1,), (1,)), ((), ())),
            precision=HIGH,
            preferred_element_type=F32,
        )[:1]
        for c, g in zip(cut, grad)
    ]
    totals = tuple(jnp.zeros((HEAD_DIM, count), F32) for _ in cut)
    for ref, out_ref, normed_ref in ((first_ref, ga_ref, na_ref), (second_ref, gb_ref, nb_ref)):
        rows = ref.shape[1]
        block = block_rows(rows, 512)

        def step(i, totals, ref=ref, out_ref=out_ref, normed_ref=normed_ref, block=block):
            place = pl.ds(pl.multiple_of(i * block, block), block)
            keys, grads, sums = [], [], []
            for h in range(heads):
                key = ref[0, place, cut[h]]
                value = ref[0, place, slice(cols + cut[h].start, cols + cut[h].stop)]
                shares = jnp.exp(dot_dims(key, query[h], 1, 1) - logsum_ref[0, h : h + 1, :])
                grad_shares = dot_dims(value, grad[h], 1, 1)
                grad_scores = (shares * (grad_shares - inner[h])).astype(BF)
                keys.append(jnp.dot(grad_scores, query[h], preferred_element_type=F32))
                grads.append(jnp.dot(shares.astype(BF), grad[h], preferred_element_type=F32))
                sums.append(totals[h] + dot_dims(key, grad_scores, 0, 0))
            made = jnp.concatenate(keys + grads, axis=1).astype(BF)
            out_ref[0, place, :] = made
            part_ref[...] += dot_dims(made, normed_ref[0, place, :], 0, 0)
            sum_ref[...] += jnp.sum(made.astype(F32), axis=0, keepdims=True)
            return tuple(sums)

        totals = lax.fori_loop(0, rows // block, step, totals, unroll=True)
    gq_ref[0] = (jnp.concatenate(totals, axis=0) * scale).T.astype(BF)


def attend_back(scene, queries, first, second, grad, logsum, normed_first, normed_second, before, heads):
    scenes, count, cols = queries.shape
    keys, width = first.shape[1] + second.shape[1], normed_first.shape[2]
    mine = lambda i: (scene, 0, 0)
    whole = lambda i: (0, 0)
    operands = (queries, first, second, grad, logsum, normed_first, normed_second)
    totals = [(2 * cols, width), (1, 2 * cols)]
    outs = [(1,) + a.shape[1:] for a in (queries, first, second)]
    return pl.pallas_call(
        functools.partial(attend_back_kernel, heads),
        grid=(1,),
        in_specs=[pl.BlockSpec((1,) + a.shape[1:], mine) for a in operands]
        + [pl.BlockSpec(a.shape, whole) for a in before],
        out_specs=[pl.BlockSpec(a, lambda i: (0, 0, 0)) for a in outs]
        + [pl.BlockSpec(a, whole) for a in totals],
        out_shape=[jax.ShapeDtypeStruct(a, BF) for a in outs]
        + [jax.ShapeDtypeStruct(a, F32) for a in totals],
        compiler_params=params(),
        cost_estimate=cost(
            heads * count * keys * 40 * HEAD_DIM * 2 + 4 * keys * cols * width,
            keys * (cols * 8 + width * 2),
            heads * count * keys,
        ),
        name="attend_back",
    )(*operands, *before)


def finish_kernel(cols, rank_ref, kv_ref, extra_ref, weight_ref, gain_ref, patch_ref, plane_ref, *outs):
    own_patch = patch_ref.shape[2]
    parts = kv_ref.shape[0]
    total = sum(dot_dims(kv_ref[t, 0], weight_ref[t, : 2 * cols], 1, 0) for t in range(parts))
    more = sum(
        dot_dims(extra_ref[t, 0, :, :cols], weight_ref[t, 2 * cols :], 1, 0)
        for t in range(parts)
    )
    grads = (total[:own_patch], total[own_patch:] + more)
    extra = jnp.concatenate([extra_ref[t, 0, :, cols:] for t in range(parts)], axis=1)
    added = (0.0, extra.astype(F32))
    for ref, out_ref, grad, plus in zip((patch_ref, plane_ref), outs, grads, added):
        standard, scale = standard_rows(ref[0, 0].astype(F32))
        out_ref[0] = norm_back(standard, scale, gain_ref[...], grad) + plus


def finish(kv_sent, extra_sent, weights, patch_rows, plane_rows, gain, rank, cols):
    parts, scenes, rows, _ = kv_sent.shape
    width = weights.shape[2]
    tokens = [a.reshape(scenes, parts, -1, width) for a in (patch_rows, plane_rows)]
    by_part = lambda n, rank: (0, n, 0, 0)
    spec = pltpu.PrefetchScalarGridSpec(
        num_scalar_prefetch=1,
        grid=(scenes,),
        in_specs=[
            pl.BlockSpec((parts, 1) + kv_sent.shape[2:], by_part),
            pl.BlockSpec((parts, 1) + extra_sent.shape[2:], by_part),
            pl.BlockSpec(weights.shape, lambda n, rank: (0, 0, 0)),
            pl.BlockSpec((1, width), lambda n, rank: (0, 0)),
        ]
        + [pl.BlockSpec((1, 1) + a.shape[2:], lambda n, rank: (n, rank[0], 0, 0)) for a in tokens],
        out_specs=[pl.BlockSpec((1,) + a.shape[2:], lambda n, rank: (n, 0, 0)) for a in tokens],
    )
    return pl.pallas_call(
        functools.partial(finish_kernel, cols),
        grid_spec=spec,
        out_shape=[jax.ShapeDtypeStruct((scenes,) + a.shape[2:], F32) for a in tokens],
        compiler_params=params(),
        cost_estimate=cost(
            scenes * rows * width * parts * 3 * cols * 2, weights.size * 2 + rows * width * 16
        ),
        name="finish",
    )(rank.reshape(1), kv_sent, extra_sent, weights, gain[None], *tokens)


def turn_kernel(rank_ref, *refs):
    parts, outs = refs[:-3], refs[-3:]
    cols, size = outs[0].shape[1], parts[0].shape[1]
    for mask, part in enumerate(parts):
        place = pl.ds(pl.multiple_of((rank_ref[0] ^ mask) * size, size), size)
        for k, ref in enumerate(outs):
            ref[place, :] = part[k * cols : (k + 1) * cols].astype(F32).T


def turn(rank, parts):
    rows, width = parts[0].shape[0], parts[0].shape[1] * len(parts)
    whole = lambda i, r: (0, 0)
    spec = pltpu.PrefetchScalarGridSpec(
        num_scalar_prefetch=1,
        grid=(1,),
        in_specs=[pl.BlockSpec(a.shape, whole) for a in parts],
        out_specs=[pl.BlockSpec((width, rows // 3), whole)] * 3,
    )
    return pl.pallas_call(
        turn_kernel,
        grid_spec=spec,
        out_shape=[jax.ShapeDtypeStruct((width, rows // 3), F32)] * 3,
        compiler_params=params(),
        cost_estimate=cost(1, 1),
        name="turn",
    )(rank.reshape(1), *parts)


def gelu_parts(value):
    slope = 0.7978845608028654
    square = value * value
    bent = jnp.tanh(slope * value * (1.0 + 0.044715 * square))
    half = 0.5 * (1.0 + bent)
    rise = 0.5 * value * (1.0 - bent * bent) * (slope * (1.0 + 0.134145 * square))
    return value * half, half + rise


def weights_kernel(width, rows_ref, up_ref, down_ref, mixed_ref, hidden_ref, tile_ref, *outs):
    up_out, down_out, mix_out, tile_out, sum_out = outs
    unit_step, pick_step = pl.program_id(0), pl.program_id(1)
    normed, result, grad_result = [rows_ref[:, k * width : (k + 1) * width] for k in range(3)]

    @pl.when(pick_step == 0)
    def _():
        up_out[...] = jnp.zeros_like(up_out)
        down_out[...] = jnp.zeros_like(down_out)

    @pl.when((pick_step == 0) & (unit_step == 0))
    def _():
        mix_out[...] = jnp.zeros_like(mix_out)
        tile_out[...] = jnp.zeros_like(tile_out)
        sum_out[...] = jnp.zeros_like(sum_out)

    preact = jnp.dot(normed, up_ref[...], preferred_element_type=F32)
    active, slope = gelu_parts(preact)
    down_out[...] += dot_dims(active.astype(BF), grad_result, 0, 0)
    grad = (dot_dims(grad_result, down_ref[...], 1, 1) * slope).astype(BF)
    up_out[...] += dot_dims(normed, grad, 0, 0)

    @pl.when(unit_step == 0)
    def _():
        parts = [dot_dims(mixed_ref[...], hidden_ref[t], 0, 0) for t in range(hidden_ref.shape[0])]
        mix_out[...] += jnp.concatenate(parts, axis=1)
        tile_out[...] += dot_dims(result, tile_ref[...], 0, 0)
        sum_out[...] += jnp.sum(tile_ref[...].astype(F32), axis=0, keepdims=True)


def weight_grads(rows, w_up, w_down, mixed, hidden, tiles):
    picks, width = rows.shape[0], rows.shape[1] // 3
    units, cols, tile_cols = w_up.shape[1], mixed.shape[1], tiles.shape[1]
    block, units_block = block_rows(picks, 768), block_rows(units, 512)
    here = lambda g, p: (p, 0)
    whole = lambda g, p: (0, 0)
    return pl.pallas_call(
        functools.partial(weights_kernel, width),
        grid=(units // units_block, picks // block),
        in_specs=[
            pl.BlockSpec((block, 3 * width), here),
            pl.BlockSpec((width, units_block), lambda g, p: (0, g)),
            pl.BlockSpec((units_block, width), lambda g, p: (g, 0)),
            pl.BlockSpec((block, cols), here),
            pl.BlockSpec((hidden.shape[0], block, cols), lambda g, p: (0, p, 0)),
            pl.BlockSpec((block, tile_cols), here),
        ],
        out_specs=[
            pl.BlockSpec((width, units_block), lambda g, p: (0, g)),
            pl.BlockSpec((units_block, width), lambda g, p: (g, 0)),
            pl.BlockSpec((cols, width), whole),
            pl.BlockSpec((width, tile_cols), whole),
            pl.BlockSpec((1, tile_cols), whole),
        ],
        out_shape=[
            jax.ShapeDtypeStruct(shape, F32)
            for shape in (
                (width, units),
                (units, width),
                (cols, width),
                (width, tile_cols),
                (1, tile_cols),
            )
        ],
        compiler_params=params(),
        cost_estimate=cost(
            2 * picks * width * (4 * units + cols + tile_cols),
            rows.size * 2 + width * units * 12,
            picks * units,
        ),
        name="weight_grads",
    )(rows, w_up, w_down, mixed, hidden, tiles)


def scatter_kernel(scenes, own, rank_ref, ids_ref, hidden_ref, *refs):
    parts, out_ref = refs[:-1], refs[-1]
    rank = rank_ref[0]
    seq_picks = parts[0].shape[0]
    values = [
        jnp.concatenate([part[...], hidden_ref[rank ^ m]], axis=1) for m, part in enumerate(parts)
    ]
    row = lax.broadcasted_iota(jnp.int32, (own, seq_picks), 0)
    blocks = out_ref.shape[0]

    def step(t, carry):
        for n in range(scenes):
            first = (n * blocks + t) * own
            total = sum(
                jnp.dot(
                    (row + first == ids_ref[rank ^ m]).astype(F32).astype(BF),
                    value,
                    preferred_element_type=F32,
                )
                for m, value in enumerate(values)
            )
            out_ref[t, n] = total.astype(BF)
        return carry

    lax.fori_loop(0, blocks, step, 0)


def scatter(rank, ids, hidden, parts, shape):
    spec = pltpu.PrefetchScalarGridSpec(
        num_scalar_prefetch=1,
        grid=(1,),
        in_specs=[
            pl.BlockSpec(a.shape, lambda i, r, k=a.ndim: (0,) * k) for a in (ids, hidden, *parts)
        ],
        out_specs=pl.BlockSpec(shape, lambda i, r: (0, 0, 0, 0)),
    )
    return pl.pallas_call(
        functools.partial(scatter_kernel, shape[1], shape[2]),
        grid_spec=spec,
        out_shape=jax.ShapeDtypeStruct(shape, BF),
        compiler_params=params(),
        cost_estimate=cost(2 * shape[0] * shape[1] * shape[2] * shape[3] * ids.size, hidden.size * 8),
        name="scatter",
    )(rank.reshape(1), ids, hidden, *parts)


def spread(value, axis):
    size, rank = lax.axis_size(axis), lax.axis_index(axis)
    out = jnp.zeros((size,) + value.shape, value.dtype)
    for mask in range(size):
        other = lax.ppermute(value, axis, xor_pairs(size, mask)) if mask else value
        out = lax.dynamic_update_index_in_dim(out, other, rank ^ mask, 0)
    return out


def split_sum(value, axis):
    size, rank = lax.axis_size(axis), lax.axis_index(axis)
    value = value.reshape((size, value.shape[0] // size) + value.shape[1:])
    total = lax.dynamic_index_in_dim(value, rank, 0, keepdims=False)
    for mask in range(1, size):
        block = lax.dynamic_index_in_dim(value, rank ^ mask, 0, keepdims=False).astype(BF)
        total = total + lax.ppermute(block, axis, xor_pairs(size, mask)).astype(F32)
    return total


def dot_high(left, right, left_dim, right_dim):
    dims = (((left_dim,), (right_dim,)), ((), ()))
    return lax.dot_general(left, right, dims, precision=HIGH, preferred_element_type=F32)


def render_kernel(*refs):
    came_ref, hidden_ref, unpatch_ref, shift_ref, corner_ref, select_ref = refs[:6]
    w1_ref, b1_ref, w2_ref, live_ref, cotangent_ref = refs[6:11]
    (result_ref, colour_ref, tiles_ref, grad_ref, low_ref, g1_ref, gb_ref, g2_ref) = refs[11:]
    parts, rows, _ = came_ref.shape
    rays, _, samples = corner_ref.shape
    result = hidden_ref[...] + sum(came_ref[t].astype(F32) for t in range(parts))
    result = result.astype(BF)
    result_ref[...] = result
    tiles = [
        (jnp.dot(result, unpatch_ref[t], preferred_element_type=F32) + shift_ref[t]).astype(BF)
        for t in range(parts)
    ]
    tiles = jnp.concatenate(tiles, axis=0)
    lines, tile_cols = corner_ref.shape[1], tiles.shape[1]

    def place(shape, dim):
        return lax.broadcasted_iota(jnp.int32, shape, dim)

    pixel_mask = tile_cols // CH - 1
    pixel = place((lines, tile_cols), 1) >> (CH.bit_length() - 1)
    pixel = (pixel == (place((lines, tile_cols), 0) & pixel_mask)).astype(F32)
    pick_out = (place((CH, tile_cols), 1) & (CH - 1)) == place((CH, tile_cols), 0)
    pick_out = pick_out.astype(F32).astype(BF)
    units = b1_ref.shape[1]
    bias = jnp.where(place((units, units), 0) == place((units, units), 1), b1_ref[...], 0.0)
    bias = jnp.sum(bias, axis=1, keepdims=True)
    features = []
    for r in range(rays):
        mine = jnp.dot(select_ref[r], tiles, preferred_element_type=F32) * pixel
        mine = dot_dims(mine.astype(BF), pick_out, 1, 1).astype(BF)
        features.append(dot_dims(mine, corner_ref[r], 0, 0))
    features = jnp.concatenate(features, axis=1)
    preact = dot_high(w1_ref[...], features, 0, 0) + bias
    gate = 1.0 / (1.0 + jnp.exp(-preact))
    hidden = preact * gate
    output = dot_high(w2_ref[...], hidden, 0, 0)

    def by_ray(row):
        return jnp.concatenate(
            [row[:, r * samples : (r + 1) * samples] for r in range(rays)], axis=0
        )

    def in_row(value):
        return jnp.concatenate([value[r : r + 1] for r in range(rays)], axis=1)

    first = by_ray(output[0:1])
    density = jnp.maximum(first, 0.0) + jnp.log1p(jnp.exp(-jnp.abs(first)))
    shades = [1.0 / (1.0 + jnp.exp(-by_ray(output[k : k + 1]))) for k in (1, 2, 3)]
    optical = density * (2.0 / samples)
    before = (
        lax.broadcasted_iota(jnp.int32, (samples, samples), 0)
        < lax.broadcasted_iota(jnp.int32, (samples, samples), 1)
    ).astype(F32)
    through = jnp.exp(-dot_high(optical, before, 1, 0))
    kept = jnp.exp(-optical)
    weight = through * (1.0 - kept)
    live = live_ref[...]
    colour_ref[...] = jnp.concatenate(
        [jnp.sum(weight * shade, axis=1, keepdims=True) * live for shade in shades], axis=1
    )
    grads = [cotangent_ref[:, k : k + 1] * live for k in range(3)]
    grad_weight = sum(g * shade for g, shade in zip(grads, shades))
    grad_before = -through * grad_weight * (1.0 - kept)
    grad_optical = dot_high(grad_before, before, 1, 1) + grad_weight * through * kept
    grad_first = grad_optical * (2.0 / samples) * (1.0 / (1.0 + jnp.exp(-first)))
    grad_shades = [g * weight * shade * (1.0 - shade) for g, shade in zip(grads, shades)]
    grad_output = jnp.concatenate([in_row(g) for g in [grad_first] + grad_shades], axis=0)
    grad_preact = jnp.dot(w2_ref[...], grad_output, precision=HIGH, preferred_element_type=F32)
    grad_preact = grad_preact * (gate * (1.0 + preact * (1.0 - gate)))
    g2_ref[...] = dot_high(hidden, grad_output, 1, 1)
    gb_ref[...] = jnp.sum(grad_preact, axis=1, keepdims=True)
    g1_ref[...] = dot_high(features, grad_preact, 1, 1)
    grad_features = jnp.dot(w1_ref[...], grad_preact, precision=HIGH, preferred_element_type=F32)
    total = jnp.zeros(tiles.shape, F32)
    for r in range(rays):
        mine = grad_features[:, r * samples : (r + 1) * samples]
        high = mine.astype(BF)
        low = (mine - high.astype(F32)).astype(BF)
        corner = corner_ref[r]
        mine = (dot_dims(corner, high, 1, 1) + dot_dims(corner, low, 1, 1)).astype(BF)
        mine = jnp.dot(mine, pick_out, preferred_element_type=F32) * pixel
        total = total + dot_dims(select_ref[r], mine.astype(BF), 0, 0)
    grad = jnp.zeros(grad_ref.shape, F32)
    for t in range(parts):
        mine = total[t * rows : (t + 1) * rows].astype(BF)
        tiles_ref[t] = mine
        grad = grad + dot_dims(mine, unpatch_ref[t], 1, 1)
    grad_ref[...] = grad
    low_ref[...] = grad.astype(BF)


def render(came, hidden_own, unpatch, shift, corners, w1, b1, w2, live, cotangent):
    parts, rows, width = came.shape
    scenes, rays, tile_cols = corners.shape[1], corners.shape[2], unpatch.shape[2]
    pixels, samples = corners.shape[4], corners.shape[5]
    corners = jnp.transpose(corners, (1, 2, 0, 3, 4, 5))
    corners = corners.reshape(scenes * rays, parts * 3 * pixels, samples)
    ray = jnp.arange(scenes * rays)[:, None, None]
    line = jnp.arange(parts * 3 * pixels)[None, :, None]
    source = (line // (3 * pixels)) * rows + (line // pixels) % 3 * rays
    source = source + (ray // rays) * (3 * rays) + ray % rays
    select = (source == jnp.arange(parts * rows)[None, None, :]).astype(BF)
    hidden_units = w1.shape[1]
    operands = (came, hidden_own, unpatch, shift[:, None], corners, select)
    operands += (w1, b1[None], w2, live, cotangent)
    outs = [
        ((rows, width), BF),
        (cotangent.shape, F32),
        ((parts, rows, tile_cols), BF),
        ((rows, width), F32),
        ((rows, width), BF),
        (w1.shape, F32),
        ((hidden_units, 1), F32),
        (w2.shape, F32),
    ]
    return pl.pallas_call(
        render_kernel,
        out_shape=[jax.ShapeDtypeStruct(shape, kind) for shape, kind in outs],
        compiler_params=params(32),
        cost_estimate=cost(8 * rows * width * tile_cols * parts, unpatch.size * 2, 0),
        name="render",
    )(*operands)


def on_device(
    patch_tokens,
    plane_tokens,
    norm1_gain,
    norm1_bias,
    w_query,
    w_key,
    w_value,
    w_out,
    norm2_gain,
    norm2_bias,
    w_up,
    w_down,
    w_unpatch,
    b_unpatch,
    w_dec1,
    b_dec1,
    w_dec2,
    tile_index,
    corner_weights,
    ray_count,
    color_grad,
):
    scenes, patch_local, width = patch_tokens.shape
    plane_local = plane_tokens.shape[1]
    seq_count, tp_count = lax.axis_size("seq"), lax.axis_size("tp")
    seq_rank, tp_rank = lax.axis_index("seq"), lax.axis_index("tp")
    own_patch = patch_local // tp_count
    own_plane = plane_local // tp_count
    cols = w_query.shape[1]
    heads = cols // HEAD_DIM
    ray_seq = tile_index.shape[2]
    rays = ray_seq // tp_count
    picks = 3 * rays
    seq_picks = tp_count * scenes * picks
    all_picks = seq_count * seq_picks
    score_scale = HEAD_DIM**-0.5

    base = (jnp.arange(3, dtype=jnp.int32) * (TRI_SIDE * TRI_SIDE))[None, :, None]
    ids = (tile_index + base).reshape(scenes, 3, tp_count, rays)
    ids = jnp.transpose(ids, (2, 0, 1, 3)).reshape(tp_count, scenes, picks)
    ids = jnp.broadcast_to(ids[None], (seq_count,) + ids.shape)
    ids = lax.all_to_all(ids, "seq", 0, 0, tiled=True)
    plane_normed, plane_kv, query_rows = project(
        plane_tokens.reshape(-1, width), norm1_gain, norm1_bias, w_key, w_value, w_query
    )
    ids, query_rows = lax.optimization_barrier((ids, query_rows))
    local_ids = ids - seq_rank * plane_local
    inside = (local_ids >= 0) & (local_ids < plane_local)
    scene_base = (jnp.arange(scenes, dtype=jnp.int32) * plane_local)[None, None, :, None]
    row_ids = jnp.where(inside, local_ids + scene_base, -1).reshape(all_picks)
    onehot = (
        row_ids[:, None] == jnp.arange(scenes * plane_local, dtype=jnp.int32)[None, :]
    ).astype(BF)

    own_cols = lax.dynamic_slice_in_dim(plane_tokens, tp_rank * cols, cols, 2)
    chosen = jnp.dot(onehot, jnp.concatenate([query_rows, own_cols.reshape(-1, cols)], axis=1))
    chosen, corner_weights, w_key_later, patch_tokens = lax.optimization_barrier(
        (chosen, corner_weights, w_key, patch_tokens)
    )
    chosen = split_sum(chosen, "seq").astype(BF)
    chosen, patch_tokens = lax.optimization_barrier((chosen, patch_tokens))
    queries = spread(chosen[:, :cols], "seq").reshape(all_picks, cols)
    picked_cols = chosen[:, cols:]

    w_out_all = lax.all_gather(w_out, "tp", axis=0)
    unpatch_all = lax.all_gather(w_unpatch, "tp", axis=0)
    qkv_weight = jnp.concatenate([w_key_later.T, w_value.T, w_query.T], axis=0)
    qkv_all = lax.all_gather(qkv_weight, "tp", axis=0)

    corners = corner_weights.reshape(
        scenes, tp_count, rays, 3, corner_weights.shape[3], corner_weights.shape[4]
    )
    corners = lax.all_to_all(jnp.moveaxis(corners, 1, 0), "tp", 0, 0, tiled=True)

    patch_normed, patch_kv = project(
        patch_tokens.reshape(-1, width), norm1_gain, norm1_bias, w_key, w_value
    )
    queries, corners, patch_kv, picked_cols, w_out_all = lax.optimization_barrier(
        (queries, corners, patch_kv, picked_cols, w_out_all)
    )
    plane_kv = plane_kv.reshape(scenes, plane_local, 2 * cols)
    patch_kv = patch_kv.reshape(scenes, patch_local, 2 * cols)

    def by_scene(value):
        value = value.reshape(seq_count, tp_count, scenes, picks, -1)
        return jnp.moveaxis(value, 2, 0).reshape(scenes, seq_count * tp_count * picks, -1)

    def by_seq(value):
        value = value.reshape(scenes, seq_count, tp_count, picks, -1)
        return jnp.moveaxis(value, 0, 2).reshape(seq_count, seq_picks, -1)

    def in_heads(value):
        return value.reshape(value.shape[:-1] + (heads, HEAD_DIM))

    queries = by_scene(queries)
    part, logsum = attend(queries, patch_kv, plane_kv, heads)
    part = by_seq(part)
    flat = jnp.stack(pieces_of(logsum)).reshape(-1)
    stat_rows = -(-flat.shape[0] // (16 * cols)) * 16
    flat = jnp.pad(flat, (0, stat_rows * cols - flat.shape[0])).reshape(stat_rows, cols)
    flat = jnp.broadcast_to(flat[None], (seq_count, stat_rows, cols))
    part = lax.all_to_all(jnp.concatenate([part, flat], axis=1), "seq", 0, 0, tiled=True)
    logsums = part[:, seq_picks:].reshape(seq_count, -1)[:, : 3 * logsum.size]
    logsums = jnp.sum(logsums.reshape((seq_count, 3) + logsum.shape).astype(F32), axis=1)
    top = jnp.max(logsums, axis=0)
    logsum = top + jnp.log(jnp.sum(jnp.exp(logsums - top), axis=0))
    shares = jnp.exp(logsums - logsum)
    shares = shares.reshape(seq_count, scenes, heads, seq_count, tp_count, picks)
    shares = lax.dynamic_index_in_dim(shares, seq_rank, 3, keepdims=False)
    shares = jnp.transpose(shares, (0, 3, 1, 4, 2)).reshape(seq_count, seq_picks, heads, 1)
    mixed_low = jnp.sum(in_heads(part[:, :seq_picks].astype(F32)) * shares, axis=0)
    mixed_low = mixed_low.reshape(seq_picks, cols).astype(BF)

    bias_rows = jnp.stack(pieces_of(b_unpatch) + [jnp.zeros_like(b_unpatch, BF)] * 13)
    mixed_low = jnp.concatenate([mixed_low, picked_cols], axis=1)
    mixed_low = jnp.concatenate([mixed_low, bias_rows], axis=0)
    mixed_all = lax.all_gather(mixed_low, "tp", axis=0)
    bias_all = jnp.sum(mixed_all[:, seq_picks : seq_picks + 3].astype(F32), axis=1)
    mixed_all, unpatch_all = lax.optimization_barrier((mixed_all[:, :seq_picks], unpatch_all))
    branch = dot("tre,ted->rd", mixed_all[..., :cols], w_out_all)
    picked_rows = jnp.moveaxis(mixed_all[..., cols:], 0, 1).reshape(seq_picks, width)
    picked_rows = picked_rows.astype(F32)
    hidden_state = picked_rows + branch
    normed2 = norm_rows(hidden_state, norm2_gain, norm2_bias).astype(BF)
    preact = jnp.dot(normed2, w_up, preferred_element_type=F32)
    active = jax.nn.gelu(preact).astype(BF)
    down = jnp.dot(active, w_down, preferred_element_type=F32).astype(BF)
    own_rows = scenes * picks

    def to_all(value):
        value = jnp.broadcast_to(value[None], (seq_count,) + value.shape)
        value = value.reshape((seq_count * tp_count,) + value.shape[2:])
        return lax.all_to_all(value, ("seq", "tp"), 0, 0, tiled=True)

    def tp_first(value):
        value = value.reshape((seq_count, tp_count, own_rows) + value.shape[1:])
        return jnp.moveaxis(value, 1, 0).reshape((all_picks,) + value.shape[3:])

    def to_own(value):
        return lax.all_to_all(value.reshape(tp_count, own_rows, width), "tp", 0, 0, tiled=True)

    hidden_own = lax.dynamic_slice_in_dim(hidden_state, tp_rank * own_rows, own_rows, 0)
    normed2_own = lax.dynamic_slice_in_dim(normed2, tp_rank * own_rows, own_rows, 0)
    tile_cols = w_unpatch.shape[1]
    first_ray = (seq_rank * tp_count + tp_rank) * rays
    live_rays = (
        (first_ray + jnp.arange(rays, dtype=jnp.int32))[None, :] < ray_count[:, None]
    ).astype(F32)
    (
        result_own,
        colours,
        grad_tiles,
        grad_result,
        grad_result_low,
        dec1_part,
        dec1_bias_part,
        dec2_part,
    ) = render(
        to_own(down),
        hidden_own,
        unpatch_all,
        bias_all,
        corners,
        w_dec1,
        b_dec1,
        w_dec2,
        live_rays.reshape(-1, 1),
        jnp.moveaxis(color_grad, 1, -1).reshape(-1, 3),
    )
    colours = colours.reshape(scenes, rays, 3)
    result_rows = lax.all_gather(grad_result_low, "tp", axis=0, tiled=True)
    early = jnp.concatenate([normed2_own, result_own, grad_result_low], axis=1)
    early, result_rows = lax.optimization_barrier((early, result_rows))
    early = spread(early, "seq").reshape(-1, 3 * width)
    grad_active = dot("rd,fd->rf", result_rows, w_down)
    grad_preact = jax.vjp(jax.nn.gelu, preact)[1](grad_active)[0].astype(BF)
    grad_normed2 = dot("rf,df->rd", grad_preact, w_up).astype(BF)
    grad_normed2, qkv_all = lax.optimization_barrier((grad_normed2, qkv_all))
    dec1_cols = w_dec1.shape[1] // tp_count
    dec1_part = jnp.moveaxis(dec1_part.reshape(-1, tp_count, dec1_cols), 1, 0)
    small = [dec1_part, dec1_bias_part, dec2_part]
    small = jnp.concatenate([piece.reshape(tp_count, -1) for piece in small], axis=1)
    colours = jnp.moveaxis(colours, -1, 1)
    grad_normed2, small, colours, early = lax.optimization_barrier(
        (to_own(grad_normed2), small, colours, early)
    )
    early = lax.all_gather(early, "tp", axis=0, tiled=True)
    grad_normed2 = jnp.sum(grad_normed2.astype(F32), axis=0)
    standard2, scale2 = standard_rows(hidden_own)
    gain2_part = jnp.sum(grad_normed2 * standard2, axis=0)
    shift2_part = jnp.sum(grad_normed2, axis=0)
    grad_hidden = grad_result + norm_back(standard2, scale2, norm2_gain, grad_normed2)
    def to_owner(value):
        return lax.all_to_all(value, "tp", 0, 0, tiled=True)

    def by_owner(value, own):
        value = value.reshape(-1, tp_count, own, value.shape[-1])
        return jnp.moveaxis(value, 1, 0)

    normed_picks = norm_rows(picked_rows, norm1_gain, norm1_bias).astype(BF)
    hidden_low = grad_hidden.astype(BF)
    grad_mixed = dot("kd,ted->tke", hidden_low, w_out_all).astype(BF)
    hidden_cols = jnp.moveaxis(hidden_low.reshape(own_rows, tp_count, cols), 1, 0)
    mixed_own = lax.dynamic_slice_in_dim(mixed_all[..., :cols], tp_rank * own_rows, own_rows, 1)
    sent = to_all(jnp.concatenate([grad_mixed, mixed_own], axis=-1))
    later = jnp.concatenate([hidden_cols, grad_tiles], axis=-1)
    small = [gain2_part.reshape(tp_count, -1), shift2_part.reshape(tp_count, -1), small]
    small = jnp.concatenate(small, axis=1)
    sent, later, small = lax.optimization_barrier((sent, later, small))
    later = to_all(later).reshape(all_picks, cols + tile_cols)

    scene_sent = by_scene(sent)
    made, totals = [], []
    operands = (queries, patch_kv, plane_kv, scene_sent, logsum)
    operands += (
        patch_normed.reshape(scenes, patch_local, width),
        plane_normed.reshape(scenes, plane_local, width),
    )
    for n in range(scenes):
        if n == scenes - 1:
            operands, later, made = lax.optimization_barrier((operands, later, made))
        *one, part, sums = attend_back(n, *operands, totals, heads)
        made.append(one)
        totals = [part, sums]
    kv_sent = to_owner(
        jnp.concatenate(
            [
                jnp.concatenate([by_owner(one[1], own_patch), by_owner(one[2], own_plane)], axis=2)
                for one in made
            ],
            axis=1,
        )
    )
    grad_query = jnp.concatenate([one[0] for one in made], axis=0)
    kv_part, kv_sum = totals
    hidden_cols = later[:, :cols]
    hidden_late, early, made = lax.optimization_barrier((hidden_cols, early, made))
    hidden_cols_all = lax.all_gather(hidden_late, "tp", axis=0)
    grad_query = split_sum(by_seq(grad_query).reshape(all_picks, cols), "seq").astype(BF)
    grad_query, sent = lax.optimization_barrier((grad_query, sent))
    query_part = dot("rd,re->ed", normed_picks, grad_query)
    qkv_part = jnp.concatenate([kv_part, query_part], axis=0)
    size = width // seq_count

    def block_of(mask):
        return lax.dynamic_slice_in_dim(qkv_part, (seq_rank ^ mask) * size, size, 1)

    own_block = block_of(0)
    received = []
    for mask in range(1, seq_count):
        block = lax.ppermute(block_of(mask).astype(BF), "seq", xor_pairs(seq_count, mask))
        received.append(block)
    query_parts = [grad_query] + [
        lax.ppermute(grad_query, "seq", xor_pairs(seq_count, mask)) for mask in range(1, seq_count)
    ]
    query_sum = jnp.sum(grad_query.astype(F32), axis=0)
    sums = jnp.concatenate([kv_sum[0], query_sum])[:, None]
    wide = qkv_weight.astype(F32)
    shift1_part = jnp.sum(wide * sums, axis=0)
    product = jnp.sum(wide * qkv_part, axis=0)
    gain1_part = (product - norm1_bias * shift1_part) / norm1_gain

    up_grad, down_grad, out_grad, unpatch_grad, unpatch_bias_grad = weight_grads(
        early,
        w_up,
        w_down,
        sent.reshape(all_picks, 2 * cols)[:, cols:],
        hidden_cols_all,
        tp_first(later[:, cols:]),
    )
    query_parts, own_block, up_grad = lax.optimization_barrier((query_parts, own_block, up_grad))
    qkv_sum = (own_block + sum(block.astype(F32) for block in received)).astype(BF)
    scattered = scatter(
        seq_rank,
        row_ids.reshape(seq_count, 1, seq_picks),
        hidden_cols.reshape(seq_count, seq_picks, cols),
        query_parts,
        (tp_count, scenes, own_plane, 2 * cols),
    )

    unpatch_bias_grad = unpatch_bias_grad[0]

    scattered, kv_sent, up_grad, qkv_sum = lax.optimization_barrier(
        (scattered, kv_sent, up_grad, qkv_sum)
    )
    extra_sent = to_owner(scattered)
    qkv_parts = [qkv_sum] + [
        lax.ppermute(qkv_sum, "seq", xor_pairs(seq_count, mask)) for mask in range(1, seq_count)
    ]

    pieces = [gain1_part.reshape(tp_count, -1), shift1_part.reshape(tp_count, -1), small]
    pieces, _ = lax.optimization_barrier((jnp.concatenate(pieces, axis=1), extra_sent))
    pieces = jnp.sum(to_all(pieces), axis=0)
    sizes = [width // tp_count] * 4
    sizes += [w_dec1.shape[0] * dec1_cols, dec1_cols, dec1_cols * w_dec2.shape[1]]
    totals = []
    for count in sizes:
        totals.append(pieces[:count])
        pieces = pieces[count:]
    gain1_grad, shift1_grad, gain2_grad, shift2_grad = totals[:4]
    dec1_grad, dec1_bias_grad, dec2_grad = totals[4:]

    patch_grad, plane_grad = finish(
        kv_sent, extra_sent, qkv_all, patch_tokens, plane_tokens, norm1_gain, tp_rank, cols
    )
    qkv_parts, patch_grad = lax.optimization_barrier((qkv_parts, patch_grad))
    key_grad, value_grad, query_grad = turn(seq_rank, qkv_parts)
    return (
        colours,
        patch_grad,
        plane_grad,
        gain1_grad,
        shift1_grad,
        query_grad,
        key_grad,
        value_grad,
        out_grad,
        gain2_grad,
        shift2_grad,
        up_grad,
        down_grad,
        unpatch_grad,
        unpatch_bias_grad,
        dec1_grad.reshape(-1, dec1_cols),
        dec1_bias_grad,
        dec2_grad.reshape(-1, w_dec2.shape[1]),
    )


def solution(mesh):
    in_specs = (
        P(None, "seq", None),
        P(None, "seq", None),
        P(),
        P(),
        P(None, "tp"),
        P(None, "tp"),
        P(None, "tp"),
        P("tp", None),
        P(),
        P(),
        P(None, "tp"),
        P("tp", None),
        P(None, "tp"),
        P("tp"),
        P(),
        P(),
        P(),
        P(None, None, "seq"),
        P(None, "seq", None, "tp", None),
        P(),
        P(None, None, ("seq", "tp")),
    )
    out_specs = (
        P(None, None, ("seq", "tp")),
        P(None, ("seq", "tp"), None),
        P(None, ("seq", "tp"), None),
        P("tp"),
        P("tp"),
        P(None, "tp"),
        P(None, "tp"),
        P(None, "tp"),
        P("tp", None),
        P("tp"),
        P("tp"),
        P(None, "tp"),
        P("tp", None),
        P(None, "tp"),
        P("tp"),
        P(None, "tp"),
        P("tp"),
        P("tp", None),
    )
    return jax.shard_map(
        on_device, mesh=mesh, in_specs=in_specs, out_specs=out_specs, check_vma=False
    )
```

```python
import functools

import jax
import jax.numpy as jnp
from jax import lax
from jax.experimental import pallas as pl
from jax.experimental.pallas import tpu as pltpu
from jax.sharding import PartitionSpec as P

HEAD_DIM = 64
CH = 32
TRI_SIDE = 32
BF = jnp.bfloat16
F32 = jnp.float32
HIGH = lax.Precision.HIGHEST


def dot(spec, *operands):
    return jnp.einsum(spec, *operands, preferred_element_type=F32)


def standard_rows(token_rows):
    centre = jnp.mean(token_rows, axis=-1, keepdims=True)
    offset = token_rows - centre
    spread = jnp.mean(offset * offset, axis=-1, keepdims=True)
    scale = lax.rsqrt(spread + 1e-05)
    return offset * scale, scale


def norm_rows(token_rows, norm_gain, norm_shift):
    return standard_rows(token_rows)[0] * norm_gain + norm_shift


def norm_back(standard, scale, norm_gain, grad):
    scaled = grad * norm_gain
    first = jnp.mean(scaled, axis=-1, keepdims=True)
    second = jnp.mean(scaled * standard, axis=-1, keepdims=True)
    return scale * (scaled - first - standard * second)


def xor_pairs(size, mask):
    return [(i, i ^ mask) for i in range(size)]


def hyper_sum(value, axes):
    for axis in axes:
        size = lax.axis_size(axis)
        mask = 1
        while mask < size:
            value = value + lax.ppermute(value, axis, xor_pairs(size, mask))
            mask *= 2
    return value


def block_rows(rows, limit):
    best = rows
    for size in range(16, limit + 1, 16):
        if rows % size == 0:
            best = size
    return best


def params(size=60):
    return pltpu.CompilerParams(vmem_limit_bytes=size * 2**20)


def cost(flops, bytes_accessed, transcendentals=0):
    return pl.CostEstimate(
        flops=flops, bytes_accessed=bytes_accessed, transcendentals=transcendentals
    )


def project_kernel(weight_count, rows_ref, gain_ref, bias_ref, *refs):
    weights, (normed_ref, kv_ref, *query_refs) = refs[:weight_count], refs[weight_count:]
    rows = rows_ref[...].astype(F32)
    normed = norm_rows(rows, gain_ref[...], bias_ref[...]).astype(BF)
    normed_ref[...] = normed
    made = [jnp.dot(normed, w[...], preferred_element_type=F32).astype(BF) for w in weights]
    kv_ref[...] = jnp.concatenate(made[:2], axis=1)
    for ref, value in zip(query_refs, made[2:]):
        ref[...] = value


def project(token_rows, gain, bias, *weights):
    rows, width = token_rows.shape
    cols = weights[0].shape[1]
    block = block_rows(rows, 512)
    widths = [width, 2 * cols] + [cols] * (len(weights) - 2)
    whole = lambda i: (0, 0)
    mine = lambda i: (i, 0)
    return pl.pallas_call(
        functools.partial(project_kernel, len(weights)),
        grid=(rows // block,),
        in_specs=[
            pl.BlockSpec((block, width), mine),
            pl.BlockSpec((1, width), whole),
            pl.BlockSpec((1, width), whole),
        ]
        + [pl.BlockSpec((width, cols), whole) for _ in weights],
        out_specs=[pl.BlockSpec((block, w), mine) for w in widths],
        out_shape=[jax.ShapeDtypeStruct((rows, w), BF) for w in widths],
        compiler_params=params(),
        cost_estimate=cost(
            2 * rows * width * cols * len(weights), rows * (width + sum(widths)) * 2
        ),
        name="norm_project",
    )(token_rows, gain[None], bias[None], *weights)


def pieces_of(value):
    high = lax.reduce_precision(value, 8, 7)
    middle = lax.reduce_precision(value - high, 8, 7)
    return [high.astype(BF), middle.astype(BF), (value - high - middle).astype(BF)]


def dot_dims(left, right, left_dim, right_dim):
    dims = (((left_dim,), (right_dim,)), ((), ()))
    return lax.dot_general(left, right, dims, preferred_element_type=F32)


def attend_kernel(heads, q_ref, first_ref, second_ref, out_ref, logsum_ref):
    cols = heads * HEAD_DIM
    parts, stats = [], []
    for h in range(heads):
        here = slice(h * HEAD_DIM, (h + 1) * HEAD_DIM)
        there = slice(cols + h * HEAD_DIM, cols + (h + 1) * HEAD_DIM)
        query = q_ref[0, :, here] * BF(HEAD_DIM**-0.5)
        scores = [dot_dims(ref[0, :, here], query, 1, 1) for ref in (first_ref, second_ref)]
        top = jnp.maximum(*[jnp.max(s, axis=0, keepdims=True) for s in scores])
        raised = [jnp.exp(s - top) for s in scores]
        total = sum(jnp.sum(r, axis=0, keepdims=True) for r in raised)
        mixed = sum(
            dot_dims(ref[0, :, there], r.astype(BF), 0, 0)
            for ref, r in zip((first_ref, second_ref), raised)
        )
        parts.append(mixed / total)
        stats.append(top + jnp.log(total))
    out_ref[0] = jnp.concatenate(parts, axis=0).T.astype(BF)
    logsum_ref[0] = jnp.concatenate(stats, axis=0)


def attend(queries, first, second, heads):
    scenes, count, cols = queries.shape
    keys = first.shape[1] + second.shape[1]
    scene = lambda n: (n, 0, 0)
    return pl.pallas_call(
        functools.partial(attend_kernel, heads),
        grid=(scenes,),
        in_specs=[pl.BlockSpec((1,) + a.shape[1:], scene) for a in (queries, first, second)],
        out_specs=[
            pl.BlockSpec((1, count, cols), scene),
            pl.BlockSpec((1, heads, count), scene),
        ],
        out_shape=[
            jax.ShapeDtypeStruct((scenes, count, cols), BF),
            jax.ShapeDtypeStruct((scenes, heads, count), F32),
        ],
        compiler_params=params(44),
        cost_estimate=cost(
            scenes * heads * count * keys * 16 * HEAD_DIM * 2,
            scenes * keys * cols * 4,
            scenes * heads * count * keys,
        ),
        name="attend",
    )(queries, first, second)


def attend_back_kernel(heads, *refs):
    q_ref, first_ref, second_ref, grad_ref, logsum_ref, na_ref, nb_ref = refs[:7]
    gq_ref, ga_ref, gb_ref, part_ref, sum_ref = refs[-5:]
    if len(refs) > 12:
        part_ref[...] = refs[7][...]
        sum_ref[...] = refs[8][...]
    else:
        part_ref[...] = jnp.zeros_like(part_ref)
        sum_ref[...] = jnp.zeros_like(sum_ref)
    cols = heads * HEAD_DIM
    count = q_ref.shape[1]
    scale = HEAD_DIM**-0.5
    cut = [slice(h * HEAD_DIM, (h + 1) * HEAD_DIM) for h in range(heads)]
    query = [q_ref[0, :, c] * BF(scale) for c in cut]
    grad = [grad_ref[0, :, c] for c in cut]
    ones = jnp.ones((8, HEAD_DIM), F32)
    inner = [
        lax.dot_general(
            ones,
            grad_ref[0, :, cols + c.start : cols + c.stop].astype(F32) * g.astype(F32),
            (((1,), (1,)), ((), ())),
            precision=HIGH,
            preferred_element_type=F32,
        )[:1]
        for c, g in zip(cut, grad)
    ]
    totals = tuple(jnp.zeros((HEAD_DIM, count), F32) for _ in cut)
    for ref, out_ref, normed_ref in ((first_ref, ga_ref, na_ref), (second_ref, gb_ref, nb_ref)):
        rows = ref.shape[1]
        block = block_rows(rows, 512)

        def step(i, totals, ref=ref, out_ref=out_ref, normed_ref=normed_ref, block=block):
            place = pl.ds(pl.multiple_of(i * block, block), block)
            keys, grads, sums = [], [], []
            for h in range(heads):
                key = ref[0, place, cut[h]]
                value = ref[0, place, slice(cols + cut[h].start, cols + cut[h].stop)]
                shares = jnp.exp(dot_dims(key, query[h], 1, 1) - logsum_ref[0, h : h + 1, :])
                grad_shares = dot_dims(value, grad[h], 1, 1)
                grad_scores = (shares * (grad_shares - inner[h])).astype(BF)
                keys.append(jnp.dot(grad_scores, query[h], preferred_element_type=F32))
                grads.append(jnp.dot(shares.astype(BF), grad[h], preferred_element_type=F32))
                sums.append(totals[h] + dot_dims(key, grad_scores, 0, 0))
            made = jnp.concatenate(keys + grads, axis=1).astype(BF)
            out_ref[0, place, :] = made
            part_ref[...] += dot_dims(made, normed_ref[0, place, :], 0, 0)
            sum_ref[...] += jnp.sum(made.astype(F32), axis=0, keepdims=True)
            return tuple(sums)

        totals = lax.fori_loop(0, rows // block, step, totals, unroll=True)
    gq_ref[0] = (jnp.concatenate(totals, axis=0) * scale).T.astype(BF)


def attend_back(scene, queries, first, second, grad, logsum, normed_first, normed_second, before, heads):
    scenes, count, cols = queries.shape
    keys, width = first.shape[1] + second.shape[1], normed_first.shape[2]
    mine = lambda i: (scene, 0, 0)
    whole = lambda i: (0, 0)
    operands = (queries, first, second, grad, logsum, normed_first, normed_second)
    totals = [(2 * cols, width), (1, 2 * cols)]
    outs = [(1,) + a.shape[1:] for a in (queries, first, second)]
    return pl.pallas_call(
        functools.partial(attend_back_kernel, heads),
        grid=(1,),
        in_specs=[pl.BlockSpec((1,) + a.shape[1:], mine) for a in operands]
        + [pl.BlockSpec(a.shape, whole) for a in before],
        out_specs=[pl.BlockSpec(a, lambda i: (0, 0, 0)) for a in outs]
        + [pl.BlockSpec(a, whole) for a in totals],
        out_shape=[jax.ShapeDtypeStruct(a, BF) for a in outs]
        + [jax.ShapeDtypeStruct(a, F32) for a in totals],
        compiler_params=params(),
        cost_estimate=cost(
            heads * count * keys * 40 * HEAD_DIM * 2 + 4 * keys * cols * width,
            keys * (cols * 8 + width * 2),
            heads * count * keys,
        ),
        name="attend_back",
    )(*operands, *before)


def finish_kernel(cols, rank_ref, kv_ref, extra_ref, weight_ref, gain_ref, patch_ref, plane_ref, *outs):
    own_patch = patch_ref.shape[2]
    parts = kv_ref.shape[0]
    total = sum(dot_dims(kv_ref[t, 0], weight_ref[t, : 2 * cols], 1, 0) for t in range(parts))
    more = sum(
        dot_dims(extra_ref[t, 0, :, :cols], weight_ref[t, 2 * cols :], 1, 0)
        for t in range(parts)
    )
    grads = (total[:own_patch], total[own_patch:] + more)
    extra = jnp.concatenate([extra_ref[t, 0, :, cols:] for t in range(parts)], axis=1)
    added = (0.0, extra.astype(F32))
    for ref, out_ref, grad, plus in zip((patch_ref, plane_ref), outs, grads, added):
        standard, scale = standard_rows(ref[0, 0].astype(F32))
        out_ref[0] = norm_back(standard, scale, gain_ref[...], grad) + plus


def finish(kv_sent, extra_sent, weights, patch_rows, plane_rows, gain, rank, cols):
    parts, scenes, rows, _ = kv_sent.shape
    width = weights.shape[2]
    tokens = [a.reshape(scenes, parts, -1, width) for a in (patch_rows, plane_rows)]
    by_part = lambda n, rank: (0, n, 0, 0)
    spec = pltpu.PrefetchScalarGridSpec(
        num_scalar_prefetch=1,
        grid=(scenes,),
        in_specs=[
            pl.BlockSpec((parts, 1) + kv_sent.shape[2:], by_part),
            pl.BlockSpec((parts, 1) + extra_sent.shape[2:], by_part),
            pl.BlockSpec(weights.shape, lambda n, rank: (0, 0, 0)),
            pl.BlockSpec((1, width), lambda n, rank: (0, 0)),
        ]
        + [pl.BlockSpec((1, 1) + a.shape[2:], lambda n, rank: (n, rank[0], 0, 0)) for a in tokens],
        out_specs=[pl.BlockSpec((1,) + a.shape[2:], lambda n, rank: (n, 0, 0)) for a in tokens],
    )
    return pl.pallas_call(
        functools.partial(finish_kernel, cols),
        grid_spec=spec,
        out_shape=[jax.ShapeDtypeStruct((scenes,) + a.shape[2:], F32) for a in tokens],
        compiler_params=params(),
        cost_estimate=cost(
            scenes * rows * width * parts * 3 * cols * 2, weights.size * 2 + rows * width * 16
        ),
        name="finish",
    )(rank.reshape(1), kv_sent, extra_sent, weights, gain[None], *tokens)


def turn_kernel(rank_ref, *refs):
    parts, outs = refs[:-3], refs[-3:]
    cols, size = outs[0].shape[1], parts[0].shape[1]
    for mask, part in enumerate(parts):
        place = pl.ds(pl.multiple_of((rank_ref[0] ^ mask) * size, size), size)
        for k, ref in enumerate(outs):
            ref[place, :] = part[k * cols : (k + 1) * cols].astype(F32).T


def turn(rank, parts):
    rows, width = parts[0].shape[0], parts[0].shape[1] * len(parts)
    whole = lambda i, r: (0, 0)
    spec = pltpu.PrefetchScalarGridSpec(
        num_scalar_prefetch=1,
        grid=(1,),
        in_specs=[pl.BlockSpec(a.shape, whole) for a in parts],
        out_specs=[pl.BlockSpec((width, rows // 3), whole)] * 3,
    )
    return pl.pallas_call(
        turn_kernel,
        grid_spec=spec,
        out_shape=[jax.ShapeDtypeStruct((width, rows // 3), F32)] * 3,
        compiler_params=params(),
        cost_estimate=cost(1, 1),
        name="turn",
    )(rank.reshape(1), *parts)


def gelu_parts(value):
    slope = 0.7978845608028654
    square = value * value
    bent = jnp.tanh(slope * value * (1.0 + 0.044715 * square))
    half = 0.5 * (1.0 + bent)
    rise = 0.5 * value * (1.0 - bent * bent) * (slope * (1.0 + 0.134145 * square))
    return value * half, half + rise


def weights_kernel(width, rows_ref, up_ref, down_ref, mixed_ref, hidden_ref, tile_ref, *outs):
    up_out, down_out, mix_out, tile_out, sum_out = outs
    unit_step, pick_step = pl.program_id(0), pl.program_id(1)
    normed, result, grad_result = [rows_ref[:, k * width : (k + 1) * width] for k in range(3)]

    @pl.when(pick_step == 0)
    def _():
        up_out[...] = jnp.zeros_like(up_out)
        down_out[...] = jnp.zeros_like(down_out)

    @pl.when((pick_step == 0) & (unit_step == 0))
    def _():
        mix_out[...] = jnp.zeros_like(mix_out)
        tile_out[...] = jnp.zeros_like(tile_out)
        sum_out[...] = jnp.zeros_like(sum_out)

    preact = jnp.dot(normed, up_ref[...], preferred_element_type=F32)
    active, slope = gelu_parts(preact)
    down_out[...] += dot_dims(active.astype(BF), grad_result, 0, 0)
    grad = (dot_dims(grad_result, down_ref[...], 1, 1) * slope).astype(BF)
    up_out[...] += dot_dims(normed, grad, 0, 0)

    @pl.when(unit_step == 0)
    def _():
        parts = [dot_dims(mixed_ref[...], hidden_ref[t], 0, 0) for t in range(hidden_ref.shape[0])]
        mix_out[...] += jnp.concatenate(parts, axis=1)
        tile_out[...] += dot_dims(result, tile_ref[...], 0, 0)
        sum_out[...] += jnp.sum(tile_ref[...].astype(F32), axis=0, keepdims=True)


def weight_grads(rows, w_up, w_down, mixed, hidden, tiles):
    picks, width = rows.shape[0], rows.shape[1] // 3
    units, cols, tile_cols = w_up.shape[1], mixed.shape[1], tiles.shape[1]
    block, units_block = block_rows(picks, 768), block_rows(units, 512)
    here = lambda g, p: (p, 0)
    whole = lambda g, p: (0, 0)
    return pl.pallas_call(
        functools.partial(weights_kernel, width),
        grid=(units // units_block, picks // block),
        in_specs=[
            pl.BlockSpec((block, 3 * width), here),
            pl.BlockSpec((width, units_block), lambda g, p: (0, g)),
            pl.BlockSpec((units_block, width), lambda g, p: (g, 0)),
            pl.BlockSpec((block, cols), here),
            pl.BlockSpec((hidden.shape[0], block, cols), lambda g, p: (0, p, 0)),
            pl.BlockSpec((block, tile_cols), here),
        ],
        out_specs=[
            pl.BlockSpec((width, units_block), lambda g, p: (0, g)),
            pl.BlockSpec((units_block, width), lambda g, p: (g, 0)),
            pl.BlockSpec((cols, width), whole),
            pl.BlockSpec((width, tile_cols), whole),
            pl.BlockSpec((1, tile_cols), whole),
        ],
        out_shape=[
            jax.ShapeDtypeStruct(shape, F32)
            for shape in (
                (width, units),
                (units, width),
                (cols, width),
                (width, tile_cols),
                (1, tile_cols),
            )
        ],
        compiler_params=params(),
        cost_estimate=cost(
            2 * picks * width * (4 * units + cols + tile_cols),
            rows.size * 2 + width * units * 12,
            picks * units,
        ),
        name="weight_grads",
    )(rows, w_up, w_down, mixed, hidden, tiles)


def scatter_kernel(scenes, own, rank_ref, ids_ref, hidden_ref, *refs):
    parts, out_ref = refs[:-1], refs[-1]
    rank = rank_ref[0]
    seq_picks = parts[0].shape[0]
    values = [
        jnp.concatenate([part[...], hidden_ref[rank ^ m]], axis=1) for m, part in enumerate(parts)
    ]
    row = lax.broadcasted_iota(jnp.int32, (own, seq_picks), 0)
    blocks = out_ref.shape[0]

    def step(t, carry):
        for n in range(scenes):
            first = (n * blocks + t) * own
            total = sum(
                jnp.dot(
                    (row + first == ids_ref[rank ^ m]).astype(F32).astype(BF),
                    value,
                    preferred_element_type=F32,
                )
                for m, value in enumerate(values)
            )
            out_ref[t, n] = total.astype(BF)
        return carry

    lax.fori_loop(0, blocks, step, 0)


def scatter(rank, ids, hidden, parts, shape):
    spec = pltpu.PrefetchScalarGridSpec(
        num_scalar_prefetch=1,
        grid=(1,),
        in_specs=[
            pl.BlockSpec(a.shape, lambda i, r, k=a.ndim: (0,) * k) for a in (ids, hidden, *parts)
        ],
        out_specs=pl.BlockSpec(shape, lambda i, r: (0, 0, 0, 0)),
    )
    return pl.pallas_call(
        functools.partial(scatter_kernel, shape[1], shape[2]),
        grid_spec=spec,
        out_shape=jax.ShapeDtypeStruct(shape, BF),
        compiler_params=params(),
        cost_estimate=cost(2 * shape[0] * shape[1] * shape[2] * shape[3] * ids.size, hidden.size * 8),
        name="scatter",
    )(rank.reshape(1), ids, hidden, *parts)


def spread(value, axis):
    size, rank = lax.axis_size(axis), lax.axis_index(axis)
    out = jnp.zeros((size,) + value.shape, value.dtype)
    for mask in range(size):
        other = lax.ppermute(value, axis, xor_pairs(size, mask)) if mask else value
        out = lax.dynamic_update_index_in_dim(out, other, rank ^ mask, 0)
    return out


def split_sum(value, axis):
    size, rank = lax.axis_size(axis), lax.axis_index(axis)
    value = value.reshape((size, value.shape[0] // size) + value.shape[1:])
    total = lax.dynamic_index_in_dim(value, rank, 0, keepdims=False)
    for mask in range(1, size):
        block = lax.dynamic_index_in_dim(value, rank ^ mask, 0, keepdims=False).astype(BF)
        total = total + lax.ppermute(block, axis, xor_pairs(size, mask)).astype(F32)
    return total


def dot_high(left, right, left_dim, right_dim):
    dims = (((left_dim,), (right_dim,)), ((), ()))
    return lax.dot_general(left, right, dims, precision=HIGH, preferred_element_type=F32)


def render_kernel(*refs):
    came_ref, hidden_ref, unpatch_ref, shift_ref, corner_ref, select_ref = refs[:6]
    w1_ref, b1_ref, w2_ref, live_ref, cotangent_ref = refs[6:11]
    (result_ref, colour_ref, tiles_ref, grad_ref, low_ref, g1_ref, gb_ref, g2_ref) = refs[11:]
    parts, rows, _ = came_ref.shape
    rays, _, samples = corner_ref.shape
    result = hidden_ref[...] + sum(came_ref[t].astype(F32) for t in range(parts))
    result = result.astype(BF)
    result_ref[...] = result
    tiles = [
        (jnp.dot(result, unpatch_ref[t], preferred_element_type=F32) + shift_ref[t]).astype(BF)
        for t in range(parts)
    ]
    tiles = jnp.concatenate(tiles, axis=0)
    lines, tile_cols = corner_ref.shape[1], tiles.shape[1]

    def place(shape, dim):
        return lax.broadcasted_iota(jnp.int32, shape, dim)

    pixel_mask = tile_cols // CH - 1
    pixel = place((lines, tile_cols), 1) >> (CH.bit_length() - 1)
    pixel = (pixel == (place((lines, tile_cols), 0) & pixel_mask)).astype(F32)
    pick_out = (place((CH, tile_cols), 1) & (CH - 1)) == place((CH, tile_cols), 0)
    pick_out = pick_out.astype(F32).astype(BF)
    units = b1_ref.shape[1]
    bias = jnp.where(place((units, units), 0) == place((units, units), 1), b1_ref[...], 0.0)
    bias = jnp.sum(bias, axis=1, keepdims=True)
    features = []
    for r in range(rays):
        mine = jnp.dot(select_ref[r], tiles, preferred_element_type=F32) * pixel
        mine = dot_dims(mine.astype(BF), pick_out, 1, 1).astype(BF)
        features.append(dot_dims(mine, corner_ref[r], 0, 0))
    features = jnp.concatenate(features, axis=1)
    preact = dot_high(w1_ref[...], features, 0, 0) + bias
    gate = 1.0 / (1.0 + jnp.exp(-preact))
    hidden = preact * gate
    output = dot_high(w2_ref[...], hidden, 0, 0)

    def by_ray(row):
        return jnp.concatenate(
            [row[:, r * samples : (r + 1) * samples] for r in range(rays)], axis=0
        )

    def in_row(value):
        return jnp.concatenate([value[r : r + 1] for r in range(rays)], axis=1)

    first = by_ray(output[0:1])
    density = jnp.maximum(first, 0.0) + jnp.log1p(jnp.exp(-jnp.abs(first)))
    shades = [1.0 / (1.0 + jnp.exp(-by_ray(output[k : k + 1]))) for k in (1, 2, 3)]
    optical = density * (2.0 / samples)
    before = (
        lax.broadcasted_iota(jnp.int32, (samples, samples), 0)
        < lax.broadcasted_iota(jnp.int32, (samples, samples), 1)
    ).astype(F32)
    through = jnp.exp(-dot_high(optical, before, 1, 0))
    kept = jnp.exp(-optical)
    weight = through * (1.0 - kept)
    live = live_ref[...]
    colour_ref[...] = jnp.concatenate(
        [jnp.sum(weight * shade, axis=1, keepdims=True) * live for shade in shades], axis=1
    )
    grads = [cotangent_ref[:, k : k + 1] * live for k in range(3)]
    grad_weight = sum(g * shade for g, shade in zip(grads, shades))
    grad_before = -through * grad_weight * (1.0 - kept)
    grad_optical = dot_high(grad_before, before, 1, 1) + grad_weight * through * kept
    grad_first = grad_optical * (2.0 / samples) * (1.0 / (1.0 + jnp.exp(-first)))
    grad_shades = [g * weight * shade * (1.0 - shade) for g, shade in zip(grads, shades)]
    grad_output = jnp.concatenate([in_row(g) for g in [grad_first] + grad_shades], axis=0)
    grad_preact = jnp.dot(w2_ref[...], grad_output, precision=HIGH, preferred_element_type=F32)
    grad_preact = grad_preact * (gate * (1.0 + preact * (1.0 - gate)))
    g2_ref[...] = dot_high(hidden, grad_output, 1, 1)
    gb_ref[...] = jnp.sum(grad_preact, axis=1, keepdims=True)
    g1_ref[...] = dot_high(features, grad_preact, 1, 1)
    grad_features = jnp.dot(w1_ref[...], grad_preact, precision=HIGH, preferred_element_type=F32)
    total = jnp.zeros(tiles.shape, F32)
    for r in range(rays):
        mine = grad_features[:, r * samples : (r + 1) * samples]
        high = mine.astype(BF)
        low = (mine - high.astype(F32)).astype(BF)
        corner = corner_ref[r]
        mine = (dot_dims(corner, high, 1, 1) + dot_dims(corner, low, 1, 1)).astype(BF)
        mine = jnp.dot(mine, pick_out, preferred_element_type=F32) * pixel
        total = total + dot_dims(select_ref[r], mine.astype(BF), 0, 0)
    grad = jnp.zeros(grad_ref.shape, F32)
    for t in range(parts):
        mine = total[t * rows : (t + 1) * rows].astype(BF)
        tiles_ref[t] = mine
        grad = grad + dot_dims(mine, unpatch_ref[t], 1, 1)
    grad_ref[...] = grad
    low_ref[...] = grad.astype(BF)


def render(came, hidden_own, unpatch, shift, corners, w1, b1, w2, live, cotangent):
    parts, rows, width = came.shape
    scenes, rays, tile_cols = corners.shape[1], corners.shape[2], unpatch.shape[2]
    pixels, samples = corners.shape[4], corners.shape[5]
    corners = jnp.transpose(corners, (1, 2, 0, 3, 4, 5))
    corners = corners.reshape(scenes * rays, parts * 3 * pixels, samples)
    ray = jnp.arange(scenes * rays)[:, None, None]
    line = jnp.arange(parts * 3 * pixels)[None, :, None]
    source = (line // (3 * pixels)) * rows + (line // pixels) % 3 * rays
    source = source + (ray // rays) * (3 * rays) + ray % rays
    select = (source == jnp.arange(parts * rows)[None, None, :]).astype(BF)
    hidden_units = w1.shape[1]
    operands = (came, hidden_own, unpatch, shift[:, None], corners, select)
    operands += (w1, b1[None], w2, live, cotangent)
    outs = [
        ((rows, width), BF),
        (cotangent.shape, F32),
        ((parts, rows, tile_cols), BF),
        ((rows, width), F32),
        ((rows, width), BF),
        (w1.shape, F32),
        ((hidden_units, 1), F32),
        (w2.shape, F32),
    ]
    return pl.pallas_call(
        render_kernel,
        out_shape=[jax.ShapeDtypeStruct(shape, kind) for shape, kind in outs],
        compiler_params=params(32),
        cost_estimate=cost(8 * rows * width * tile_cols * parts, unpatch.size * 2, 0),
        name="render",
    )(*operands)


def on_device(
    patch_tokens,
    plane_tokens,
    norm1_gain,
    norm1_bias,
    w_query,
    w_key,
    w_value,
    w_out,
    norm2_gain,
    norm2_bias,
    w_up,
    w_down,
    w_unpatch,
    b_unpatch,
    w_dec1,
    b_dec1,
    w_dec2,
    tile_index,
    corner_weights,
    ray_count,
    color_grad,
):
    scenes, patch_local, width = patch_tokens.shape
    plane_local = plane_tokens.shape[1]
    seq_count, tp_count = lax.axis_size("seq"), lax.axis_size("tp")
    seq_rank, tp_rank = lax.axis_index("seq"), lax.axis_index("tp")
    own_patch = patch_local // tp_count
    own_plane = plane_local // tp_count
    cols = w_query.shape[1]
    heads = cols // HEAD_DIM
    ray_seq = tile_index.shape[2]
    rays = ray_seq // tp_count
    picks = 3 * rays
    seq_picks = tp_count * scenes * picks
    all_picks = seq_count * seq_picks
    score_scale = HEAD_DIM**-0.5

    base = (jnp.arange(3, dtype=jnp.int32) * (TRI_SIDE * TRI_SIDE))[None, :, None]
    ids = (tile_index + base).reshape(scenes, 3, tp_count, rays)
    ids = jnp.transpose(ids, (2, 0, 1, 3)).reshape(tp_count, scenes, picks)
    ids = jnp.broadcast_to(ids[None], (seq_count,) + ids.shape)
    ids = lax.all_to_all(ids, "seq", 0, 0, tiled=True)
    plane_normed, plane_kv, query_rows = project(
        plane_tokens.reshape(-1, width), norm1_gain, norm1_bias, w_key, w_value, w_query
    )
    ids, query_rows = lax.optimization_barrier((ids, query_rows))
    local_ids = ids - seq_rank * plane_local
    inside = (local_ids >= 0) & (local_ids < plane_local)
    scene_base = (jnp.arange(scenes, dtype=jnp.int32) * plane_local)[None, None, :, None]
    row_ids = jnp.where(inside, local_ids + scene_base, -1).reshape(all_picks)
    onehot = (
        row_ids[:, None] == jnp.arange(scenes * plane_local, dtype=jnp.int32)[None, :]
    ).astype(BF)

    own_cols = lax.dynamic_slice_in_dim(plane_tokens, tp_rank * cols, cols, 2)
    chosen = jnp.dot(onehot, jnp.concatenate([query_rows, own_cols.reshape(-1, cols)], axis=1))
    chosen, corner_weights, w_key_later, patch_tokens = lax.optimization_barrier(
        (chosen, corner_weights, w_key, patch_tokens)
    )
    chosen = split_sum(chosen, "seq").astype(BF)
    chosen, patch_tokens = lax.optimization_barrier((chosen, patch_tokens))
    queries = spread(chosen[:, :cols], "seq").reshape(all_picks, cols)
    picked_cols = chosen[:, cols:]

    w_out_all = lax.all_gather(w_out, "tp", axis=0)
    unpatch_all = lax.all_gather(w_unpatch, "tp", axis=0)
    qkv_weight = jnp.concatenate([w_key_later.T, w_value.T, w_query.T], axis=0)
    qkv_all = lax.all_gather(qkv_weight, "tp", axis=0)

    corners = corner_weights.reshape(
        scenes, tp_count, rays, 3, corner_weights.shape[3], corner_weights.shape[4]
    )
    corners = lax.all_to_all(jnp.moveaxis(corners, 1, 0), "tp", 0, 0, tiled=True)

    patch_normed, patch_kv = project(
        patch_tokens.reshape(-1, width), norm1_gain, norm1_bias, w_key, w_value
    )
    queries, corners, patch_kv, picked_cols, w_out_all = lax.optimization_barrier(
        (queries, corners, patch_kv, picked_cols, w_out_all)
    )
    plane_kv = plane_kv.reshape(scenes, plane_local, 2 * cols)
    patch_kv = patch_kv.reshape(scenes, patch_local, 2 * cols)

    def by_scene(value):
        value = value.reshape(seq_count, tp_count, scenes, picks, -1)
        return jnp.moveaxis(value, 2, 0).reshape(scenes, seq_count * tp_count * picks, -1)

    def by_seq(value):
        value = value.reshape(scenes, seq_count, tp_count, picks, -1)
        return jnp.moveaxis(value, 0, 2).reshape(seq_count, seq_picks, -1)

    def in_heads(value):
        return value.reshape(value.shape[:-1] + (heads, HEAD_DIM))

    queries = by_scene(queries)
    part, logsum = attend(queries, patch_kv, plane_kv, heads)
    part = by_seq(part)
    flat = jnp.stack(pieces_of(logsum)).reshape(-1)
    stat_rows = -(-flat.shape[0] // (16 * cols)) * 16
    flat = jnp.pad(flat, (0, stat_rows * cols - flat.shape[0])).reshape(stat_rows, cols)
    flat = jnp.broadcast_to(flat[None], (seq_count, stat_rows, cols))
    part = lax.all_to_all(jnp.concatenate([part, flat], axis=1), "seq", 0, 0, tiled=True)
    logsums = part[:, seq_picks:].reshape(seq_count, -1)[:, : 3 * logsum.size]
    logsums = jnp.sum(logsums.reshape((seq_count, 3) + logsum.shape).astype(F32), axis=1)
    top = jnp.max(logsums, axis=0)
    logsum = top + jnp.log(jnp.sum(jnp.exp(logsums - top), axis=0))
    shares = jnp.exp(logsums - logsum)
    shares = shares.reshape(seq_count, scenes, heads, seq_count, tp_count, picks)
    shares = lax.dynamic_index_in_dim(shares, seq_rank, 3, keepdims=False)
    shares = jnp.transpose(shares, (0, 3, 1, 4, 2)).reshape(seq_count, seq_picks, heads, 1)
    mixed_low = jnp.sum(in_heads(part[:, :seq_picks].astype(F32)) * shares, axis=0)
    mixed_low = mixed_low.reshape(seq_picks, cols).astype(BF)

    bias_rows = jnp.stack(pieces_of(b_unpatch) + [jnp.zeros_like(b_unpatch, BF)] * 13)
    mixed_low = jnp.concatenate([mixed_low, picked_cols], axis=1)
    mixed_low = jnp.concatenate([mixed_low, bias_rows], axis=0)
    mixed_all = lax.all_gather(mixed_low, "tp", axis=0)
    bias_all = jnp.sum(mixed_all[:, seq_picks : seq_picks + 3].astype(F32), axis=1)
    mixed_all, unpatch_all = lax.optimization_barrier((mixed_all[:, :seq_picks], unpatch_all))
    branch = dot("tre,ted->rd", mixed_all[..., :cols], w_out_all)
    picked_rows = jnp.moveaxis(mixed_all[..., cols:], 0, 1).reshape(seq_picks, width)
    picked_rows = picked_rows.astype(F32)
    hidden_state = picked_rows + branch
    normed2 = norm_rows(hidden_state, norm2_gain, norm2_bias).astype(BF)
    preact = jnp.dot(normed2, w_up, preferred_element_type=F32)
    active = jax.nn.gelu(preact).astype(BF)
    down = jnp.dot(active, w_down, preferred_element_type=F32).astype(BF)
    own_rows = scenes * picks

    def to_all(value):
        value = jnp.broadcast_to(value[None], (seq_count,) + value.shape)
        value = value.reshape((seq_count * tp_count,) + value.shape[2:])
        return lax.all_to_all(value, ("seq", "tp"), 0, 0, tiled=True)

    def tp_first(value):
        value = value.reshape((seq_count, tp_count, own_rows) + value.shape[1:])
        return jnp.moveaxis(value, 1, 0).reshape((all_picks,) + value.shape[3:])

    def to_own(value):
        return lax.all_to_all(value.reshape(tp_count, own_rows, width), "tp", 0, 0, tiled=True)

    hidden_own = lax.dynamic_slice_in_dim(hidden_state, tp_rank * own_rows, own_rows, 0)
    normed2_own = lax.dynamic_slice_in_dim(normed2, tp_rank * own_rows, own_rows, 0)
    tile_cols = w_unpatch.shape[1]
    first_ray = (seq_rank * tp_count + tp_rank) * rays
    live_rays = (
        (first_ray + jnp.arange(rays, dtype=jnp.int32))[None, :] < ray_count[:, None]
    ).astype(F32)
    (
        result_own,
        colours,
        grad_tiles,
        grad_result,
        grad_result_low,
        dec1_part,
        dec1_bias_part,
        dec2_part,
    ) = render(
        to_own(down),
        hidden_own,
        unpatch_all,
        bias_all,
        corners,
        w_dec1,
        b_dec1,
        w_dec2,
        live_rays.reshape(-1, 1),
        jnp.moveaxis(color_grad, 1, -1).reshape(-1, 3),
    )
    colours = colours.reshape(scenes, rays, 3)
    result_rows = lax.all_gather(grad_result_low, "tp", axis=0, tiled=True)
    early = jnp.concatenate([normed2_own, result_own, grad_result_low], axis=1)
    early, result_rows = lax.optimization_barrier((early, result_rows))
    early = spread(early, "seq").reshape(-1, 3 * width)
    grad_active = dot("rd,fd->rf", result_rows, w_down)
    grad_preact = jax.vjp(jax.nn.gelu, preact)[1](grad_active)[0].astype(BF)
    grad_normed2 = dot("rf,df->rd", grad_preact, w_up).astype(BF)
    grad_normed2, qkv_all = lax.optimization_barrier((grad_normed2, qkv_all))
    dec1_cols = w_dec1.shape[1] // tp_count
    dec1_part = jnp.moveaxis(dec1_part.reshape(-1, tp_count, dec1_cols), 1, 0)
    small = [dec1_part, dec1_bias_part, dec2_part]
    small = jnp.concatenate([piece.reshape(tp_count, -1) for piece in small], axis=1)
    colours = jnp.moveaxis(colours, -1, 1)
    grad_normed2, small, colours, early = lax.optimization_barrier(
        (to_own(grad_normed2), small, colours, early)
    )
    early = lax.all_gather(early, "tp", axis=0, tiled=True)
    grad_normed2 = jnp.sum(grad_normed2.astype(F32), axis=0)
    standard2, scale2 = standard_rows(hidden_own)
    gain2_part = jnp.sum(grad_normed2 * standard2, axis=0)
    shift2_part = jnp.sum(grad_normed2, axis=0)
    grad_hidden = grad_result + norm_back(standard2, scale2, norm2_gain, grad_normed2)
    def to_owner(value):
        return lax.all_to_all(value, "tp", 0, 0, tiled=True)

    def by_owner(value, own):
        value = value.reshape(-1, tp_count, own, value.shape[-1])
        return jnp.moveaxis(value, 1, 0)

    normed_picks = norm_rows(picked_rows, norm1_gain, norm1_bias).astype(BF)
    hidden_low = grad_hidden.astype(BF)
    grad_mixed = dot("kd,ted->tke", hidden_low, w_out_all).astype(BF)
    hidden_cols = jnp.moveaxis(hidden_low.reshape(own_rows, tp_count, cols), 1, 0)
    mixed_own = lax.dynamic_slice_in_dim(mixed_all[..., :cols], tp_rank * own_rows, own_rows, 1)
    sent = to_all(jnp.concatenate([grad_mixed, mixed_own], axis=-1))
    later = jnp.concatenate([hidden_cols, grad_tiles], axis=-1)
    small = [gain2_part.reshape(tp_count, -1), shift2_part.reshape(tp_count, -1), small]
    small = jnp.concatenate(small, axis=1)
    sent, later, small = lax.optimization_barrier((sent, later, small))
    later = to_all(later).reshape(all_picks, cols + tile_cols)

    scene_sent = by_scene(sent)
    made, totals = [], []
    operands = (queries, patch_kv, plane_kv, scene_sent, logsum)
    operands += (
        patch_normed.reshape(scenes, patch_local, width),
        plane_normed.reshape(scenes, plane_local, width),
    )
    for n in range(scenes):
        if n == scenes - 1:
            operands, later, made = lax.optimization_barrier((operands, later, made))
        *one, part, sums = attend_back(n, *operands, totals, heads)
        made.append(one)
        totals = [part, sums]
    kv_sent = to_owner(
        jnp.concatenate(
            [
                jnp.concatenate([by_owner(one[1], own_patch), by_owner(one[2], own_plane)], axis=2)
                for one in made
            ],
            axis=1,
        )
    )
    grad_query = jnp.concatenate([one[0] for one in made], axis=0)
    kv_part, kv_sum = totals
    hidden_cols = later[:, :cols]
    hidden_late, early, made = lax.optimization_barrier((hidden_cols, early, made))
    hidden_cols_all = lax.all_gather(hidden_late, "tp", axis=0)
    grad_query = split_sum(by_seq(grad_query).reshape(all_picks, cols), "seq").astype(BF)
    grad_query, sent = lax.optimization_barrier((grad_query, sent))
    query_part = dot("rd,re->ed", normed_picks, grad_query)
    qkv_part = jnp.concatenate([kv_part, query_part], axis=0)
    size = width // seq_count

    def block_of(mask):
        return lax.dynamic_slice_in_dim(qkv_part, (seq_rank ^ mask) * size, size, 1)

    own_block = block_of(0)
    received = []
    for mask in range(1, seq_count):
        block = lax.ppermute(block_of(mask).astype(BF), "seq", xor_pairs(seq_count, mask))
        received.append(block)
    query_parts = [grad_query] + [
        lax.ppermute(grad_query, "seq", xor_pairs(seq_count, mask)) for mask in range(1, seq_count)
    ]
    query_sum = jnp.sum(grad_query.astype(F32), axis=0)
    sums = jnp.concatenate([kv_sum[0], query_sum])[:, None]
    wide = qkv_weight.astype(F32)
    shift1_part = jnp.sum(wide * sums, axis=0)
    product = jnp.sum(wide * qkv_part, axis=0)
    gain1_part = (product - norm1_bias * shift1_part) / norm1_gain

    up_grad, down_grad, out_grad, unpatch_grad, unpatch_bias_grad = weight_grads(
        early,
        w_up,
        w_down,
        sent.reshape(all_picks, 2 * cols)[:, cols:],
        hidden_cols_all,
        tp_first(later[:, cols:]),
    )
    query_parts, own_block, up_grad = lax.optimization_barrier((query_parts, own_block, up_grad))
    qkv_sum = (own_block + sum(block.astype(F32) for block in received)).astype(BF)
    scattered = scatter(
        seq_rank,
        row_ids.reshape(seq_count, 1, seq_picks),
        hidden_cols.reshape(seq_count, seq_picks, cols),
        query_parts,
        (tp_count, scenes, own_plane, 2 * cols),
    )

    unpatch_bias_grad = unpatch_bias_grad[0]

    scattered, kv_sent, up_grad, qkv_sum = lax.optimization_barrier(
        (scattered, kv_sent, up_grad, qkv_sum)
    )
    extra_sent = to_owner(scattered)
    qkv_parts = [qkv_sum] + [
        lax.ppermute(qkv_sum, "seq", xor_pairs(seq_count, mask)) for mask in range(1, seq_count)
    ]

    pieces = [gain1_part.reshape(tp_count, -1), shift1_part.reshape(tp_count, -1), small]
    pieces, _ = lax.optimization_barrier((jnp.concatenate(pieces, axis=1), extra_sent))
    pieces = jnp.sum(to_all(pieces), axis=0)
    sizes = [width // tp_count] * 4
    sizes += [w_dec1.shape[0] * dec1_cols, dec1_cols, dec1_cols * w_dec2.shape[1]]
    totals = []
    for count in sizes:
        totals.append(pieces[:count])
        pieces = pieces[count:]
    gain1_grad, shift1_grad, gain2_grad, shift2_grad = totals[:4]
    dec1_grad, dec1_bias_grad, dec2_grad = totals[4:]

    patch_grad, plane_grad = finish(
        kv_sent, extra_sent, qkv_all, patch_tokens, plane_tokens, norm1_gain, tp_rank, cols
    )
    qkv_parts, patch_grad = lax.optimization_barrier((qkv_parts, patch_grad))
    key_grad, value_grad, query_grad = turn(seq_rank, qkv_parts)
    return (
        colours,
        patch_grad,
        plane_grad,
        gain1_grad,
        shift1_grad,
        query_grad,
        key_grad,
        value_grad,
        out_grad,
        gain2_grad,
        shift2_grad,
        up_grad,
        down_grad,
        unpatch_grad,
        unpatch_bias_grad,
        dec1_grad.reshape(-1, dec1_cols),
        dec1_bias_grad,
        dec2_grad.reshape(-1, w_dec2.shape[1]),
    )


def solution(mesh):
    in_specs = (
        P(None, "seq", None),
        P(None, "seq", None),
        P(),
        P(),
        P(None, "tp"),
        P(None, "tp"),
        P(None, "tp"),
        P("tp", None),
        P(),
        P(),
        P(None, "tp"),
        P("tp", None),
        P(None, "tp"),
        P("tp"),
        P(),
        P(),
        P(),
        P(None, None, "seq"),
        P(None, "seq", None, "tp", None),
        P(),
        P(None, None, ("seq", "tp")),
    )
    out_specs = (
        P(None, None, ("seq", "tp")),
        P(None, ("seq", "tp"), None),
        P(None, ("seq", "tp"), None),
        P("tp"),
        P("tp"),
        P(None, "tp"),
        P(None, "tp"),
        P(None, "tp"),
        P("tp", None),
        P("tp"),
        P("tp"),
        P(None, "tp"),
        P("tp", None),
        P(None, "tp"),
        P("tp"),
        P(None, "tp"),
        P("tp"),
        P("tp", None),
    )
    return jax.shard_map(
        on_device, mesh=mesh, in_specs=in_specs, out_specs=out_specs, check_vma=False
    )
```

```python
import functools

import jax
import jax.numpy as jnp
from jax import lax
from jax.experimental import pallas as pl
from jax.experimental.pallas import tpu as pltpu
from jax.sharding import PartitionSpec as P

HEAD_DIM = 64
CH = 32
TRI_SIDE = 32
BF = jnp.bfloat16
F32 = jnp.float32
HIGH = lax.Precision.HIGHEST


def dot(spec, *operands):
    return jnp.einsum(spec, *operands, preferred_element_type=F32)


def standard_rows(token_rows):
    centre = jnp.mean(token_rows, axis=-1, keepdims=True)
    offset = token_rows - centre
    spread = jnp.mean(offset * offset, axis=-1, keepdims=True)
    scale = lax.rsqrt(spread + 1e-05)
    return offset * scale, scale


def norm_rows(token_rows, norm_gain, norm_shift):
    return standard_rows(token_rows)[0] * norm_gain + norm_shift


def norm_back(standard, scale, norm_gain, grad):
    scaled = grad * norm_gain
    first = jnp.mean(scaled, axis=-1, keepdims=True)
    second = jnp.mean(scaled * standard, axis=-1, keepdims=True)
    return scale * (scaled - first - standard * second)


def xor_pairs(size, mask):
    return [(i, i ^ mask) for i in range(size)]


def hyper_sum(value, axes):
    for axis in axes:
        size = lax.axis_size(axis)
        mask = 1
        while mask < size:
            value = value + lax.ppermute(value, axis, xor_pairs(size, mask))
            mask *= 2
    return value


def block_rows(rows, limit):
    best = rows
    for size in range(16, limit + 1, 16):
        if rows % size == 0:
            best = size
    return best


def params(size=60):
    return pltpu.CompilerParams(vmem_limit_bytes=size * 2**20)


def cost(flops, bytes_accessed, transcendentals=0):
    return pl.CostEstimate(
        flops=flops, bytes_accessed=bytes_accessed, transcendentals=transcendentals
    )


def project_kernel(weight_count, rows_ref, gain_ref, bias_ref, *refs):
    weights, (normed_ref, kv_ref, *query_refs) = refs[:weight_count], refs[weight_count:]
    rows = rows_ref[...].astype(F32)
    normed = norm_rows(rows, gain_ref[...], bias_ref[...]).astype(BF)
    normed_ref[...] = normed
    made = [jnp.dot(normed, w[...], preferred_element_type=F32).astype(BF) for w in weights]
    kv_ref[...] = jnp.concatenate(made[:2], axis=1)
    for ref, value in zip(query_refs, made[2:]):
        ref[...] = value


def project(token_rows, gain, bias, *weights):
    rows, width = token_rows.shape
    cols = weights[0].shape[1]
    block = block_rows(rows, 512)
    widths = [width, 2 * cols] + [cols] * (len(weights) - 2)
    whole = lambda i: (0, 0)
    mine = lambda i: (i, 0)
    return pl.pallas_call(
        functools.partial(project_kernel, len(weights)),
        grid=(rows // block,),
        in_specs=[
            pl.BlockSpec((block, width), mine),
            pl.BlockSpec((1, width), whole),
            pl.BlockSpec((1, width), whole),
        ]
        + [pl.BlockSpec((width, cols), whole) for _ in weights],
        out_specs=[pl.BlockSpec((block, w), mine) for w in widths],
        out_shape=[jax.ShapeDtypeStruct((rows, w), BF) for w in widths],
        compiler_params=params(),
        cost_estimate=cost(
            2 * rows * width * cols * len(weights), rows * (width + sum(widths)) * 2
        ),
        name="norm_project",
    )(token_rows, gain[None], bias[None], *weights)


def pieces_of(value):
    high = lax.reduce_precision(value, 8, 7)
    middle = lax.reduce_precision(value - high, 8, 7)
    return [high.astype(BF), middle.astype(BF), (value - high - middle).astype(BF)]


def dot_dims(left, right, left_dim, right_dim):
    dims = (((left_dim,), (right_dim,)), ((), ()))
    return lax.dot_general(left, right, dims, preferred_element_type=F32)


def attend_kernel(heads, q_ref, first_ref, second_ref, out_ref, logsum_ref):
    cols = heads * HEAD_DIM
    parts, stats = [], []
    for h in range(heads):
        here = slice(h * HEAD_DIM, (h + 1) * HEAD_DIM)
        there = slice(cols + h * HEAD_DIM, cols + (h + 1) * HEAD_DIM)
        query = q_ref[0, :, here] * BF(HEAD_DIM**-0.5)
        scores = [dot_dims(ref[0, :, here], query, 1, 1) for ref in (first_ref, second_ref)]
        top = jnp.maximum(*[jnp.max(s, axis=0, keepdims=True) for s in scores])
        raised = [jnp.exp(s - top) for s in scores]
        total = sum(jnp.sum(r, axis=0, keepdims=True) for r in raised)
        mixed = sum(
            dot_dims(ref[0, :, there], r.astype(BF), 0, 0)
            for ref, r in zip((first_ref, second_ref), raised)
        )
        parts.append(mixed / total)
        stats.append(top + jnp.log(total))
    out_ref[0] = jnp.concatenate(parts, axis=0).T.astype(BF)
    logsum_ref[0] = jnp.concatenate(stats, axis=0)


def attend(queries, first, second, heads):
    scenes, count, cols = queries.shape
    keys = first.shape[1] + second.shape[1]
    scene = lambda n: (n, 0, 0)
    return pl.pallas_call(
        functools.partial(attend_kernel, heads),
        grid=(scenes,),
        in_specs=[pl.BlockSpec((1,) + a.shape[1:], scene) for a in (queries, first, second)],
        out_specs=[
            pl.BlockSpec((1, count, cols), scene),
            pl.BlockSpec((1, heads, count), scene),
        ],
        out_shape=[
            jax.ShapeDtypeStruct((scenes, count, cols), BF),
            jax.ShapeDtypeStruct((scenes, heads, count), F32),
        ],
        compiler_params=params(44),
        cost_estimate=cost(
            scenes * heads * count * keys * 16 * HEAD_DIM * 2,
            scenes * keys * cols * 4,
            scenes * heads * count * keys,
        ),
        name="attend",
    )(queries, first, second)


def attend_back_kernel(heads, *refs):
    q_ref, first_ref, second_ref, grad_ref, logsum_ref, na_ref, nb_ref = refs[:7]
    gq_ref, ga_ref, gb_ref, part_ref, sum_ref = refs[-5:]
    if len(refs) > 12:
        part_ref[...] = refs[7][...]
        sum_ref[...] = refs[8][...]
    else:
        part_ref[...] = jnp.zeros_like(part_ref)
        sum_ref[...] = jnp.zeros_like(sum_ref)
    cols = heads * HEAD_DIM
    count = q_ref.shape[1]
    scale = HEAD_DIM**-0.5
    cut = [slice(h * HEAD_DIM, (h + 1) * HEAD_DIM) for h in range(heads)]
    query = [q_ref[0, :, c] * BF(scale) for c in cut]
    grad = [grad_ref[0, :, c] for c in cut]
    ones = jnp.ones((8, HEAD_DIM), F32)
    inner = [
        lax.dot_general(
            ones,
            grad_ref[0, :, cols + c.start : cols + c.stop].astype(F32) * g.astype(F32),
            (((1,), (1,)), ((), ())),
            precision=HIGH,
            preferred_element_type=F32,
        )[:1]
        for c, g in zip(cut, grad)
    ]
    totals = tuple(jnp.zeros((HEAD_DIM, count), F32) for _ in cut)
    for ref, out_ref, normed_ref in ((first_ref, ga_ref, na_ref), (second_ref, gb_ref, nb_ref)):
        rows = ref.shape[1]
        block = block_rows(rows, 1024)

        def step(i, totals, ref=ref, out_ref=out_ref, normed_ref=normed_ref, block=block):
            place = pl.ds(pl.multiple_of(i * block, block), block)
            keys, grads, sums = [], [], []
            for h in range(heads):
                key = ref[0, place, cut[h]]
                value = ref[0, place, slice(cols + cut[h].start, cols + cut[h].stop)]
                shares = jnp.exp(dot_dims(key, query[h], 1, 1) - logsum_ref[0, h : h + 1, :])
                grad_shares = dot_dims(value, grad[h], 1, 1)
                grad_scores = (shares * (grad_shares - inner[h])).astype(BF)
                keys.append(jnp.dot(grad_scores, query[h], preferred_element_type=F32))
                grads.append(jnp.dot(shares.astype(BF), grad[h], preferred_element_type=F32))
                sums.append(totals[h] + dot_dims(key, grad_scores, 0, 0))
            made = jnp.concatenate(keys + grads, axis=1).astype(BF)
            out_ref[0, place, :] = made
            part_ref[...] += dot_dims(made, normed_ref[0, place, :], 0, 0)
            sum_ref[...] += jnp.sum(made.astype(F32), axis=0, keepdims=True)
            return tuple(sums)

        totals = lax.fori_loop(0, rows // block, step, totals, unroll=True)
    gq_ref[0] = (jnp.concatenate(totals, axis=0) * scale).T.astype(BF)


def attend_back(scene, queries, first, second, grad, logsum, normed_first, normed_second, before, heads):
    scenes, count, cols = queries.shape
    keys, width = first.shape[1] + second.shape[1], normed_first.shape[2]
    mine = lambda i: (scene, 0, 0)
    whole = lambda i: (0, 0)
    operands = (queries, first, second, grad, logsum, normed_first, normed_second)
    totals = [(2 * cols, width), (1, 2 * cols)]
    outs = [(1,) + a.shape[1:] for a in (queries, first, second)]
    return pl.pallas_call(
        functools.partial(attend_back_kernel, heads),
        grid=(1,),
        in_specs=[pl.BlockSpec((1,) + a.shape[1:], mine) for a in operands]
        + [pl.BlockSpec(a.shape, whole) for a in before],
        out_specs=[pl.BlockSpec(a, lambda i: (0, 0, 0)) for a in outs]
        + [pl.BlockSpec(a, whole) for a in totals],
        out_shape=[jax.ShapeDtypeStruct(a, BF) for a in outs]
        + [jax.ShapeDtypeStruct(a, F32) for a in totals],
        compiler_params=params(),
        cost_estimate=cost(
            heads * count * keys * 40 * HEAD_DIM * 2 + 4 * keys * cols * width,
            keys * (cols * 8 + width * 2),
            heads * count * keys,
        ),
        name="attend_back",
    )(*operands, *before)


def finish_kernel(cols, rank_ref, kv_ref, extra_ref, weight_ref, gain_ref, patch_ref, plane_ref, *outs):
    own_patch = patch_ref.shape[2]
    parts = kv_ref.shape[0]
    total = sum(dot_dims(kv_ref[t, 0], weight_ref[t, : 2 * cols], 1, 0) for t in range(parts))
    more = sum(
        dot_dims(extra_ref[t, 0, :, :cols], weight_ref[t, 2 * cols :], 1, 0)
        for t in range(parts)
    )
    grads = (total[:own_patch], total[own_patch:] + more)
    extra = jnp.concatenate([extra_ref[t, 0, :, cols:] for t in range(parts)], axis=1)
    added = (0.0, extra.astype(F32))
    for ref, out_ref, grad, plus in zip((patch_ref, plane_ref), outs, grads, added):
        standard, scale = standard_rows(ref[0, 0].astype(F32))
        out_ref[0] = norm_back(standard, scale, gain_ref[...], grad) + plus


def finish(kv_sent, extra_sent, weights, patch_rows, plane_rows, gain, rank, cols):
    parts, scenes, rows, _ = kv_sent.shape
    width = weights.shape[2]
    tokens = [a.reshape(scenes, parts, -1, width) for a in (patch_rows, plane_rows)]
    by_part = lambda n, rank: (0, n, 0, 0)
    spec = pltpu.PrefetchScalarGridSpec(
        num_scalar_prefetch=1,
        grid=(scenes,),
        in_specs=[
            pl.BlockSpec((parts, 1) + kv_sent.shape[2:], by_part),
            pl.BlockSpec((parts, 1) + extra_sent.shape[2:], by_part),
            pl.BlockSpec(weights.shape, lambda n, rank: (0, 0, 0)),
            pl.BlockSpec((1, width), lambda n, rank: (0, 0)),
        ]
        + [pl.BlockSpec((1, 1) + a.shape[2:], lambda n, rank: (n, rank[0], 0, 0)) for a in tokens],
        out_specs=[pl.BlockSpec((1,) + a.shape[2:], lambda n, rank: (n, 0, 0)) for a in tokens],
    )
    return pl.pallas_call(
        functools.partial(finish_kernel, cols),
        grid_spec=spec,
        out_shape=[jax.ShapeDtypeStruct((scenes,) + a.shape[2:], F32) for a in tokens],
        compiler_params=params(),
        cost_estimate=cost(
            scenes * rows * width * parts * 3 * cols * 2, weights.size * 2 + rows * width * 16
        ),
        name="finish",
    )(rank.reshape(1), kv_sent, extra_sent, weights, gain[None], *tokens)


def turn_kernel(rank_ref, *refs):
    parts, outs = refs[:-3], refs[-3:]
    cols, size = outs[0].shape[1], parts[0].shape[1]
    for mask, part in enumerate(parts):
        place = pl.ds(pl.multiple_of((rank_ref[0] ^ mask) * size, size), size)
        for k, ref in enumerate(outs):
            ref[place, :] = part[k * cols : (k + 1) * cols].astype(F32).T


def turn(rank, parts):
    rows, width = parts[0].shape[0], parts[0].shape[1] * len(parts)
    whole = lambda i, r: (0, 0)
    spec = pltpu.PrefetchScalarGridSpec(
        num_scalar_prefetch=1,
        grid=(1,),
        in_specs=[pl.BlockSpec(a.shape, whole) for a in parts],
        out_specs=[pl.BlockSpec((width, rows // 3), whole)] * 3,
    )
    return pl.pallas_call(
        turn_kernel,
        grid_spec=spec,
        out_shape=[jax.ShapeDtypeStruct((width, rows // 3), F32)] * 3,
        compiler_params=params(),
        cost_estimate=cost(1, 1),
        name="turn",
    )(rank.reshape(1), *parts)


def gelu_parts(value):
    slope = 0.7978845608028654
    square = value * value
    bent = jnp.tanh(slope * value * (1.0 + 0.044715 * square))
    half = 0.5 * (1.0 + bent)
    rise = 0.5 * value * (1.0 - bent * bent) * (slope * (1.0 + 0.134145 * square))
    return value * half, half + rise


def weights_kernel(width, rows_ref, up_ref, down_ref, mixed_ref, hidden_ref, tile_ref, *outs):
    up_out, down_out, mix_out, tile_out, sum_out = outs
    unit_step, pick_step = pl.program_id(0), pl.program_id(1)
    normed, result, grad_result = [rows_ref[:, k * width : (k + 1) * width] for k in range(3)]

    @pl.when(pick_step == 0)
    def _():
        up_out[...] = jnp.zeros_like(up_out)
        down_out[...] = jnp.zeros_like(down_out)

    @pl.when((pick_step == 0) & (unit_step == 0))
    def _():
        mix_out[...] = jnp.zeros_like(mix_out)
        tile_out[...] = jnp.zeros_like(tile_out)
        sum_out[...] = jnp.zeros_like(sum_out)

    preact = jnp.dot(normed, up_ref[...], preferred_element_type=F32)
    active, slope = gelu_parts(preact)
    down_out[...] += dot_dims(active.astype(BF), grad_result, 0, 0)
    grad = (dot_dims(grad_result, down_ref[...], 1, 1) * slope).astype(BF)
    up_out[...] += dot_dims(normed, grad, 0, 0)

    @pl.when(unit_step == 0)
    def _():
        parts = [dot_dims(mixed_ref[...], hidden_ref[t], 0, 0) for t in range(hidden_ref.shape[0])]
        mix_out[...] += jnp.concatenate(parts, axis=1)
        tile_out[...] += dot_dims(result, tile_ref[...], 0, 0)
        sum_out[...] += jnp.sum(tile_ref[...].astype(F32), axis=0, keepdims=True)


def weight_grads(rows, w_up, w_down, mixed, hidden, tiles):
    picks, width = rows.shape[0], rows.shape[1] // 3
    units, cols, tile_cols = w_up.shape[1], mixed.shape[1], tiles.shape[1]
    block, units_block = block_rows(picks, 768), block_rows(units, 512)
    here = lambda g, p: (p, 0)
    whole = lambda g, p: (0, 0)
    return pl.pallas_call(
        functools.partial(weights_kernel, width),
        grid=(units // units_block, picks // block),
        in_specs=[
            pl.BlockSpec((block, 3 * width), here),
            pl.BlockSpec((width, units_block), lambda g, p: (0, g)),
            pl.BlockSpec((units_block, width), lambda g, p: (g, 0)),
            pl.BlockSpec((block, cols), here),
            pl.BlockSpec((hidden.shape[0], block, cols), lambda g, p: (0, p, 0)),
            pl.BlockSpec((block, tile_cols), here),
        ],
        out_specs=[
            pl.BlockSpec((width, units_block), lambda g, p: (0, g)),
            pl.BlockSpec((units_block, width), lambda g, p: (g, 0)),
            pl.BlockSpec((cols, width), whole),
            pl.BlockSpec((width, tile_cols), whole),
            pl.BlockSpec((1, tile_cols), whole),
        ],
        out_shape=[
            jax.ShapeDtypeStruct(shape, F32)
            for shape in (
                (width, units),
                (units, width),
                (cols, width),
                (width, tile_cols),
                (1, tile_cols),
            )
        ],
        compiler_params=params(),
        cost_estimate=cost(
            2 * picks * width * (4 * units + cols + tile_cols),
            rows.size * 2 + width * units * 12,
            picks * units,
        ),
        name="weight_grads",
    )(rows, w_up, w_down, mixed, hidden, tiles)


def scatter_kernel(scenes, own, rank_ref, ids_ref, hidden_ref, *refs):
    parts, out_ref = refs[:-1], refs[-1]
    rank = rank_ref[0]
    seq_picks = parts[0].shape[0]
    values = [
        jnp.concatenate([part[...], hidden_ref[rank ^ m]], axis=1) for m, part in enumerate(parts)
    ]
    row = lax.broadcasted_iota(jnp.int32, (own, seq_picks), 0)
    blocks = out_ref.shape[0]

    def step(t, carry):
        for n in range(scenes):
            first = (n * blocks + t) * own
            total = sum(
                jnp.dot(
                    (row + first == ids_ref[rank ^ m]).astype(F32).astype(BF),
                    value,
                    preferred_element_type=F32,
                )
                for m, value in enumerate(values)
            )
            out_ref[t, n] = total.astype(BF)
        return carry

    lax.fori_loop(0, blocks, step, 0)


def scatter(rank, ids, hidden, parts, shape):
    spec = pltpu.PrefetchScalarGridSpec(
        num_scalar_prefetch=1,
        grid=(1,),
        in_specs=[
            pl.BlockSpec(a.shape, lambda i, r, k=a.ndim: (0,) * k) for a in (ids, hidden, *parts)
        ],
        out_specs=pl.BlockSpec(shape, lambda i, r: (0, 0, 0, 0)),
    )
    return pl.pallas_call(
        functools.partial(scatter_kernel, shape[1], shape[2]),
        grid_spec=spec,
        out_shape=jax.ShapeDtypeStruct(shape, BF),
        compiler_params=params(),
        cost_estimate=cost(2 * shape[0] * shape[1] * shape[2] * shape[3] * ids.size, hidden.size * 8),
        name="scatter",
    )(rank.reshape(1), ids, hidden, *parts)


def spread(value, axis):
    size, rank = lax.axis_size(axis), lax.axis_index(axis)
    out = jnp.zeros((size,) + value.shape, value.dtype)
    for mask in range(size):
        other = lax.ppermute(value, axis, xor_pairs(size, mask)) if mask else value
        out = lax.dynamic_update_index_in_dim(out, other, rank ^ mask, 0)
    return out


def split_sum(value, axis):
    size, rank = lax.axis_size(axis), lax.axis_index(axis)
    value = value.reshape((size, value.shape[0] // size) + value.shape[1:])
    total = lax.dynamic_index_in_dim(value, rank, 0, keepdims=False)
    for mask in range(1, size):
        block = lax.dynamic_index_in_dim(value, rank ^ mask, 0, keepdims=False).astype(BF)
        total = total + lax.ppermute(block, axis, xor_pairs(size, mask)).astype(F32)
    return total


def dot_high(left, right, left_dim, right_dim):
    dims = (((left_dim,), (right_dim,)), ((), ()))
    return lax.dot_general(left, right, dims, precision=HIGH, preferred_element_type=F32)


def render_kernel(*refs):
    came_ref, hidden_ref, unpatch_ref, shift_ref, corner_ref, select_ref = refs[:6]
    w1_ref, b1_ref, w2_ref, live_ref, cotangent_ref = refs[6:11]
    (result_ref, colour_ref, tiles_ref, grad_ref, low_ref, g1_ref, gb_ref, g2_ref) = refs[11:]
    parts, rows, _ = came_ref.shape
    rays, _, samples = corner_ref.shape
    result = hidden_ref[...] + sum(came_ref[t].astype(F32) for t in range(parts))
    result = result.astype(BF)
    result_ref[...] = result
    tiles = [
        (jnp.dot(result, unpatch_ref[t], preferred_element_type=F32) + shift_ref[t]).astype(BF)
        for t in range(parts)
    ]
    tiles = jnp.concatenate(tiles, axis=0)
    lines, tile_cols = corner_ref.shape[1], tiles.shape[1]

    def place(shape, dim):
        return lax.broadcasted_iota(jnp.int32, shape, dim)

    pixel_mask = tile_cols // CH - 1
    pixel = place((lines, tile_cols), 1) >> (CH.bit_length() - 1)
    pixel = (pixel == (place((lines, tile_cols), 0) & pixel_mask)).astype(F32)
    pick_out = (place((CH, tile_cols), 1) & (CH - 1)) == place((CH, tile_cols), 0)
    pick_out = pick_out.astype(F32).astype(BF)
    units = b1_ref.shape[1]
    bias = jnp.where(place((units, units), 0) == place((units, units), 1), b1_ref[...], 0.0)
    bias = jnp.sum(bias, axis=1, keepdims=True)
    features = []
    for r in range(rays):
        mine = jnp.dot(select_ref[r], tiles, preferred_element_type=F32) * pixel
        mine = dot_dims(mine.astype(BF), pick_out, 1, 1).astype(BF)
        features.append(dot_dims(mine, corner_ref[r], 0, 0))
    features = jnp.concatenate(features, axis=1)
    preact = dot_high(w1_ref[...], features, 0, 0) + bias
    gate = 1.0 / (1.0 + jnp.exp(-preact))
    hidden = preact * gate
    output = dot_high(w2_ref[...], hidden, 0, 0)

    def by_ray(row):
        return jnp.concatenate(
            [row[:, r * samples : (r + 1) * samples] for r in range(rays)], axis=0
        )

    def in_row(value):
        return jnp.concatenate([value[r : r + 1] for r in range(rays)], axis=1)

    first = by_ray(output[0:1])
    density = jnp.maximum(first, 0.0) + jnp.log1p(jnp.exp(-jnp.abs(first)))
    shades = [1.0 / (1.0 + jnp.exp(-by_ray(output[k : k + 1]))) for k in (1, 2, 3)]
    optical = density * (2.0 / samples)
    before = (
        lax.broadcasted_iota(jnp.int32, (samples, samples), 0)
        < lax.broadcasted_iota(jnp.int32, (samples, samples), 1)
    ).astype(F32)
    through = jnp.exp(-dot_high(optical, before, 1, 0))
    kept = jnp.exp(-optical)
    weight = through * (1.0 - kept)
    live = live_ref[...]
    colour_ref[...] = jnp.concatenate(
        [jnp.sum(weight * shade, axis=1, keepdims=True) * live for shade in shades], axis=1
    )
    grads = [cotangent_ref[:, k : k + 1] * live for k in range(3)]
    grad_weight = sum(g * shade for g, shade in zip(grads, shades))
    grad_before = -through * grad_weight * (1.0 - kept)
    grad_optical = dot_high(grad_before, before, 1, 1) + grad_weight * through * kept
    grad_first = grad_optical * (2.0 / samples) * (1.0 / (1.0 + jnp.exp(-first)))
    grad_shades = [g * weight * shade * (1.0 - shade) for g, shade in zip(grads, shades)]
    grad_output = jnp.concatenate([in_row(g) for g in [grad_first] + grad_shades], axis=0)
    grad_preact = jnp.dot(w2_ref[...], grad_output, precision=HIGH, preferred_element_type=F32)
    grad_preact = grad_preact * (gate * (1.0 + preact * (1.0 - gate)))
    g2_ref[...] = dot_high(hidden, grad_output, 1, 1)
    gb_ref[...] = jnp.sum(grad_preact, axis=1, keepdims=True)
    g1_ref[...] = dot_high(features, grad_preact, 1, 1)
    grad_features = jnp.dot(w1_ref[...], grad_preact, precision=HIGH, preferred_element_type=F32)
    total = jnp.zeros(tiles.shape, F32)
    for r in range(rays):
        mine = grad_features[:, r * samples : (r + 1) * samples]
        high = mine.astype(BF)
        low = (mine - high.astype(F32)).astype(BF)
        corner = corner_ref[r]
        mine = (dot_dims(corner, high, 1, 1) + dot_dims(corner, low, 1, 1)).astype(BF)
        mine = jnp.dot(mine, pick_out, preferred_element_type=F32) * pixel
        total = total + dot_dims(select_ref[r], mine.astype(BF), 0, 0)
    grad = jnp.zeros(grad_ref.shape, F32)
    for t in range(parts):
        mine = total[t * rows : (t + 1) * rows].astype(BF)
        tiles_ref[t] = mine
        grad = grad + dot_dims(mine, unpatch_ref[t], 1, 1)
    grad_ref[...] = grad
    low_ref[...] = grad.astype(BF)


def render(came, hidden_own, unpatch, shift, corners, w1, b1, w2, live, cotangent):
    parts, rows, width = came.shape
    scenes, rays, tile_cols = corners.shape[1], corners.shape[2], unpatch.shape[2]
    pixels, samples = corners.shape[4], corners.shape[5]
    corners = jnp.transpose(corners, (1, 2, 0, 3, 4, 5))
    corners = corners.reshape(scenes * rays, parts * 3 * pixels, samples)
    ray = jnp.arange(scenes * rays)[:, None, None]
    line = jnp.arange(parts * 3 * pixels)[None, :, None]
    source = (line // (3 * pixels)) * rows + (line // pixels) % 3 * rays
    source = source + (ray // rays) * (3 * rays) + ray % rays
    select = (source == jnp.arange(parts * rows)[None, None, :]).astype(BF)
    hidden_units = w1.shape[1]
    operands = (came, hidden_own, unpatch, shift[:, None], corners, select)
    operands += (w1, b1[None], w2, live, cotangent)
    outs = [
        ((rows, width), BF),
        (cotangent.shape, F32),
        ((parts, rows, tile_cols), BF),
        ((rows, width), F32),
        ((rows, width), BF),
        (w1.shape, F32),
        ((hidden_units, 1), F32),
        (w2.shape, F32),
    ]
    return pl.pallas_call(
        render_kernel,
        out_shape=[jax.ShapeDtypeStruct(shape, kind) for shape, kind in outs],
        compiler_params=params(32),
        cost_estimate=cost(8 * rows * width * tile_cols * parts, unpatch.size * 2, 0),
        name="render",
    )(*operands)


def on_device(
    patch_tokens,
    plane_tokens,
    norm1_gain,
    norm1_bias,
    w_query,
    w_key,
    w_value,
    w_out,
    norm2_gain,
    norm2_bias,
    w_up,
    w_down,
    w_unpatch,
    b_unpatch,
    w_dec1,
    b_dec1,
    w_dec2,
    tile_index,
    corner_weights,
    ray_count,
    color_grad,
):
    scenes, patch_local, width = patch_tokens.shape
    plane_local = plane_tokens.shape[1]
    seq_count, tp_count = lax.axis_size("seq"), lax.axis_size("tp")
    seq_rank, tp_rank = lax.axis_index("seq"), lax.axis_index("tp")
    own_patch = patch_local // tp_count
    own_plane = plane_local // tp_count
    cols = w_query.shape[1]
    heads = cols // HEAD_DIM
    ray_seq = tile_index.shape[2]
    rays = ray_seq // tp_count
    picks = 3 * rays
    seq_picks = tp_count * scenes * picks
    all_picks = seq_count * seq_picks
    score_scale = HEAD_DIM**-0.5

    base = (jnp.arange(3, dtype=jnp.int32) * (TRI_SIDE * TRI_SIDE))[None, :, None]
    ids = (tile_index + base).reshape(scenes, 3, tp_count, rays)
    ids = jnp.transpose(ids, (2, 0, 1, 3)).reshape(tp_count, scenes, picks)
    ids = jnp.broadcast_to(ids[None], (seq_count,) + ids.shape)
    ids = lax.all_to_all(ids, "seq", 0, 0, tiled=True)
    plane_normed, plane_kv, query_rows = project(
        plane_tokens.reshape(-1, width), norm1_gain, norm1_bias, w_key, w_value, w_query
    )
    ids, query_rows = lax.optimization_barrier((ids, query_rows))
    local_ids = ids - seq_rank * plane_local
    inside = (local_ids >= 0) & (local_ids < plane_local)
    scene_base = (jnp.arange(scenes, dtype=jnp.int32) * plane_local)[None, None, :, None]
    row_ids = jnp.where(inside, local_ids + scene_base, -1).reshape(all_picks)
    onehot = (
        row_ids[:, None] == jnp.arange(scenes * plane_local, dtype=jnp.int32)[None, :]
    ).astype(BF)

    own_cols = lax.dynamic_slice_in_dim(plane_tokens, tp_rank * cols, cols, 2)
    chosen = jnp.dot(onehot, jnp.concatenate([query_rows, own_cols.reshape(-1, cols)], axis=1))
    chosen, corner_weights, w_key_later, patch_tokens = lax.optimization_barrier(
        (chosen, corner_weights, w_key, patch_tokens)
    )
    chosen = split_sum(chosen, "seq").astype(BF)
    chosen, patch_tokens = lax.optimization_barrier((chosen, patch_tokens))
    queries = spread(chosen[:, :cols], "seq").reshape(all_picks, cols)
    picked_cols = chosen[:, cols:]

    w_out_all = lax.all_gather(w_out, "tp", axis=0)
    unpatch_all = lax.all_gather(w_unpatch, "tp", axis=0)
    qkv_weight = jnp.concatenate([w_key_later.T, w_value.T, w_query.T], axis=0)
    qkv_all = lax.all_gather(qkv_weight, "tp", axis=0)

    corners = corner_weights.reshape(
        scenes, tp_count, rays, 3, corner_weights.shape[3], corner_weights.shape[4]
    )
    corners = lax.all_to_all(jnp.moveaxis(corners, 1, 0), "tp", 0, 0, tiled=True)

    patch_normed, patch_kv = project(
        patch_tokens.reshape(-1, width), norm1_gain, norm1_bias, w_key, w_value
    )
    queries, corners, patch_kv, picked_cols, w_out_all = lax.optimization_barrier(
        (queries, corners, patch_kv, picked_cols, w_out_all)
    )
    plane_kv = plane_kv.reshape(scenes, plane_local, 2 * cols)
    patch_kv = patch_kv.reshape(scenes, patch_local, 2 * cols)

    def by_scene(value):
        value = value.reshape(seq_count, tp_count, scenes, picks, -1)
        return jnp.moveaxis(value, 2, 0).reshape(scenes, seq_count * tp_count * picks, -1)

    def by_seq(value):
        value = value.reshape(scenes, seq_count, tp_count, picks, -1)
        return jnp.moveaxis(value, 0, 2).reshape(seq_count, seq_picks, -1)

    def in_heads(value):
        return value.reshape(value.shape[:-1] + (heads, HEAD_DIM))

    queries = by_scene(queries)
    part, logsum = attend(queries, patch_kv, plane_kv, heads)
    part = by_seq(part)
    flat = jnp.stack(pieces_of(logsum)).reshape(-1)
    stat_rows = -(-flat.shape[0] // (16 * cols)) * 16
    flat = jnp.pad(flat, (0, stat_rows * cols - flat.shape[0])).reshape(stat_rows, cols)
    flat = jnp.broadcast_to(flat[None], (seq_count, stat_rows, cols))
    part = lax.all_to_all(jnp.concatenate([part, flat], axis=1), "seq", 0, 0, tiled=True)
    logsums = part[:, seq_picks:].reshape(seq_count, -1)[:, : 3 * logsum.size]
    logsums = jnp.sum(logsums.reshape((seq_count, 3) + logsum.shape).astype(F32), axis=1)
    top = jnp.max(logsums, axis=0)
    logsum = top + jnp.log(jnp.sum(jnp.exp(logsums - top), axis=0))
    shares = jnp.exp(logsums - logsum)
    shares = shares.reshape(seq_count, scenes, heads, seq_count, tp_count, picks)
    shares = lax.dynamic_index_in_dim(shares, seq_rank, 3, keepdims=False)
    shares = jnp.transpose(shares, (0, 3, 1, 4, 2)).reshape(seq_count, seq_picks, heads, 1)
    mixed_low = jnp.sum(in_heads(part[:, :seq_picks].astype(F32)) * shares, axis=0)
    mixed_low = mixed_low.reshape(seq_picks, cols).astype(BF)

    bias_rows = jnp.stack(pieces_of(b_unpatch) + [jnp.zeros_like(b_unpatch, BF)] * 13)
    mixed_low = jnp.concatenate([mixed_low, picked_cols], axis=1)
    mixed_low = jnp.concatenate([mixed_low, bias_rows], axis=0)
    mixed_all = lax.all_gather(mixed_low, "tp", axis=0)
    bias_all = jnp.sum(mixed_all[:, seq_picks : seq_picks + 3].astype(F32), axis=1)
    mixed_all, unpatch_all = lax.optimization_barrier((mixed_all[:, :seq_picks], unpatch_all))
    branch = dot("tre,ted->rd", mixed_all[..., :cols], w_out_all)
    picked_rows = jnp.moveaxis(mixed_all[..., cols:], 0, 1).reshape(seq_picks, width)
    picked_rows = picked_rows.astype(F32)
    hidden_state = picked_rows + branch
    normed2 = norm_rows(hidden_state, norm2_gain, norm2_bias).astype(BF)
    preact = jnp.dot(normed2, w_up, preferred_element_type=F32)
    active = jax.nn.gelu(preact).astype(BF)
    down = jnp.dot(active, w_down, preferred_element_type=F32).astype(BF)
    own_rows = scenes * picks

    def to_all(value):
        value = jnp.broadcast_to(value[None], (seq_count,) + value.shape)
        value = value.reshape((seq_count * tp_count,) + value.shape[2:])
        return lax.all_to_all(value, ("seq", "tp"), 0, 0, tiled=True)

    def tp_first(value):
        value = value.reshape((seq_count, tp_count, own_rows) + value.shape[1:])
        return jnp.moveaxis(value, 1, 0).reshape((all_picks,) + value.shape[3:])

    def to_own(value):
        return lax.all_to_all(value.reshape(tp_count, own_rows, width), "tp", 0, 0, tiled=True)

    hidden_own = lax.dynamic_slice_in_dim(hidden_state, tp_rank * own_rows, own_rows, 0)
    normed2_own = lax.dynamic_slice_in_dim(normed2, tp_rank * own_rows, own_rows, 0)
    tile_cols = w_unpatch.shape[1]
    first_ray = (seq_rank * tp_count + tp_rank) * rays
    live_rays = (
        (first_ray + jnp.arange(rays, dtype=jnp.int32))[None, :] < ray_count[:, None]
    ).astype(F32)
    (
        result_own,
        colours,
        grad_tiles,
        grad_result,
        grad_result_low,
        dec1_part,
        dec1_bias_part,
        dec2_part,
    ) = render(
        to_own(down),
        hidden_own,
        unpatch_all,
        bias_all,
        corners,
        w_dec1,
        b_dec1,
        w_dec2,
        live_rays.reshape(-1, 1),
        jnp.moveaxis(color_grad, 1, -1).reshape(-1, 3),
    )
    colours = colours.reshape(scenes, rays, 3)
    result_rows = lax.all_gather(grad_result_low, "tp", axis=0, tiled=True)
    early = jnp.concatenate([normed2_own, result_own, grad_result_low], axis=1)
    early, result_rows = lax.optimization_barrier((early, result_rows))
    early = spread(early, "seq").reshape(-1, 3 * width)
    grad_active = dot("rd,fd->rf", result_rows, w_down)
    grad_preact = jax.vjp(jax.nn.gelu, preact)[1](grad_active)[0].astype(BF)
    grad_normed2 = dot("rf,df->rd", grad_preact, w_up).astype(BF)
    grad_normed2, qkv_all = lax.optimization_barrier((grad_normed2, qkv_all))
    dec1_cols = w_dec1.shape[1] // tp_count
    dec1_part = jnp.moveaxis(dec1_part.reshape(-1, tp_count, dec1_cols), 1, 0)
    small = [dec1_part, dec1_bias_part, dec2_part]
    small = jnp.concatenate([piece.reshape(tp_count, -1) for piece in small], axis=1)
    colours = jnp.moveaxis(colours, -1, 1)
    grad_normed2, small, colours, early = lax.optimization_barrier(
        (to_own(grad_normed2), small, colours, early)
    )
    early = lax.all_gather(early, "tp", axis=0, tiled=True)
    grad_normed2 = jnp.sum(grad_normed2.astype(F32), axis=0)
    standard2, scale2 = standard_rows(hidden_own)
    gain2_part = jnp.sum(grad_normed2 * standard2, axis=0)
    shift2_part = jnp.sum(grad_normed2, axis=0)
    grad_hidden = grad_result + norm_back(standard2, scale2, norm2_gain, grad_normed2)
    def to_owner(value):
        return lax.all_to_all(value, "tp", 0, 0, tiled=True)

    def by_owner(value, own):
        value = value.reshape(-1, tp_count, own, value.shape[-1])
        return jnp.moveaxis(value, 1, 0)

    normed_picks = norm_rows(picked_rows, norm1_gain, norm1_bias).astype(BF)
    hidden_low = grad_hidden.astype(BF)
    grad_mixed = dot("kd,ted->tke", hidden_low, w_out_all).astype(BF)
    hidden_cols = jnp.moveaxis(hidden_low.reshape(own_rows, tp_count, cols), 1, 0)
    mixed_own = lax.dynamic_slice_in_dim(mixed_all[..., :cols], tp_rank * own_rows, own_rows, 1)
    sent = to_all(jnp.concatenate([grad_mixed, mixed_own], axis=-1))
    later = jnp.concatenate([hidden_cols, grad_tiles], axis=-1)
    small = [gain2_part.reshape(tp_count, -1), shift2_part.reshape(tp_count, -1), small]
    small = jnp.concatenate(small, axis=1)
    sent, later, small = lax.optimization_barrier((sent, later, small))
    later = to_all(later).reshape(all_picks, cols + tile_cols)

    scene_sent = by_scene(sent)
    made, totals = [], []
    operands = (queries, patch_kv, plane_kv, scene_sent, logsum)
    operands += (
        patch_normed.reshape(scenes, patch_local, width),
        plane_normed.reshape(scenes, plane_local, width),
    )
    for n in range(scenes):
        if n == scenes - 1:
            operands, later, made = lax.optimization_barrier((operands, later, made))
        *one, part, sums = attend_back(n, *operands, totals, heads)
        made.append(one)
        totals = [part, sums]
    kv_sent = to_owner(
        jnp.concatenate(
            [
                jnp.concatenate([by_owner(one[1], own_patch), by_owner(one[2], own_plane)], axis=2)
                for one in made
            ],
            axis=1,
        )
    )
    grad_query = jnp.concatenate([one[0] for one in made], axis=0)
    kv_part, kv_sum = totals
    hidden_cols = later[:, :cols]
    hidden_late, early, made = lax.optimization_barrier((hidden_cols, early, made))
    hidden_cols_all = lax.all_gather(hidden_late, "tp", axis=0)
    grad_query = split_sum(by_seq(grad_query).reshape(all_picks, cols), "seq").astype(BF)
    grad_query, sent = lax.optimization_barrier((grad_query, sent))
    query_part = dot("rd,re->ed", normed_picks, grad_query)
    qkv_part = jnp.concatenate([kv_part, query_part], axis=0)
    size = width // seq_count

    def block_of(mask):
        return lax.dynamic_slice_in_dim(qkv_part, (seq_rank ^ mask) * size, size, 1)

    own_block = block_of(0)
    received = []
    for mask in range(1, seq_count):
        block = lax.ppermute(block_of(mask).astype(BF), "seq", xor_pairs(seq_count, mask))
        received.append(block)
    query_parts = [grad_query] + [
        lax.ppermute(grad_query, "seq", xor_pairs(seq_count, mask)) for mask in range(1, seq_count)
    ]
    query_sum = jnp.sum(grad_query.astype(F32), axis=0)
    sums = jnp.concatenate([kv_sum[0], query_sum])[:, None]
    wide = qkv_weight.astype(F32)
    shift1_part = jnp.sum(wide * sums, axis=0)
    product = jnp.sum(wide * qkv_part, axis=0)
    gain1_part = (product - norm1_bias * shift1_part) / norm1_gain

    up_grad, down_grad, out_grad, unpatch_grad, unpatch_bias_grad = weight_grads(
        early,
        w_up,
        w_down,
        sent.reshape(all_picks, 2 * cols)[:, cols:],
        hidden_cols_all,
        tp_first(later[:, cols:]),
    )
    query_parts, own_block, up_grad = lax.optimization_barrier((query_parts, own_block, up_grad))
    qkv_sum = (own_block + sum(block.astype(F32) for block in received)).astype(BF)
    scattered = scatter(
        seq_rank,
        row_ids.reshape(seq_count, 1, seq_picks),
        hidden_cols.reshape(seq_count, seq_picks, cols),
        query_parts,
        (tp_count, scenes, own_plane, 2 * cols),
    )

    unpatch_bias_grad = unpatch_bias_grad[0]

    scattered, kv_sent, up_grad, qkv_sum = lax.optimization_barrier(
        (scattered, kv_sent, up_grad, qkv_sum)
    )
    extra_sent = to_owner(scattered)
    qkv_parts = [qkv_sum] + [
        lax.ppermute(qkv_sum, "seq", xor_pairs(seq_count, mask)) for mask in range(1, seq_count)
    ]

    pieces = [gain1_part.reshape(tp_count, -1), shift1_part.reshape(tp_count, -1), small]
    pieces, _ = lax.optimization_barrier((jnp.concatenate(pieces, axis=1), extra_sent))
    pieces = jnp.sum(to_all(pieces), axis=0)
    sizes = [width // tp_count] * 4
    sizes += [w_dec1.shape[0] * dec1_cols, dec1_cols, dec1_cols * w_dec2.shape[1]]
    totals = []
    for count in sizes:
        totals.append(pieces[:count])
        pieces = pieces[count:]
    gain1_grad, shift1_grad, gain2_grad, shift2_grad = totals[:4]
    dec1_grad, dec1_bias_grad, dec2_grad = totals[4:]

    patch_grad, plane_grad = finish(
        kv_sent, extra_sent, qkv_all, patch_tokens, plane_tokens, norm1_gain, tp_rank, cols
    )
    qkv_parts, patch_grad = lax.optimization_barrier((qkv_parts, patch_grad))
    key_grad, value_grad, query_grad = turn(seq_rank, qkv_parts)
    return (
        colours,
        patch_grad,
        plane_grad,
        gain1_grad,
        shift1_grad,
        query_grad,
        key_grad,
        value_grad,
        out_grad,
        gain2_grad,
        shift2_grad,
        up_grad,
        down_grad,
        unpatch_grad,
        unpatch_bias_grad,
        dec1_grad.reshape(-1, dec1_cols),
        dec1_bias_grad,
        dec2_grad.reshape(-1, w_dec2.shape[1]),
    )


def solution(mesh):
    in_specs = (
        P(None, "seq", None),
        P(None, "seq", None),
        P(),
        P(),
        P(None, "tp"),
        P(None, "tp"),
        P(None, "tp"),
        P("tp", None),
        P(),
        P(),
        P(None, "tp"),
        P("tp", None),
        P(None, "tp"),
        P("tp"),
        P(),
        P(),
        P(),
        P(None, None, "seq"),
        P(None, "seq", None, "tp", None),
        P(),
        P(None, None, ("seq", "tp")),
    )
    out_specs = (
        P(None, None, ("seq", "tp")),
        P(None, ("seq", "tp"), None),
        P(None, ("seq", "tp"), None),
        P("tp"),
        P("tp"),
        P(None, "tp"),
        P(None, "tp"),
        P(None, "tp"),
        P("tp", None),
        P("tp"),
        P("tp"),
        P(None, "tp"),
        P("tp", None),
        P(None, "tp"),
        P("tp"),
        P(None, "tp"),
        P("tp"),
        P("tp", None),
    )
    return jax.shard_map(
        on_device, mesh=mesh, in_specs=in_specs, out_specs=out_specs, check_vma=False
    )
```
